32 devices in a mesh: dp: 16 (over z, y, x), head: 2 (over core).
Axes of the slice: x: 2, y: 2, z: 4, core: 2. Of those that a mesh axis runs over, the one named last changes fastest.
Arguments:
- tokens: bfloat16 [16384, 768], P('dp'), may hold values from -6 to 6
- row_bucket: int32 [16], P('dp'), may hold values from 0 to 2, as said below
- row_lengths: int32 [16, 8], P('dp'), may hold values from 0 to 512, as said below
- teacher_query_weight: bfloat16 [768, 768], P(None, 'head'), may hold values from -0.21875 to 0.21875
- teacher_query_bias: float32 [768], P('head'), may hold values from -1.8 to 1.8
- teacher_key_weight: bfloat16 [768, 768], P(None, 'head'), may hold values from -0.21875 to 0.21875
- teacher_value_weight: bfloat16 [768, 768], P(None, 'head'), may hold values from -0.21875 to 0.21875
- teacher_value_bias: float32 [768], P('head'), may hold values from -1.8 to 1.8
- teacher_output_weight: bfloat16 [768, 768], P('head'), may hold values from -0.875 to 0.875
- teacher_output_bias: float32 [768], replicated, may hold values from -1.8 to 1.8
- teacher_first_gain: float32 [768], replicated, may hold values from 0.5 to 1.5
- teacher_first_shift: float32 [768], replicated, may hold values from -1.8 to 1.8
- teacher_hidden_weight: bfloat16 [768, 3072], P(None, 'head'), may hold values from -0.21875 to 0.21875
- teacher_hidden_bias: float32 [3072], P('head'), may hold values from -3 to 3
- teacher_return_weight: bfloat16 [3072, 768], P('head'), may hold values from -0.15625 to 0.15625
- teacher_return_bias: float32 [768], replicated, may hold values from -1.8 to 1.8
- teacher_second_gain: float32 [768], replicated, may hold values from 0.5 to 1.5
- teacher_second_shift: float32 [768], replicated, may hold values from -1.8 to 1.8
- student_query_weight: bfloat16 [768, 768], P(None, 'head'), may hold values from -0.21875 to 0.21875
- student_query_bias: float32 [768], P('head'), may hold values from -1.8 to 1.8
- student_key_weight: bfloat16 [768, 768], P(None, 'head'), may hold values from -0.21875 to 0.21875
- student_value_weight: bfloat16 [768, 768], P(None, 'head'), may hold values from -0.21875 to 0.21875
- student_value_bias: float32 [768], P('head'), may hold values from -1.8 to 1.8
- student_output_weight: bfloat16 [768, 768], P('head'), may hold values from -0.875 to 0.875
- student_output_bias: float32 [768], replicated, may hold values from -1.8 to 1.8
- student_first_gain: float32 [768], replicated, may hold values from 0.5 to 1.5
- student_first_shift: float32 [768], replicated, may hold values from -1.8 to 1.8
- student_hidden_weight: bfloat16 [768, 3072], P(None, 'head'), may hold values from -0.21875 to 0.21875
- student_hidden_bias: float32 [3072], P('head'), may hold values from -3 to 3
- student_return_weight: bfloat16 [3072, 768], P('head'), may hold values from -0.15625 to 0.15625
- student_return_bias: float32 [768], replicated, may hold values from -1.8 to 1.8
- student_second_gain: float32 [768], replicated, may hold values from 0.5 to 1.5
- student_second_shift: float32 [768], replicated, may hold values from -1.8 to 1.8
Outputs:
- student_out: float32 [16384, 768], P('dp')
- input_grad: float32 [16384, 768], P('dp')
- grad_query_weight: float32 [768, 768], P('dp', 'head')
- grad_query_bias: float32 [768], P('head')
- grad_key_weight: float32 [768, 768], P('dp', 'head')
- grad_value_weight: float32 [768, 768], P('dp', 'head')
- grad_value_bias: float32 [768], P('head')
- grad_output_weight: float32 [768, 768], P('head', 'dp')
- grad_output_bias: float32 [768], replicated
- grad_first_gain: float32 [768], replicated
- grad_first_shift: float32 [768], replicated
- grad_hidden_weight: float32 [768, 3072], P('dp', 'head')
- grad_hidden_bias: float32 [3072], P('head')
- grad_return_weight: float32 [3072, 768], P('head', 'dp')
- grad_return_bias: float32 [768], replicated
- grad_second_gain: float32 [768], replicated
- grad_second_shift: float32 [768], replicated
The draws below stay inside these ranges and needn't reach their ends.
Inputs may be any that keep to these rules, and one draw needn't show every extreme that they name: `row_bucket`: bucket 2 is the bucket of some index of dp in every draw. `row_lengths`: entry [d, j] is the number of real tokens at the start of row j of index d of dp, whose rows hold (128) * 2^row_bucket[d] slots: more than half of the row and at most all of it; entries past the index's last row are 0. Some index of bucket 2 has a first row of exactly 512 real tokens.
All inputs are finite; a program needn't handle non-finite values.
Results may differ from the reference program's by a relative error of at most 0.014.
The reference program's roundings to bfloat16 on the way count: a program that leaves them out, or rounds other values in their place, can miss the bound.
Values sent between devices are 32-bit elements; how exact they have to be, the bound alone decides.
A program may use at most 192 MiB of HBM per device.

```python
import functools
import math
import jax
import jax.numpy as jnp
from jax import lax

D = 768
HEAD_DIM = 64
FF = 3072
SPAN = 512
TOK_DEV = 1024
TOKENS = 16384
N_DP = 16


def shared_layout(key):
    bucket_key = jax.random.fold_in(key, 101)
    lead_key = jax.random.fold_in(key, 102)
    buckets = jax.random.randint(bucket_key, (N_DP,), 0, 3, dtype=jnp.int32)
    lead = jax.random.randint(lead_key, (), 0, N_DP, dtype=jnp.int32)
    places = jnp.arange(N_DP, dtype=jnp.int32)
    buckets = jnp.where(places == lead, 2, buckets).astype(jnp.int32)
    return (buckets, lead)


def draw_row_bucket(key, part):
    buckets, lead = shared_layout(key)
    return buckets


def draw_row_lengths(key, part):
    buckets, lead = shared_layout(key)
    key = jax.random.fold_in(key, 7)
    slot_count = 4 * TOK_DEV // SPAN
    row_span = jnp.where(buckets == 0, SPAN // 4, jnp.where(buckets == 1, SPAN // 2, SPAN)).astype(jnp.int32)
    rows_used = TOK_DEV // row_span
    raw = jax.random.randint(key, (N_DP, slot_count), 0, 1 << 20, dtype=jnp.int32)
    half_span = row_span // 2
    lengths = half_span[:, None] + 1 + raw % half_span[:, None]
    column = jnp.arange(slot_count, dtype=jnp.int32)[None, :]
    lengths = jnp.where(column < rows_used[:, None], lengths, 0)
    first = (jnp.arange(N_DP, dtype=jnp.int32)[:, None] == lead) & (column == 0)
    lengths = jnp.where(first, SPAN, lengths)
    return lengths.astype(jnp.int32)


def raised(values, key, source, target, blocks, factor):
    def block_of(axis_at):
        return (jnp.arange(values.shape[axis_at]) // (values.shape[axis_at] // blocks)).reshape((-1,) + (1,) * (values.ndim - 1 - axis_at))

    near = jax.random.permutation(key, blocks)[block_of(target)]
    second = (block_of(target) + blocks // 2) % blocks
    return jnp.where((block_of(source) == near) | (block_of(source) == second), factor * values, values)


def shard_levels(rng, shape, pieces, smallest, high):
    def one(position, parts):
        draws = jax.random.uniform(jax.random.fold_in(jax.random.fold_in(rng, 6), position), (parts,), jnp.float32, smallest / len(pieces), high / len(pieces))
        return jnp.repeat(jnp.exp(draws), shape[position] // parts).reshape((-1,) + (1,) * (len(shape) - position - 1))

    gain = one(*pieces[0])
    for cut in pieces[1:]:
        gain = gain * one(*cut)
    return gain


def scatter_about(rng, extent, scale, reach, pieces=(), held_as=jnp.bfloat16):
    array = jax.random.normal(rng, extent, jnp.float32) * scale
    if len(pieces) > 0:
        array = shard_levels(rng, extent, pieces, -0.22, 0.18) * array
    return jnp.clip(array, min=-reach, max=reach).astype(held_as)


def bell_draw_with(key, extent, scale, most, split, heavy, kind=jnp.bfloat16):
    values = scale * jax.random.normal(key, extent, jnp.float32)
    if split:
        values = values * shard_levels(key, extent, split, -0.22, 0.18)
    return jnp.clip(raised(values, jax.random.fold_in(key, 3), *heavy), -most, most).astype(kind)


def setup_inputs(seed: int = 0) -> dict:
    arg_keys = jax.random.split(jax.random.key(seed), 34)
    return {
        "tokens": bell_draw_with(arg_keys[0], (TOKENS, D), 1.0, 6.0, ((0, 16),), (0, 1, 16, 2.0)),
        "row_bucket": draw_row_bucket(jax.random.fold_in(arg_keys[33], 71), 0),
        "row_lengths": draw_row_lengths(jax.random.fold_in(arg_keys[33], 71), 0),
        "teacher_query_weight": scatter_about(arg_keys[3], (D, D), D ** -0.5, 0.21875, ((1, 2),)),
        "teacher_query_bias": scatter_about(arg_keys[4], (D,), 0.3, 1.8, ((0, 2),), jnp.float32),
        "teacher_key_weight": scatter_about(arg_keys[5], (D, D), D ** -0.5, 0.21875, ((1, 2),)),
        "teacher_value_weight": scatter_about(arg_keys[6], (D, D), D ** -0.5, 0.21875, ((1, 2),)),
        "teacher_value_bias": scatter_about(arg_keys[7], (D,), 0.3, 1.8, ((0, 2),), jnp.float32),
        "teacher_output_weight": scatter_about(arg_keys[8], (D, D), (D // 16) ** -0.5, 0.875, ((0, 2),)),
        "teacher_output_bias": scatter_about(arg_keys[9], (D,), 0.3, 1.8, (), jnp.float32),
        "teacher_first_gain": jnp.clip(1.0 + 0.1 * jax.random.normal(arg_keys[10], (D,), jnp.float32), 0.5, 1.5),
        "teacher_first_shift": scatter_about(arg_keys[11], (D,), 0.3, 1.8, (), jnp.float32),
        "teacher_hidden_weight": scatter_about(arg_keys[12], (D, FF), D ** -0.5, 0.21875, ((1, 2),)),
        "teacher_hidden_bias": scatter_about(arg_keys[13], (FF,), 0.5, 3.0, ((0, 2),), jnp.float32),
        "teacher_return_weight": scatter_about(arg_keys[14], (FF, D), (FF // 2) ** -0.5, 0.15625, ((0, 2),)),
        "teacher_return_bias": scatter_about(arg_keys[15], (D,), 0.3, 1.8, (), jnp.float32),
        "teacher_second_gain": jnp.clip(1.0 + 0.1 * jax.random.normal(arg_keys[16], (D,), jnp.float32), 0.5, 1.5),
        "teacher_second_shift": scatter_about(arg_keys[17], (D,), 0.3, 1.8, (), jnp.float32),
        "student_query_weight": scatter_about(arg_keys[18], (D, D), D ** -0.5, 0.21875, ((1, 2),)),
        "student_query_bias": scatter_about(arg_keys[19], (D,), 0.3, 1.8, ((0, 2),), jnp.float32),
        "student_key_weight": scatter_about(arg_keys[20], (D, D), D ** -0.5, 0.21875, ((1, 2),)),
        "student_value_weight": scatter_about(arg_keys[21], (D, D), D ** -0.5, 0.21875, ((1, 2),)),
        "student_value_bias": scatter_about(arg_keys[22], (D,), 0.3, 1.8, ((0, 2),), jnp.float32),
        "student_output_weight": scatter_about(arg_keys[23], (D, D), (D // 16) ** -0.5, 0.875, ((0, 2),)),
        "student_output_bias": scatter_about(arg_keys[24], (D,), 0.3, 1.8, (), jnp.float32),
        "student_first_gain": jnp.clip(1.0 + 0.1 * jax.random.normal(arg_keys[25], (D,), jnp.float32), 0.5, 1.5),
        "student_first_shift": scatter_about(arg_keys[26], (D,), 0.3, 1.8, (), jnp.float32),
        "student_hidden_weight": scatter_about(arg_keys[27], (D, FF), D ** -0.5, 0.21875, ((1, 2),)),
        "student_hidden_bias": scatter_about(arg_keys[28], (FF,), 0.5, 3.0, ((0, 2),), jnp.float32),
        "student_return_weight": scatter_about(arg_keys[29], (FF, D), (FF // 2) ** -0.5, 0.15625, ((0, 2),)),
        "student_return_bias": scatter_about(arg_keys[30], (D,), 0.3, 1.8, (), jnp.float32),
        "student_second_gain": jnp.clip(1.0 + 0.1 * jax.random.normal(arg_keys[31], (D,), jnp.float32), 0.5, 1.5),
        "student_second_shift": scatter_about(arg_keys[32], (D,), 0.3, 1.8, (), jnp.float32),
    }


@jax.custom_vjp
def low(v):
    return lax.optimization_barrier(v.astype(jnp.bfloat16)).astype(jnp.float32)

@jax.custom_vjp
def low_back(v):
    return v

def low_keep(v):
    return (low(v), None)

def low_pass(kept, grad):
    return (grad,)

def back_keep(v):
    return (v, None)

def back_low(kept, grad):
    return (low(grad),)
low.defvjp(low_keep, low_pass)
low_back.defvjp(back_keep, back_low)
HIGHEST = lax.Precision.HIGHEST
SQRT_HALF = 0.7071067811865476
NORM_EPS = 1e-12

def product(left_op, right_op):
    return jnp.dot(left_op, right_op, precision=HIGHEST, preferred_element_type=jnp.float32)

def gelu_exact(values):
    return 0.5 * values * (1.0 + lax.erf(values * SQRT_HALF))

def standardize(summed):
    row_mean = lax.optimization_barrier(jnp.mean(summed, axis=-1, keepdims=True))
    centred = summed - row_mean
    variance = lax.optimization_barrier(jnp.mean(centred * centred, axis=-1, keepdims=True))
    return centred * lax.rsqrt(variance + NORM_EPS)

def span_levels():
    return [SPAN // 4, SPAN // 2, SPAN]

def attend_rows(queries, key_rows, value_rows, row_lens, row_span):
    tok_count, feat_width = queries.shape
    row_count = tok_count // row_span
    row_shape = (row_count, row_span, feat_width // HEAD_DIM, HEAD_DIM)
    query_part = queries.reshape(row_shape)
    key_part = key_rows.reshape(row_shape)
    value_part = value_rows.reshape(row_shape)
    raw = low_back(jnp.einsum('rqhd,rkhd->rhqk', query_part, key_part, precision=HIGHEST) * (1.0 / math.sqrt(HEAD_DIM)))
    allowed = (jnp.arange(row_span, dtype=jnp.int32)[None, :] < row_lens[:row_count][:, None])[:, None, None, :]
    scores = jnp.where(allowed, raw, -1000000000.0)
    row_top = lax.optimization_barrier(jnp.max(scores, axis=-1, keepdims=True))
    shifted = jnp.exp(scores - row_top)
    probs = shifted / lax.optimization_barrier(jnp.sum(shifted, axis=-1, keepdims=True))
    context = jnp.einsum('rhqk,rkhd->rqhd', low(probs), value_part, precision=HIGHEST)
    return context.reshape(tok_count, feat_width)

def row_mask(row_lens, row_span):
    tok_count = row_lens.shape[0] * (SPAN // 4)
    row_count = tok_count // row_span
    allowed = jnp.arange(row_span, dtype=jnp.int32)[None, :] < row_lens[:row_count][:, None]
    return allowed.reshape(tok_count).astype(jnp.float32)

def layer(params, inputs, row_lens, bucket):
    query_weight, query_bias, key_weight, value_weight, value_bias, output_weight, output_bias, first_gain, first_shift, hidden_weight, hidden_bias, return_weight, return_bias, second_gain, second_shift = params
    lowered = low(inputs)
    queries = low(low_back(product(lowered, query_weight) + query_bias))
    key_rows = low(low_back(product(lowered, key_weight)))
    value_rows = low(low_back(product(lowered, value_weight) + value_bias))
    branches = [functools.partial(attend_rows, row_span=level) for level in span_levels()]
    context = low(low_back(lax.switch(bucket, branches, queries, key_rows, value_rows, row_lens)))
    first_sum = inputs + low_back(product(context, output_weight) + output_bias)
    first_out = standardize(first_sum) * first_gain + first_shift
    hidden_pre = low_back(product(low(first_out), hidden_weight) + hidden_bias)
    hidden_act = low(gelu_exact(hidden_pre))
    second_sum = first_out + low_back(product(hidden_act, return_weight) + return_bias)
    return standardize(second_sum) * second_gain + second_shift

def reference(tokens, row_bucket, row_lengths, teacher_query_weight, teacher_query_bias, teacher_key_weight, teacher_value_weight, teacher_value_bias, teacher_output_weight, teacher_output_bias, teacher_first_gain, teacher_first_shift, teacher_hidden_weight, teacher_hidden_bias, teacher_return_weight, teacher_return_bias, teacher_second_gain, teacher_second_shift, student_query_weight, student_query_bias, student_key_weight, student_value_weight, student_value_bias, student_output_weight, student_output_bias, student_first_gain, student_first_shift, student_hidden_weight, student_hidden_bias, student_return_weight, student_return_bias, student_second_gain, student_second_shift):
    inputs = tokens.astype(jnp.float32).reshape(N_DP, TOK_DEV, D)
    teacher = tuple((item.astype(jnp.float32) for item in (teacher_query_weight, teacher_query_bias, teacher_key_weight, teacher_value_weight, teacher_value_bias, teacher_output_weight, teacher_output_bias, teacher_first_gain, teacher_first_shift, teacher_hidden_weight, teacher_hidden_bias, teacher_return_weight, teacher_return_bias, teacher_second_gain, teacher_second_shift)))
    student = tuple((item.astype(jnp.float32) for item in (student_query_weight, student_query_bias, student_key_weight, student_value_weight, student_value_bias, student_output_weight, student_output_bias, student_first_gain, student_first_shift, student_hidden_weight, student_hidden_bias, student_return_weight, student_return_bias, student_second_gain, student_second_shift)))

    def teach(item):
        shard, bucket, row_lens = item
        return layer(teacher, shard, row_lens, bucket)
    target = lax.map(teach, (inputs, row_bucket, row_lengths))

    def mask_shard(item):
        bucket, row_lens = item
        branches = [functools.partial(row_mask, row_span=level) for level in span_levels()]
        return lax.switch(bucket, branches, row_lens)
    masks = lax.map(mask_shard, (row_bucket, row_lengths))
    stepper = jax.checkpoint(layer)

    def total_loss(shards, params):

        def one_shard(item):
            shard, bucket, row_lens, goal, token_valid = item
            result = stepper(params, shard, row_lens, bucket)
            differ = (result - goal) * token_valid[:, None]
            return (result, 0.5 * jnp.sum(differ * differ))
        results, losses = lax.map(one_shard, (shards, row_bucket, row_lengths, target, masks))
        return (jnp.sum(losses), results)
    loss_value, pullback, results = jax.vjp(total_loss, inputs, student, has_aux=True)
    grad_inputs, grads = pullback(jnp.ones_like(loss_value))
    return (results.reshape(TOKENS, D), grad_inputs.reshape(TOKENS, D), grads[0], grads[1], grads[2], grads[3], grads[4], grads[5], grads[6], grads[7], grads[8], grads[9], grads[10], grads[11], grads[12], grads[13], grads[14])
```

```python
import functools
import math

import jax
import jax.numpy as jnp
from jax import lax
from jax.experimental import pallas as pl
from jax.experimental.pallas import tpu as pltpu
from jax.sharding import PartitionSpec as P

MESH = pl.DeviceIdType.MESH
HEAD_DIM = 64
SPAN = 512


NORM_EPS = 1e-12
SQRT_HALF = 0.7071067811865476


CW = 256
NZ, NY, NX = 4, 2, 2
ROWS = 48


class Place:
    def __init__(self):
        self.dp = lax.axis_index("dp")
        self.head = lax.axis_index("head")
        self.z = self.dp // 4
        self.y = lax.rem(self.dp // 2, 2)
        self.x = lax.rem(self.dp, 2)

    def at(self, dz=0, y=None, x=None):
        y = self.y if y is None else y
        x = self.x if x is None else x
        return ((self.z + dz) * 4 + y * 2 + x, self.head)


class Ring:
    def __init__(self, place, kinds, grad, pair_a, pair_b, path, zpath, zpair_a, zpair_b, send, recv, slot=None):
        self.p = place
        self.kinds = kinds
        self.grad, self.pair_a, self.pair_b, self.path = grad, pair_a, pair_b, path
        self.zpath, self.zpair_a, self.zpair_b = zpath, zpair_a, zpair_b
        self.send, self.recv = send, recv
        self.slot = slot or list(range(len(kinds)))
        flat = [c for c, k in enumerate(kinds) if not k.startswith("z")]
        deep = [c for c, k in enumerate(kinds) if k.startswith("z")]
        self.place_of = {c: i for i, c in enumerate(flat)} | {c: i for i, c in enumerate(deep)}

    def _pair(self, c, step):
        kind, p, i = self.kinds[c], self.p, self.place_of[c]
        g = self.grad.at[self.slot[c]]
        if kind.startswith("z"):
            axis = kind[1 + step]
            land = (self.zpair_a if step == 0 else self.zpair_b).at[i]
            view = g.at[p.z]
            if step == 0:
                pick = (lambda j: view.at[:, j]) if axis == "x" else (lambda j: view.at[j])
            else:
                pick = (lambda j: view.at[p.y, j]) if axis == "x" else (lambda j: view.at[j, p.x])
        else:
            axis = kind[step]
            land = (self.pair_a if step == 0 else self.pair_b).at[i]
            if step == 0:
                pick = (lambda j: g.at[:, :, j]) if axis == "x" else (lambda j: g.at[:, j])
            else:
                pick = (lambda j: g.at[:, p.y, j]) if axis == "x" else (lambda j: g.at[:, j, p.x])
        mine = p.x if axis == "x" else p.y
        to = p.at(x=1 - p.x) if axis == "x" else p.at(y=1 - p.y)
        copy = pltpu.make_async_remote_copy(
            src_ref=pick(1 - mine), dst_ref=land, send_sem=self.send.at[c, step], recv_sem=self.recv.at[c, step],
            device_id=to, device_id_type=MESH)
        return copy, pick(mine), land

    def pair_send(self, c, step):
        self._pair(c, step)[0].start()

    def pair_take(self, c, step):
        copy, mine, land = self._pair(c, step)
        copy.wait_recv()
        mine[...] += land[...]

    def _path_refs(self, c):
        kind, p, i = self.kinds[c], self.p, self.place_of[c]
        g = self.grad.at[self.slot[c]]
        if kind.startswith("z"):
            return (lambda lo, n: g.at[pl.ds(lo, n)]), self.zpath.at[i]
        return (lambda lo, n: g.at[pl.ds(lo, n), p.y, p.x]), self.path.at[i]

    def _hop(self, c, z, up):
        blocks, land = self._path_refs(c)
        if up:
            src, dst, k, dz = blocks(z + 1, 3 - z), land.at[pl.ds(0, 3 - z)], 2, 1
        else:
            src, dst, k, dz = blocks(0, z), land.at[pl.ds(5 - z, z)], 3, -1
        return pltpu.make_async_remote_copy(
            src_ref=src, dst_ref=dst, send_sem=self.send.at[c, k], recv_sem=self.recv.at[c, k],
            device_id=self.p.at(dz=dz), device_id_type=MESH)

    def path_start(self, c):
        @pl.when(self.p.z == 0)
        def _():
            self._hop(c, 0, True).start()

        @pl.when(self.p.z == 3)
        def _():
            self._hop(c, 3, False).start()

    def path_mid(self, c, first):
        blocks, land = self._path_refs(c)
        for z in (1, 2):
            up = (z == 1) == first

            @pl.when(self.p.z == z)
            def _(z=z, up=up):
                if up:
                    self._hop(c, z - 1, True).wait_recv()
                    own = blocks(z + 1, 3 - z)
                    own[...] += land[pl.ds(1, 3 - z)]
                    self._hop(c, z, True).start()
                else:
                    self._hop(c, z + 1, False).wait_recv()
                    own = blocks(0, z)
                    own[...] += land[pl.ds(4 - z, z)]
                    self._hop(c, z, False).start()

    def path_end(self, c):
        blocks, land = self._path_refs(c)
        for z in range(NZ):
            @pl.when(self.p.z == z)
            def _(z=z):
                if z == 0:
                    self._hop(c, 1, False).wait_recv()
                if z == 3:
                    self._hop(c, 2, True).wait_recv()
                own = blocks(z, 1)
                total = own[...]
                if z > 0:
                    total = total + land[pl.ds(0, 1)]
                if z < 3:
                    total = total + land[pl.ds(4, 1)]
                own[...] = total

    def drain(self, c):
        for step in (0, 1):
            self._pair(c, step)[0].wait_send()
        for z in range(NZ):
            @pl.when(self.p.z == z)
            def _(z=z):
                if z < 3:
                    self._hop(c, z, True).wait_send()
                if z > 0:
                    self._hop(c, z, False).wait_send()

    def stage(self, c, s):
        deep = self.kinds[c].startswith("z")
        if deep:
            if s == 0: self.path_start(c)
            elif s == 1: self.path_mid(c, True)
            elif s == 2: self.path_mid(c, False)
            elif s == 3: self.path_end(c); self.pair_send(c, 0)
            elif s == 4: self.pair_take(c, 0); self.pair_send(c, 1)
            elif s == 5: self.pair_take(c, 1)
        else:
            if s == 0: self.pair_send(c, 0)
            elif s == 1: self.pair_take(c, 0); self.pair_send(c, 1)
            elif s == 2: self.pair_take(c, 1); self.path_start(c)
            elif s == 3: self.path_mid(c, True)
            elif s == 4: self.path_mid(c, False)
            elif s == 5: self.path_end(c)

    def own(self, c):
        p = self.p
        return self.grad.at[self.slot[c], p.z, p.y, p.x]


def scratch(kinds, slots):
    flat = sum(not k.startswith("z") for k in kinds)
    deep = len(kinds) - flat
    f = jnp.float32
    return [
        pltpu.VMEM((slots, NZ, NY, NX, ROWS, CW), f),
        pltpu.VMEM((flat, NZ, 2, ROWS, CW), f),
        pltpu.VMEM((flat, NZ, ROWS, CW), f),
        pltpu.VMEM((flat, 5, ROWS, CW), f),
        pltpu.VMEM((max(deep, 1), 5, NY, NX, ROWS, CW), f),
        pltpu.VMEM((max(deep, 1), 2, ROWS, CW), f),
        pltpu.VMEM((max(deep, 1), ROWS, CW), f),
        pltpu.SemaphoreType.DMA((len(kinds), 4)),
        pltpu.SemaphoreType.DMA((len(kinds), 4)),
    ]


def greet(place):
    barrier = pltpu.get_barrier_semaphore()
    p = place
    for to in (p.at(x=1 - p.x), p.at(y=1 - p.y)):
        pl.semaphore_signal(barrier, inc=1, device_id=to, device_id_type=MESH)
    @pl.when(p.z < 3)
    def _():
        pl.semaphore_signal(barrier, inc=1, device_id=p.at(dz=1), device_id_type=MESH)
    @pl.when(p.z > 0)
    def _():
        pl.semaphore_signal(barrier, inc=1, device_id=p.at(dz=-1), device_id_type=MESH)
    @pl.when((p.z == 0) | (p.z == 3))
    def _():
        pl.semaphore_wait(barrier, 3)
    @pl.when((p.z == 1) | (p.z == 2))
    def _():
        pl.semaphore_wait(barrier, 4)


class Butterfly:
    def __init__(self, place, value, land, send, recv):
        self.p, self.value, self.land, self.send, self.recv = place, value, land, send, recv

    def partner(self, step):
        p = self.p
        if step == 0:
            return p.at(x=1 - p.x)
        if step == 1:
            return p.at(y=1 - p.y)
        if step == 2:
            return p.at(dz=1 - 2 * lax.rem(p.z, 2))
        return p.at(dz=2 - 4 * (p.z // 2))

    def _copy(self, step):
        return pltpu.make_async_remote_copy(
            src_ref=self.value.at[step], dst_ref=self.land.at[step], send_sem=self.send.at[step],
            recv_sem=self.recv.at[step], device_id=self.partner(step), device_id_type=MESH)

    def start(self, step):
        self._copy(step).start()

    def take(self, step):
        self._copy(step).wait_recv()
        self.value[step + 1] = self.value[step] + self.land[step]

    def drain(self):
        for step in range(4):
            self._copy(step).wait_send()


KINDS = ["zxy", "xy", "yx", "xy", "yx", "zyx", "xy", "yx", "xy", "yx", "zxy", "xy", "yx", "xy", "yx", "zyx", "xy", "yx"]


def wavefront(count, lag):
    items = sorted((c + lag * s, -s, c, s) for c in range(count) for s in range(6))
    return [(c, s) for _, _, c, s in items]


def scatter_kernel(grads, small, out, small_out, *refs):
    ring_refs, (load, value, land, vsend, vrecv) = refs[:9], refs[9:]
    place = Place()
    grad = ring_refs[0]
    count = grads.shape[0]
    for c in range(count):
        pltpu.make_async_copy(grads.at[c], grad.at[c], load.at[c]).start()
    value[0] = small[...]
    greet(place)
    ring = Ring(place, KINDS, *ring_refs)
    fly = Butterfly(place, value, land, vsend, vrecv)
    fly.start(0)
    for c, s in wavefront(count, 2):
        if s == 0:
            pltpu.make_async_copy(grads.at[c], grad.at[c], load.at[c]).wait()
        ring.stage(c, s)
        if s == 5:
            out[:, c * CW:(c + 1) * CW] = ring.own(c)[...]
        if s == 0 and c in (4, 6, 8, 10):
            step = (c - 4) // 2
            fly.take(step)
            if step < 3:
                fly.start(step + 1)
    small_out[...] = value[4]
    for c in range(count):
        ring.drain(c)
    fly.drain()


def scatter(grads, small):
    count = grads.shape[0]
    f = jnp.float32
    return pl.pallas_call(
        scatter_kernel,
        out_shape=(jax.ShapeDtypeStruct((ROWS, count * CW), f), jax.ShapeDtypeStruct(small.shape, f)),
        in_specs=[pl.BlockSpec(memory_space=pl.ANY), pl.BlockSpec(memory_space=pltpu.VMEM)],
        out_specs=(pl.BlockSpec(memory_space=pltpu.VMEM), pl.BlockSpec(memory_space=pltpu.VMEM)),
        scratch_shapes=scratch(KINDS, count) + [
            pltpu.SemaphoreType.DMA((count,)),
            pltpu.VMEM((5,) + small.shape, f),
            pltpu.VMEM((4,) + small.shape, f),
            pltpu.SemaphoreType.DMA((4,)),
            pltpu.SemaphoreType.DMA((4,)),
        ],
        compiler_params=pltpu.CompilerParams(collective_id=0, has_side_effects=True, vmem_limit_bytes=60 * 2**20),
    )(grads, small)


def by_kernel(mats, smalls):
    wide = jnp.concatenate([mats[5].T, mats[4], mats[3].T, mats[0], mats[1], mats[2]], axis=1)
    count = wide.shape[1] // CW
    grads = jnp.transpose(wide.reshape(NZ, NY, NX, ROWS, count, CW), (4, 0, 1, 2, 3, 5))
    flat = jnp.concatenate(smalls)
    small = jnp.pad(flat, (0, 7168 - flat.shape[0])).reshape(8, 896)
    out, small_out = scatter(grads, small)
    flat = small_out.reshape(-1)
    cuts, at = [], 0
    for item in smalls:
        cuts.append(flat[at:at + item.shape[0]])
        at += item.shape[0]
    ff = mats[5].shape[0]
    hw = mats[3].shape[0]
    pieces, at = [], 0
    for width in (ff, ff, hw, hw, hw, hw):
        pieces.append(out[:, at:at + width])
        at += width
    return (pieces[3], pieces[4], pieces[5], pieces[2].T, pieces[1], pieces[0].T), cuts


def gelu_exact(values):
    return 0.5 * values * (1.0 + lax.erf(values * SQRT_HALF))


def span_levels():
    return [SPAN // 4, SPAN // 2, SPAN]


def times_trans(left_op, right_op):
    return lax.dot_general(
        left_op, right_op, (((1,), (1,)), ((), ())), preferred_element_type=jnp.float32
    )


def trans_times(left_op, right_op):
    return lax.dot_general(
        left_op, right_op, (((0,), (0,)), ((), ())), preferred_element_type=jnp.float32
    )


def masked_scores(query_low, key_low, row_lens, row_span):
    tok_count, feat_width = query_low.shape
    row_count = tok_count // row_span
    row_shape = (row_count, row_span, feat_width // HEAD_DIM, HEAD_DIM)
    query_rows = query_low.reshape(row_shape)
    key_rows = key_low.reshape(row_shape)
    scores = jnp.einsum(
        "rqhd,rkhd->rhqk", query_rows, key_rows, preferred_element_type=jnp.float32
    ) * (1.0 / math.sqrt(HEAD_DIM))
    allowed = (jnp.arange(row_span, dtype=jnp.int32)[None, :] < row_lens[:row_count][:, None])[
        :, None, None, :
    ]
    return (jnp.where(allowed, scores, -1000000000.0), row_shape, query_rows, key_rows)


def attend(query_low, key_low, value_low, row_lens, row_span):
    scores, row_shape, query_rows, key_rows = masked_scores(query_low, key_low, row_lens, row_span)
    row_top = jnp.max(scores, axis=-1, keepdims=True)
    shifted = jnp.exp(scores - row_top)
    row_mass = jnp.sum(shifted, axis=-1, keepdims=True)
    probs_low = (shifted / row_mass).astype(jnp.bfloat16)
    context = jnp.einsum(
        "rhqk,rkhd->rqhd",
        probs_low,
        value_low.reshape(row_shape),
        preferred_element_type=jnp.float32,
    )
    logmass = jnp.transpose((row_top + jnp.log(row_mass))[..., 0], (1, 0, 2)).reshape(
        row_shape[2], query_low.shape[0]
    )
    return (context.reshape(query_low.shape), logmass)


def attend_back(query_low, key_low, value_low, logmass, grad_context, row_lens, row_span):
    scores, row_shape, query_rows, key_rows = masked_scores(query_low, key_low, row_lens, row_span)
    stored = jnp.transpose(logmass.reshape(row_shape[2], row_shape[0], row_span), (1, 0, 2))[
        ..., None
    ]
    probs = jnp.exp(scores - stored)
    grad_rows = grad_context.reshape(row_shape)
    grad_value = jnp.einsum(
        "rhqk,rqhd->rkhd", probs.astype(jnp.bfloat16), grad_rows, preferred_element_type=jnp.float32
    )
    grad_probs = jnp.einsum(
        "rqhd,rkhd->rhqk",
        grad_rows,
        value_low.reshape(row_shape),
        preferred_element_type=jnp.float32,
    )
    grad_scores = (
        probs * (grad_probs - jnp.sum(probs * grad_probs, axis=-1, keepdims=True))
    ).astype(jnp.bfloat16)
    score_scale = 1.0 / math.sqrt(HEAD_DIM)
    grad_query = (
        jnp.einsum("rhqk,rkhd->rqhd", grad_scores, key_rows, preferred_element_type=jnp.float32)
        * score_scale
    )
    grad_key = (
        jnp.einsum("rhqk,rqhd->rkhd", grad_scores, query_rows, preferred_element_type=jnp.float32)
        * score_scale
    )
    flat_shape = query_low.shape
    return (
        grad_query.reshape(flat_shape),
        grad_key.reshape(flat_shape),
        grad_value.reshape(flat_shape),
    )


def row_mask(row_lens, row_span, tok_count):
    row_count = tok_count // row_span
    allowed = jnp.arange(row_span, dtype=jnp.int32)[None, :] < row_lens[:row_count][:, None]
    return allowed.reshape(tok_count).astype(jnp.float32)


def standardize(summed):
    row_mean = jnp.mean(summed, axis=-1, keepdims=True)
    centred = summed - row_mean
    variance = jnp.mean(centred * centred, axis=-1, keepdims=True)
    inv_std = lax.rsqrt(variance + NORM_EPS)
    return (centred * inv_std, inv_std[:, 0])


def settle(partial_sum, bias_vec, residual, gain_vec, shift_vec):
    whole_sum = lax.psum(partial_sum, "head")
    normed, inv_std = standardize(whole_sum + bias_vec + residual)
    return (normed * gain_vec + shift_vec, normed, inv_std)


def norm_back(upstream, normed, inv_std, gain_vec):
    scaled = upstream * gain_vec
    centred = (
        scaled
        - jnp.mean(scaled, axis=-1, keepdims=True)
        - normed * jnp.mean(scaled * normed, axis=-1, keepdims=True)
    )
    return (
        inv_std[:, None] * centred,
        jnp.sum(upstream * normed, axis=0),
        jnp.sum(upstream, axis=0),
    )


def run_block(tokens, params, row_lens, bucket):
    (
        query_weight,
        query_bias,
        key_weight,
        value_weight,
        value_bias,
        output_weight,
        output_bias,
        first_gain,
        first_shift,
        hidden_weight,
        hidden_bias,
        return_weight,
        return_bias,
        second_gain,
        second_shift,
    ) = params
    residual = tokens.astype(jnp.float32)
    query_low = (
        jnp.dot(tokens, query_weight, preferred_element_type=jnp.float32) + query_bias
    ).astype(jnp.bfloat16)
    key_low = jnp.dot(tokens, key_weight, preferred_element_type=jnp.float32).astype(jnp.bfloat16)
    value_low = (
        jnp.dot(tokens, value_weight, preferred_element_type=jnp.float32) + value_bias
    ).astype(jnp.bfloat16)
    branches = [functools.partial(attend, row_span=level) for level in span_levels()]
    context, logmass = lax.switch(bucket, branches, query_low, key_low, value_low, row_lens)
    context_low = context.astype(jnp.bfloat16)
    first_out, first_normed, first_inv = settle(
        jnp.dot(context_low, output_weight, preferred_element_type=jnp.float32),
        output_bias,
        residual,
        first_gain,
        first_shift,
    )
    first_low = first_out.astype(jnp.bfloat16)
    hidden_pre = jnp.dot(first_low, hidden_weight, preferred_element_type=jnp.float32) + hidden_bias
    hidden_low = gelu_exact(hidden_pre).astype(jnp.bfloat16)
    block_out, second_normed, second_inv = settle(
        jnp.dot(hidden_low, return_weight, preferred_element_type=jnp.float32),
        return_bias,
        first_out,
        second_gain,
        second_shift,
    )
    kept = (
        query_low,
        key_low,
        value_low,
        logmass,
        context_low,
        first_normed,
        first_inv,
        first_low,
        hidden_pre,
        hidden_low,
        second_normed,
        second_inv,
    )
    return (block_out, kept)


def shards(
    tokens,
    row_bucket,
    row_lengths,
    teacher_query_weight,
    teacher_query_bias,
    teacher_key_weight,
    teacher_value_weight,
    teacher_value_bias,
    teacher_output_weight,
    teacher_output_bias,
    teacher_first_gain,
    teacher_first_shift,
    teacher_hidden_weight,
    teacher_hidden_bias,
    teacher_return_weight,
    teacher_return_bias,
    teacher_second_gain,
    teacher_second_shift,
    student_query_weight,
    student_query_bias,
    student_key_weight,
    student_value_weight,
    student_value_bias,
    student_output_weight,
    student_output_bias,
    student_first_gain,
    student_first_shift,
    student_hidden_weight,
    student_hidden_bias,
    student_return_weight,
    student_return_bias,
    student_second_gain,
    student_second_shift,
):
    row_lens = row_lengths[0]
    bucket = row_bucket[0]
    teacher = (
        teacher_query_weight,
        teacher_query_bias,
        teacher_key_weight,
        teacher_value_weight,
        teacher_value_bias,
        teacher_output_weight,
        teacher_output_bias,
        teacher_first_gain,
        teacher_first_shift,
        teacher_hidden_weight,
        teacher_hidden_bias,
        teacher_return_weight,
        teacher_return_bias,
        teacher_second_gain,
        teacher_second_shift,
    )
    student = (
        student_query_weight,
        student_query_bias,
        student_key_weight,
        student_value_weight,
        student_value_bias,
        student_output_weight,
        student_output_bias,
        student_first_gain,
        student_first_shift,
        student_hidden_weight,
        student_hidden_bias,
        student_return_weight,
        student_return_bias,
        student_second_gain,
        student_second_shift,
    )
    target, unused = run_block(tokens, teacher, row_lens, bucket)
    student_out, kept = run_block(tokens, student, row_lens, bucket)
    (
        query_low,
        key_low,
        value_low,
        logmass,
        context_low,
        first_normed,
        first_inv,
        first_low,
        hidden_pre,
        hidden_low,
        second_normed,
        second_inv,
    ) = kept
    mask_branches = [
        functools.partial(row_mask, row_span=level, tok_count=tokens.shape[0])
        for level in span_levels()
    ]
    token_valid = lax.switch(bucket, mask_branches, row_lens)
    upstream = (student_out - target) * token_valid[:, None]
    grad_second, grad_second_gain, grad_second_shift = norm_back(
        upstream, second_normed, second_inv, student_second_gain
    )
    return_low = grad_second.astype(jnp.bfloat16)
    grad_return_bias = jnp.sum(return_low.astype(jnp.float32), axis=0)
    grad_return_weight = trans_times(hidden_low, return_low)
    grad_hidden_out = times_trans(return_low, student_return_weight)
    unused_out, gelu_back = jax.vjp(gelu_exact, hidden_pre)
    hidden_grad_low = gelu_back(grad_hidden_out)[0].astype(jnp.bfloat16)
    grad_hidden_bias = jnp.sum(hidden_grad_low.astype(jnp.float32), axis=0)
    grad_hidden_weight = trans_times(first_low, hidden_grad_low)
    grad_first_in = grad_second + lax.psum(
        times_trans(hidden_grad_low, student_hidden_weight), "head"
    )
    grad_first, grad_first_gain, grad_first_shift = norm_back(
        grad_first_in, first_normed, first_inv, student_first_gain
    )
    output_low = grad_first.astype(jnp.bfloat16)
    grad_output_bias = jnp.sum(output_low.astype(jnp.float32), axis=0)
    grad_output_weight = trans_times(context_low, output_low)
    grad_context = times_trans(output_low, student_output_weight).astype(jnp.bfloat16)
    back_branches = [functools.partial(attend_back, row_span=level) for level in span_levels()]
    grad_query, grad_key, grad_value = lax.switch(
        bucket, back_branches, query_low, key_low, value_low, logmass, grad_context, row_lens
    )
    query_grad_low = grad_query.astype(jnp.bfloat16)
    key_grad_low = grad_key.astype(jnp.bfloat16)
    value_grad_low = grad_value.astype(jnp.bfloat16)
    grad_query_bias = jnp.sum(query_grad_low.astype(jnp.float32), axis=0)
    grad_value_bias = jnp.sum(value_grad_low.astype(jnp.float32), axis=0)
    grad_query_weight = trans_times(tokens, query_grad_low)
    grad_key_weight = trans_times(tokens, key_grad_low)
    grad_value_weight = trans_times(tokens, value_grad_low)
    partial_in = (
        times_trans(query_grad_low, student_query_weight)
        + times_trans(key_grad_low, student_key_weight)
        + times_trans(value_grad_low, student_value_weight)
    )
    input_grad = grad_first + lax.psum(partial_in, "head")
    mats = (grad_query_weight, grad_key_weight, grad_value_weight, grad_output_weight, grad_hidden_weight, grad_return_weight)
    smalls = (
        grad_query_bias,
        grad_value_bias,
        grad_output_bias,
        grad_first_gain,
        grad_first_shift,
        grad_hidden_bias,
        grad_return_bias,
        grad_second_gain,
        grad_second_shift,
    )
    if lax.axis_size("dp") == NZ * NY * NX:
        summed_mats, summed_small = by_kernel(mats, smalls)
    else:
        summed_mats = tuple(
            lax.psum_scatter(item, "dp", scatter_dimension=1 if i in (3, 5) else 0, tiled=True)
            for i, item in enumerate(mats)
        )
        summed_small = lax.psum(smalls, "dp")
    return (
        student_out,
        input_grad,
        summed_mats[0],
        summed_small[0],
        summed_mats[1],
        summed_mats[2],
        summed_small[1],
        summed_mats[3],
        summed_small[2],
        summed_small[3],
        summed_small[4],
        summed_mats[4],
        summed_small[5],
        summed_mats[5],
        summed_small[6],
        summed_small[7],
        summed_small[8],
    )


def solution(mesh):
    placed = (
        P("dp", None),
        P("dp"),
        P("dp", None),
        P(None, "head"),
        P("head"),
        P(None, "head"),
        P(None, "head"),
        P("head"),
        P("head", None),
        P(),
        P(),
        P(),
        P(None, "head"),
        P("head"),
        P("head", None),
        P(),
        P(),
        P(),
        P(None, "head"),
        P("head"),
        P(None, "head"),
        P(None, "head"),
        P("head"),
        P("head", None),
        P(),
        P(),
        P(),
        P(None, "head"),
        P("head"),
        P("head", None),
        P(),
        P(),
        P(),
    )
    return jax.shard_map(
        shards,
        mesh=mesh,
        in_specs=placed,
        out_specs=(
            P("dp", None),
            P("dp", None),
            P("dp", "head"),
            P("head"),
            P("dp", "head"),
            P("dp", "head"),
            P("head"),
            P("head", "dp"),
            P(),
            P(),
            P(),
            P("dp", "head"),
            P("head"),
            P("head", "dp"),
            P(),
            P(),
            P(),
        ),
        check_vma=False,
    )
```

```python
import functools

import jax
import jax.numpy as jnp
from jax import lax
from jax.experimental import pallas as pl
from jax.experimental.pallas import tpu as pltpu
from jax.sharding import PartitionSpec as P

MESH = pl.DeviceIdType.MESH
HEAD_DIM = 64
SPAN = 512
NORM_EPS = 1e-12
SQRT_HALF = 0.7071067811865476
F32, BF16 = jnp.float32, jnp.bfloat16
VMEM_BYTES = 62 * 2**20


def nn(a, b):
    return jnp.dot(a, b, preferred_element_type=F32)


def nt(a, b):
    return lax.dot_general(a, b, (((1,), (1,)), ((), ())), preferred_element_type=F32)


def tn(a, b):
    return lax.dot_general(a, b, (((0,), (0,)), ((), ())), preferred_element_type=F32)


def row_layout(bucket, lens, slots):
    shift = jnp.where(bucket == 0, SPAN // 4, jnp.where(bucket == 1, SPAN // 2, SPAN))
    row = jnp.where(bucket == 0, slots // (SPAN // 4), jnp.where(bucket == 1, slots // (SPAN // 2), slots // SPAN))
    length = jnp.zeros_like(slots)
    for j in range(8):
        length = jnp.where(row == j, lens[0, j], length)
    return row, (slots - row * shift) < length


def fill_masks(bucket, lens, bias, valid):
    code = bucket[0]
    for b in range(bias.shape[0]):
        q = b * SPAN + lax.broadcasted_iota(jnp.int32, (SPAN, 1), 0)
        k = b * SPAN + lax.broadcasted_iota(jnp.int32, (1, SPAN), 1)
        q_row, q_ok = row_layout(code, lens, q)
        k_row, k_ok = row_layout(code, lens, k)
        k_row = jnp.where(k_ok, k_row, -1)
        bias[b] = jnp.where(q_row == k_row, 0.0, -1000000000.0)
        if valid is not None:
            valid[b] = jnp.broadcast_to(jnp.where(q_ok, 1.0, 0.0), valid.shape[1:])


def lane_half():
    return lax.broadcasted_iota(jnp.int32, (1, 128), 1) < HEAD_DIM


def attention(q, k, v, bias, ctx):
    low = lane_half()
    for pair in range(q.shape[1] // 128):
        cols = pl.ds(pair * 128, 128)
        q2, k2, v2 = q[:, cols], k[:, cols], v[:, cols]
        parts = []
        for side in (low, ~low):
            s = nt(jnp.where(side, q2, jnp.zeros_like(q2)), k2) + bias[...]
            e = jnp.exp(s - jnp.max(s, axis=1, keepdims=True))
            mass = jnp.sum(e, axis=1, keepdims=True)
            parts.append(nn(e.astype(BF16), v2) * (1.0 / mass))
        ctx[:, cols] = jnp.where(low, parts[0], parts[1]).astype(BF16)


def standardize(z):
    centred = z - jnp.mean(z, axis=-1, keepdims=True)
    inv = lax.rsqrt(jnp.mean(centred * centred, axis=-1, keepdims=True) + NORM_EPS)
    return centred * inv, inv


TILE = 128


def tiles(rows, body):
    def step(i, carry):
        body(pl.ds(pl.multiple_of(i * TILE, TILE), TILE))
        return carry
    lax.fori_loop(0, rows // TILE, step, 0)


def forward_kernel(*refs):
    (bucket, lens, tokens_h, *rest) = refs
    th, rest = rest[:6], rest[6:]
    sh, rest = rest[:6], rest[6:]
    tb, rest = rest[:9], rest[9:]
    sb, rest = rest[:9], rest[9:]
    (out_h, q_h, k_h, v_h, ctx_h, n1_h, r1_h, h1_h, f_h, dz_h, dm_h, sums), rest = rest[:12], rest[12:]
    vecs, vsem, *rest = rest
    vectors = []
    for i, src in enumerate((*tb, *sb)):
        vectors.append(pltpu.make_async_copy(src, vecs.at[i, 0, pl.ds(0, src.shape[0])], vsem.at[i]))
    for item in vectors:
        item.start()
    tb, sb = ([vecs.at[base + i, :, pl.ds(0, src.shape[0])] for i, src in enumerate(group)]
              for base, group in ((0, tb), (9, sb)))
    (tok, t_qkv, t_o, t_1, t_2, s_qkv, s_o, s_1, s_2, q, k, v, ctx, n1, r1, h1, f, tq, tk, tv, tctx, th1b, tf,
     target, own, land, bias, valid, dm, wsem, osem, ssem, rsem) = rest
    dp, head = lax.axis_index("dp"), lax.axis_index("head")
    hw = q.shape[2]

    loads = [pltpu.make_async_copy(tokens_h, tok, wsem.at[0])]
    for base, src, qkv, o, one, two in ((1, th, t_qkv, t_o, t_1, t_2), (7, sh, s_qkv, s_o, s_1, s_2)):
        for j in range(3):
            loads.append(pltpu.make_async_copy(src[j], qkv.at[:, pl.ds(j * hw, hw)], wsem.at[base + j]))
        for j, dst in enumerate((o, one, two)):
            loads.append(pltpu.make_async_copy(src[3 + j], dst, wsem.at[base + 3 + j]))
    for item in loads:
        item.start()

    barrier = pltpu.get_barrier_semaphore()
    pl.semaphore_signal(barrier, inc=1, device_id=(dp, 1 - head), device_id_type=MESH)
    fill_masks(bucket, lens, bias, valid)
    sums[...] = jnp.zeros_like(sums)
    pl.semaphore_wait(barrier, 1)

    def swap(slot):
        return pltpu.make_async_remote_copy(
            src_ref=own.at[slot], dst_ref=land.at[slot], send_sem=ssem.at[slot], recv_sem=rsem.at[slot],
            device_id=(dp, 1 - head), device_id_type=MESH)

    def half(b):
        return pl.ds(pl.multiple_of(b * SPAN, SPAN), SPAN)

    def project(a, w, vectors, q, k, v):
        bq, bv = vectors
        q[...] = ((nn(a, w[:, 0:hw]) + bq[...]).astype(BF16).astype(F32) * (1.0 / 8.0)).astype(BF16)
        k[...] = nn(a, w[:, hw:2 * hw]).astype(BF16)
        v[...] = (nn(a, w[:, 2 * hw:3 * hw]) + bv[...]).astype(BF16)

    def feed(h1b, w1, b1, w2, f, slot):
        for j in range(w1.shape[1] // 256):
            cols = pl.ds(j * 256, 256)
            u = nn(h1b[...], w1[:, cols]) + b1[:, cols]
            f[:, cols] = (0.5 * u * (1.0 + lax.erf(u * SQRT_HALF))).astype(BF16)
        own[slot] = nn(f[...], w2[...])

    def whole(slot, rows, bias_vec, residual):
        return residual + ((own[slot, rows, :] + land[slot, rows, :]) + bias_vec[...])

    def teach_attend(b, carry):
        project(tok[half(b), :], t_qkv, tb[:2], tq, tk, tv)
        attention(tq, tk, tv, bias.at[b], tctx)
        own[b] = nn(tctx[...], t_o[...])
        swap(b).start()
        return carry

    def teach_feed(b, carry):
        swap(b).wait()

        def norm(rows):
            at = pl.ds(pl.multiple_of(b * SPAN + rows.start, TILE), TILE)
            n, _ = standardize(whole(b, rows, tb[2], tok[at, :].astype(F32)))
            h = n * tb[3][...] + tb[4][...]
            target[b, rows, :] = h
            th1b[rows, :] = h.astype(BF16)
        tiles(SPAN, norm)
        feed(th1b, t_1, tb[5], t_2, tf, 2 + b)
        swap(2 + b).start()
        return carry

    def study_attend(b, carry):
        swap(2 + b).wait()

        def norm(rows):
            n, _ = standardize(whole(2 + b, rows, tb[6], target[b, rows, :]))
            target[b, rows, :] = n * tb[7][...] + tb[8][...]
        tiles(SPAN, norm)
        project(tok[half(b), :], s_qkv, sb[:2], q.at[b], k.at[b], v.at[b])
        attention(q.at[b], k.at[b], v.at[b], bias.at[b], ctx.at[b])
        own[b] = nn(ctx[b], s_o[...])
        swap(b).start()
        return carry

    def study_feed(b, carry):
        @pl.when(b == 0)
        def _():
            swap(0).wait()

        def norm(rows):
            at = pl.ds(pl.multiple_of(b * SPAN + rows.start, TILE), TILE)
            n, r = standardize(whole(b, rows, sb[2], tok[at, :].astype(F32)))
            n1[b, rows, :] = n
            r1[b, rows, :] = jnp.broadcast_to(r, (TILE, 128))
            h1[b, rows, :] = (n * sb[3][...] + sb[4][...]).astype(BF16)
        tiles(SPAN, norm)
        feed(h1.at[b], s_1, sb[5], s_2, f.at[b], 2 + b)

        @pl.when(b == 0)
        def _():
            swap(1).wait()
        swap(2 + b).start()
        return carry

    def study_end(b, carry):
        swap(2 + b).wait()

        def norm(rows):
            residual = n1[b, rows, :] * sb[3][...] + sb[4][...]
            n2, r2 = standardize(whole(2 + b, rows, sb[6], residual))
            result = n2 * sb[7][...] + sb[8][...]
            dy = (result - target[b, rows, :]) * valid[b, rows, 0:1]
            target[b, rows, :] = result
            scaled = dy * sb[7][...]
            dz = r2 * (scaled - jnp.mean(scaled, axis=-1, keepdims=True) - n2 * jnp.mean(scaled * n2, axis=-1, keepdims=True))
            own[b, rows, :] = dz
            low = dz.astype(BF16)
            dm[b, rows, :] = low
            sums[0:1, :] += jnp.sum(low.astype(F32), axis=0, keepdims=True)
            sums[1:2, :] += jnp.sum(dy * n2, axis=0, keepdims=True)
            sums[2:3, :] += jnp.sum(dy, axis=0, keepdims=True)
        tiles(SPAN, norm)
        return carry

    for item in vectors:
        item.wait()
    for item in loads[0:4]:
        item.wait()
    loads[4].wait()
    lax.fori_loop(0, 2, teach_attend, 0)
    for item in loads[5:7]:
        item.wait()
    lax.fori_loop(0, 2, teach_feed, 0)
    for item in loads[7:11]:
        item.wait()
    lax.fori_loop(0, 2, study_attend, 0)
    stores = []

    def store(src, dst):
        copy = pltpu.make_async_copy(src, dst, osem.at[len(stores)])
        copy.start()
        stores.append(copy)
    for src, dst in ((q, q_h), (k, k_h), (v, v_h), (ctx, ctx_h)):
        store(src, dst)
    for item in loads[11:13]:
        item.wait()
    lax.fori_loop(0, 2, study_feed, 0)
    for src, dst in ((n1, n1_h), (r1, r1_h), (h1, h1_h), (f, f_h)):
        store(src, dst)
    lax.fori_loop(0, 2, study_end, 0)
    store(dm, dm_h)
    store(own.at[pl.ds(0, 2)], dz_h)
    store(target, out_h)
    for item in stores:
        item.wait()


def forward(tokens, bucket, lens, teacher, student):
    def cut(layer):
        wq, bq, wk, wv, bv, wo, bo, g1, s1, w1, b1, w2, b2, g2, s2 = layer
        return [wq, wk, wv, wo, w1, w2], [bq, bv, bo, g1, s1, b1, b2, g2, s2]
    tw, tv = cut(teacher)
    sw, sv = cut(student)
    toks, d = tokens.shape
    hw, fw = tw[0].shape[1], tw[4].shape[1]
    halves = toks // SPAN
    hbm, vmem, smem = (pl.BlockSpec(memory_space=m) for m in (pl.ANY, pltpu.VMEM, pltpu.SMEM))
    def S(*shape, dtype=F32):
        return jax.ShapeDtypeStruct(shape, dtype)
    def V(*shape, dtype=F32):
        return pltpu.VMEM(shape, dtype)
    b = BF16
    outs = (S(halves, SPAN, d), S(halves, SPAN, hw, dtype=b), S(halves, SPAN, hw, dtype=b), S(halves, SPAN, hw, dtype=b),
            S(halves, SPAN, hw, dtype=b), S(halves, SPAN, d), S(halves, SPAN, 128), S(halves, SPAN, d, dtype=b),
            S(halves, SPAN, fw, dtype=b), S(halves, SPAN, d), S(halves, SPAN, d, dtype=b), S(8, d))
    weights = [V(d, 3 * hw, dtype=b), V(hw, d, dtype=b), V(d, fw, dtype=b), V(fw, d, dtype=b)]
    return pl.pallas_call(
        forward_kernel,
        out_shape=outs,
        in_specs=[smem, smem, hbm] + [hbm] * 30,
        out_specs=(hbm,) * 11 + (vmem,),
        scratch_shapes=[V(18, 1, fw), pltpu.SemaphoreType.DMA((18,)), V(toks, d, dtype=b)] + weights + weights
        + [V(halves, SPAN, hw, dtype=b)] * 4 + [V(halves, SPAN, d), V(halves, SPAN, 128), V(halves, SPAN, d, dtype=b), V(halves, SPAN, fw, dtype=b)]
        + [V(SPAN, hw, dtype=b)] * 4 + [V(SPAN, d, dtype=b), V(SPAN, fw, dtype=b)]
        + [V(halves, SPAN, d), V(4, SPAN, d), V(4, SPAN, d), V(halves, SPAN, SPAN), V(halves, SPAN, 128), V(halves, SPAN, d, dtype=b)]
        + [pltpu.SemaphoreType.DMA((13,)), pltpu.SemaphoreType.DMA((11,)), pltpu.SemaphoreType.DMA((4,)), pltpu.SemaphoreType.DMA((4,))],
        compiler_params=pltpu.CompilerParams(collective_id=1, has_side_effects=True, vmem_limit_bytes=VMEM_BYTES),
    )(bucket, lens, tokens, *tw, *sw, *tv, *sv)


CW = 256
NZ, NY, NX = 4, 2, 2
ROWS = 48


class Place:
    def __init__(self):
        self.dp = lax.axis_index("dp")
        self.head = lax.axis_index("head")
        self.z = self.dp // 4
        self.y = lax.rem(self.dp // 2, 2)
        self.x = lax.rem(self.dp, 2)

    def at(self, dz=0, y=None, x=None):
        y = self.y if y is None else y
        x = self.x if x is None else x
        return ((self.z + dz) * 4 + y * 2 + x, self.head)


class Ring:
    def __init__(self, place, kinds, grad, pair_a, pair_b, path, zpath, zpair_a, zpair_b, send, recv, slot=None):
        self.p = place
        self.kinds = kinds
        self.grad, self.pair_a, self.pair_b, self.path = grad, pair_a, pair_b, path
        self.zpath, self.zpair_a, self.zpair_b = zpath, zpair_a, zpair_b
        self.send, self.recv = send, recv
        self.slot = slot or list(range(len(kinds)))
        flat = [c for c, k in enumerate(kinds) if not k.startswith("z")]
        deep = [c for c, k in enumerate(kinds) if k.startswith("z")]
        self.place_of = {c: i for i, c in enumerate(flat)} | {c: i for i, c in enumerate(deep)}

    def _pair(self, c, step):
        kind, p, i = self.kinds[c], self.p, self.place_of[c]
        g = self.grad.at[self.slot[c]]
        if kind.startswith("z"):
            axis = kind[1 + step]
            land = (self.zpair_a if step == 0 else self.zpair_b).at[i]
            view = g.at[p.z]
            if step == 0:
                pick = (lambda j: view.at[:, j]) if axis == "x" else (lambda j: view.at[j])
            else:
                pick = (lambda j: view.at[p.y, j]) if axis == "x" else (lambda j: view.at[j, p.x])
        else:
            axis = kind[step]
            land = (self.pair_a if step == 0 else self.pair_b).at[i]
            if step == 0:
                pick = (lambda j: g.at[:, :, j]) if axis == "x" else (lambda j: g.at[:, j])
            else:
                pick = (lambda j: g.at[:, p.y, j]) if axis == "x" else (lambda j: g.at[:, j, p.x])
        mine = p.x if axis == "x" else p.y
        to = p.at(x=1 - p.x) if axis == "x" else p.at(y=1 - p.y)
        copy = pltpu.make_async_remote_copy(
            src_ref=pick(1 - mine), dst_ref=land, send_sem=self.send.at[c, step], recv_sem=self.recv.at[c, step],
            device_id=to, device_id_type=MESH)
        return copy, pick(mine), land

    def pair_send(self, c, step):
        self._pair(c, step)[0].start()

    def pair_take(self, c, step):
        copy, mine, land = self._pair(c, step)
        copy.wait_recv()
        mine[...] += land[...]

    def _path_refs(self, c):
        kind, p, i = self.kinds[c], self.p, self.place_of[c]
        g = self.grad.at[self.slot[c]]
        if kind.startswith("z"):
            return (lambda lo, n: g.at[pl.ds(lo, n)]), self.zpath.at[i]
        return (lambda lo, n: g.at[pl.ds(lo, n), p.y, p.x]), self.path.at[i]

    def _hop(self, c, z, up):
        blocks, land = self._path_refs(c)
        if up:
            src, dst, k, dz = blocks(z + 1, 3 - z), land.at[pl.ds(0, 3 - z)], 2, 1
        else:
            src, dst, k, dz = blocks(0, z), land.at[pl.ds(5 - z, z)], 3, -1
        return pltpu.make_async_remote_copy(
            src_ref=src, dst_ref=dst, send_sem=self.send.at[c, k], recv_sem=self.recv.at[c, k],
            device_id=self.p.at(dz=dz), device_id_type=MESH)

    def path_start(self, c):
        @pl.when(self.p.z == 0)
        def _():
            self._hop(c, 0, True).start()

        @pl.when(self.p.z == 3)
        def _():
            self._hop(c, 3, False).start()

    def path_mid(self, c, first):
        blocks, land = self._path_refs(c)
        for z in (1, 2):
            up = (z == 1) == first

            @pl.when(self.p.z == z)
            def _(z=z, up=up):
                if up:
                    self._hop(c, z - 1, True).wait_recv()
                    own = blocks(z + 1, 3 - z)
                    own[...] += land[pl.ds(1, 3 - z)]
                    self._hop(c, z, True).start()
                else:
                    self._hop(c, z + 1, False).wait_recv()
                    own = blocks(0, z)
                    own[...] += land[pl.ds(4 - z, z)]
                    self._hop(c, z, False).start()

    def path_end(self, c):
        blocks, land = self._path_refs(c)
        for z in range(NZ):
            @pl.when(self.p.z == z)
            def _(z=z):
                if z == 0:
                    self._hop(c, 1, False).wait_recv()
                if z == 3:
                    self._hop(c, 2, True).wait_recv()
                own = blocks(z, 1)
                total = own[...]
                if z > 0:
                    total = total + land[pl.ds(0, 1)]
                if z < 3:
                    total = total + land[pl.ds(4, 1)]
                own[...] = total

    def drain(self, c):
        for step in (0, 1):
            self._pair(c, step)[0].wait_send()
        for z in range(NZ):
            @pl.when(self.p.z == z)
            def _(z=z):
                if z < 3:
                    self._hop(c, z, True).wait_send()
                if z > 0:
                    self._hop(c, z, False).wait_send()

    def stage(self, c, s):
        deep = self.kinds[c].startswith("z")
        if deep:
            if s == 0: self.path_start(c)
            elif s == 1: self.path_mid(c, True)
            elif s == 2: self.path_mid(c, False)
            elif s == 3: self.path_end(c); self.pair_send(c, 0)
            elif s == 4: self.pair_take(c, 0); self.pair_send(c, 1)
            elif s == 5: self.pair_take(c, 1)
        else:
            if s == 0: self.pair_send(c, 0)
            elif s == 1: self.pair_take(c, 0); self.pair_send(c, 1)
            elif s == 2: self.pair_take(c, 1); self.path_start(c)
            elif s == 3: self.path_mid(c, True)
            elif s == 4: self.path_mid(c, False)
            elif s == 5: self.path_end(c)

    def own(self, c):
        p = self.p
        return self.grad.at[self.slot[c], p.z, p.y, p.x]


def ring_scratch(kinds, slots):
    flat = sum(not k.startswith("z") for k in kinds)
    deep = len(kinds) - flat
    f = jnp.float32
    return [
        pltpu.VMEM((slots, NZ, NY, NX, ROWS, CW), f),
        pltpu.VMEM((flat, NZ, 2, ROWS, CW), f),
        pltpu.VMEM((flat, NZ, ROWS, CW), f),
        pltpu.VMEM((flat, 5, ROWS, CW), f),
        pltpu.VMEM((max(deep, 1), 5, NY, NX, ROWS, CW), f),
        pltpu.VMEM((max(deep, 1), 2, ROWS, CW), f),
        pltpu.VMEM((max(deep, 1), ROWS, CW), f),
        pltpu.SemaphoreType.DMA((len(kinds), 4)),
        pltpu.SemaphoreType.DMA((len(kinds), 4)),
    ]


INV_SQRT_2PI = 0.3989422804014327


class Butterfly:
    def __init__(self, place, value, land, send, recv):
        self.p, self.value, self.land, self.send, self.recv = place, value, land, send, recv

    def partner(self, step):
        p = self.p
        if step == 0:
            return p.at(x=1 - p.x)
        if step == 1:
            return p.at(y=1 - p.y)
        if step == 2:
            return p.at(dz=1 - 2 * lax.rem(p.z, 2))
        return p.at(dz=2 - 4 * (p.z // 2))

    def _copy(self, step):
        return pltpu.make_async_remote_copy(
            src_ref=self.value.at[step], dst_ref=self.land.at[step], send_sem=self.send.at[step],
            recv_sem=self.recv.at[step], device_id=self.partner(step), device_id_type=MESH)

    def start(self, step):
        self._copy(step).start()

    def take(self, step):
        self._copy(step).wait_recv()
        self.value[step + 1] = self.value[step] + self.land[step]

    def drain(self):
        for step in range(4):
            self._copy(step).wait_send()


def greet_all(p, scatter):
    barrier = pltpu.get_barrier_semaphore()

    def hello(to):
        pl.semaphore_signal(barrier, inc=1, device_id=to, device_id_type=MESH)
    hello((p.dp, 1 - p.head))
    if not scatter:
        return lambda: pl.semaphore_wait(barrier, 1)
    hello(p.at(x=1 - p.x))
    hello(p.at(y=1 - p.y))
    for dz in (1, -1):
        @pl.when((p.z + dz >= 0) & (p.z + dz < NZ))
        def _(dz=dz):
            hello(p.at(dz=dz))
    hello(p.at(dz=2 - 4 * (p.z // 2)))

    def wait():
        inner = (p.z == 1) | (p.z == 2)

        @pl.when(inner)
        def _():
            pl.semaphore_wait(barrier, 6)

        @pl.when(~inner)
        def _():
            pl.semaphore_wait(barrier, 5)
    return wait


def gelu_slope(u):
    return 0.5 * (1.0 + lax.erf(u * SQRT_HALF)) + u * (INV_SQRT_2PI * jnp.exp(-0.5 * u * u))


def backward_kernel(scatter, kinds, program, *refs):
    (bucket, lens, sums, tokens_h, q_h, k_h, v_h, ctx_h, n1_h, r1_h, h1_h, f_h, dz_h, dm_h,
     wq_h, wk_h, wv_h, wo_h, w1_h, w2_h, b1_h, g1_h), rest = refs[:22], refs[22:]
    if scatter:
        (grad_in_h, gq, gk, gv, go, g1w, g2w, *small_outs), rest = rest[:16], rest[16:]
    else:
        (grad_in_h, wide_h, small_out), rest = rest[:3], rest[3:]
    (tok, dz, n1, r1, own, land, b1, g1, value, vland, lsem, asem, osem, ssem, rsem, credit, vsend, vrecv, *ring_refs) = rest
    p = Place()
    dp, head = p.dp, p.head
    grad = ring_refs[0]
    ready = greet_all(p, scatter)
    hw = q_h.shape[2]
    d = dz.shape[2]
    fw = w1_h.shape[1]

    def start(src, dst, sem):
        copy = pltpu.make_async_copy(src, dst, sem)
        copy.start()
        return copy

    def swap(slot):
        return pltpu.make_async_remote_copy(
            src_ref=own.at[slot], dst_ref=land.at[slot], send_sem=ssem.at[slot], recv_sem=rsem.at[slot],
            device_id=(dp, 1 - head), device_id_type=MESH)

    def put(c, cols, block):
        g = grad.at[ring.slot[c]] if scatter else grad.at[c]
        for i in range(NZ * NY * NX):
            z, y, x = i // 4, i // 2 % 2, i % 2
            g[z, y, x, :, cols] = block[i * ROWS:(i + 1) * ROWS]

    if scatter:
        ring = Ring(p, kinds, *ring_refs)
    all_cols = pl.ds(0, CW)

    def run(items, compute):
        for item in items:
            if item[0] == "c":
                compute[item[2]]()
            elif scatter:
                ring.stage(*item)

    cut = next(i for i, item in enumerate(program) if item[0] == "c" and item[2] == 19)

    def feed_part(f, dm, h1, w1, w2):
        got = {}
        for i, (name, src, dst) in enumerate((
                ("dm", dm_h, dm), ("f", f_h, f), ("h1", h1_h, h1), ("w2", w2_h, w2), ("w1", w1_h, w1), ("b1", b1_h, b1.at[0]),
                ("dz", dz_h, dz), ("n1", n1_h, n1), ("r1", r1_h, r1), ("g1", g1_h, g1.at[0]), ("tok", tokens_h, tok))):
            got[name] = start(src, dst, lsem.at[i])
        value[...] = jnp.zeros_like(value)

        def need(*names):
            for name in names:
                got.pop(name).wait() if name in got else None
        compute = {}

        def return_grad(c):
            need("dm", "f")
            cols = pl.ds(c * CW, CW)
            left, right = dm[...].reshape(-1, d), f[:, :, cols].reshape(-1, CW)
            put(c, all_cols, tn(left, right))
            if c == 0:
                ready()
        for c in range(6):
            compute[c] = functools.partial(return_grad, c)

        def slope(j):
            need("h1", "w2", "w1", "b1")
            cols = pl.ds(j * CW, CW)

            def half(b, total):
                u = nn(h1[b], w1[:, cols]) + b1[0:1, cols]
                g = nt(dm[b], w2[cols, :])
                du = (g * gelu_slope(u)).astype(BF16)
                f[b, :, cols] = du
                return total + jnp.sum(du.astype(F32), axis=0, keepdims=True)
            total = lax.fori_loop(0, 2, half, jnp.zeros((1, CW), F32))
            value[0, 6 + j // 3:7 + j // 3, pl.ds(j % 3 * CW, CW)] = total

        def hidden_grad(j):
            cols = pl.ds(j * CW, CW)
            put(6 + j, all_cols, tn(h1[...].reshape(-1, d), f[:, :, cols].reshape(-1, CW)))
        for j in range(6):
            compute[6 + 2 * j] = functools.partial(slope, j)
            compute[7 + 2 * j] = functools.partial(hidden_grad, j)

        def back_first():
            def half(b, carry):
                own[b] = nt(f[b], w1[...])
                swap(b).start()
                return carry
            lax.fori_loop(0, 2, half, 0)
            need(*list(got))
        compute[18] = back_first
        run(program[:cut], compute)

    pl.run_scoped(feed_part, pltpu.VMEM(f_h.shape, BF16), pltpu.VMEM(dm_h.shape, BF16), pltpu.VMEM(h1_h.shape, BF16),
                  pltpu.VMEM(w1_h.shape, BF16), pltpu.VMEM(w2_h.shape, BF16))

    def attend_part(q, k, v, ctx, dctx, do, bias, wqkv, wo):
        got = {}
        for i, (name, src, dst) in enumerate((
                ("wo", wo_h, wo), ("q", q_h, q), ("k", k_h, k), ("v", v_h, v), ("ctx", ctx_h, ctx),
                ("wq", wq_h, wqkv.at[:, pl.ds(0, hw)]), ("wk", wk_h, wqkv.at[:, pl.ds(hw, hw)]),
                ("wv", wv_h, wqkv.at[:, pl.ds(2 * hw, hw)]))):
            got[name] = start(src, dst, asem.at[i])
        fill_masks(bucket, lens, bias, None)
        compute = {}

        def norm_back():
            def half(b, carry):
                swap(b).wait()

                def tile(rows):
                    up = dz[b, rows, :] + (own[b, rows, :] + land[b, rows, :])
                    n = n1[b, rows, :]
                    scaled = up * g1[0:1, :]
                    out = r1[b, rows, 0:1] * (scaled - jnp.mean(scaled, axis=-1, keepdims=True)
                                              - n * jnp.mean(scaled * n, axis=-1, keepdims=True))
                    dz[b, rows, :] = out
                    low = out.astype(BF16)
                    do[b, rows, :] = low
                    value[0, 0:1, 0:d] += jnp.sum(low.astype(F32), axis=0, keepdims=True)
                    value[0, 1:2, 0:d] += jnp.sum(up * n, axis=0, keepdims=True)
                    value[0, 2:3, 0:d] += jnp.sum(up, axis=0, keepdims=True)
                tiles(SPAN, tile)
                return carry
            lax.fori_loop(0, 2, half, 0)
            pl.semaphore_signal(credit, inc=1, device_id=(dp, 1 - head), device_id_type=MESH)
            value[0, 3:6, 0:d] = sums[0:3, :]
        compute[19] = norm_back

        def context_grad():
            got["wo"].wait()

            def half(b, carry):
                dctx[b] = nt(do[b], wo[...]).astype(BF16)
                return carry
            lax.fori_loop(0, 2, half, 0)
            for name in ("q", "k", "v", "ctx"):
                got[name].wait()
        compute[20] = context_grad

        def attend_back(pair, b):
            low_side = lane_half()
            cols = pl.ds(pair * 128, 128)
            q2, k2, v2, dc2 = q[b, :, cols], k[b, :, cols], v[b, :, cols], dctx[b, :, cols]
            parts = []
            for side in (low_side, ~low_side):
                zero = jnp.zeros_like(q2)
                s = nt(jnp.where(side, q2, zero), k2) + bias[b]
                e = jnp.exp(s - jnp.max(s, axis=1, keepdims=True))
                probs = e * (1.0 / jnp.sum(e, axis=1, keepdims=True))
                dprob = nt(jnp.where(side, dc2, zero), v2)
                ds = (probs * (dprob - jnp.sum(probs * dprob, axis=1, keepdims=True))).astype(BF16)
                parts.append((nn(ds, k2), tn(ds, q2), tn(probs.astype(BF16), dc2)))
            dq = (jnp.where(low_side, parts[0][0], parts[1][0]) * (1.0 / 8.0)).astype(BF16)
            dk = jnp.where(low_side, parts[0][1], parts[1][1]).astype(BF16)
            dv = jnp.where(low_side, parts[0][2], parts[1][2]).astype(BF16)
            q[b, :, cols], k[b, :, cols], v[b, :, cols] = dq, dk, dv
            extra = pl.ds(d, 128)
            value[0, pair:pair + 1, extra] += jnp.sum(dq.astype(F32), axis=0, keepdims=True)
            value[0, 3 + pair:4 + pair, extra] += jnp.sum(dv.astype(F32), axis=0, keepdims=True)

        def attend_grad(pair, second):
            cols = pl.ds(pair * 128, 128)
            a = tok[...].reshape(-1, d)
            c = 12 + 2 * pair + second
            if second:
                put(c, pl.ds(0, 128), tn(a, k[:, :, cols].reshape(-1, 128)))
                put(c, pl.ds(128, 128), tn(a, v[:, :, cols].reshape(-1, 128)))
            else:
                put(c, pl.ds(0, 128), tn(do[...].reshape(-1, d), ctx[:, :, cols].reshape(-1, 128)))
                put(c, pl.ds(128, 128), tn(a, q[:, :, cols].reshape(-1, 128)))
        for pair in range(3):
            compute[21 + 4 * pair] = functools.partial(attend_back, pair, 0)
            compute[22 + 4 * pair] = functools.partial(attend_back, pair, 1)
            compute[23 + 4 * pair] = functools.partial(attend_grad, pair, 0)
            compute[24 + 4 * pair] = functools.partial(attend_grad, pair, 1)

        def back_in():
            for name in ("wq", "wk", "wv"):
                got[name].wait()
            pl.semaphore_wait(credit, 1)

            def half(b, carry):
                own[b] = (nt(q[b], wqkv[:, 0:hw]) + nt(k[b], wqkv[:, hw:2 * hw])) + nt(v[b], wqkv[:, 2 * hw:3 * hw])
                swap(b).start()
                return carry
            lax.fori_loop(0, 2, half, 0)
            if scatter:
                fly.start(0)
        compute[33] = back_in

        def finish_in():
            def half(b, carry):
                swap(b).wait()

                def tile(rows):
                    dz[b, rows, :] += own[b, rows, :] + land[b, rows, :]
                tiles(SPAN, tile)
                return carry
            lax.fori_loop(0, 2, half, 0)
            start(dz, grad_in_h, osem.at[0])
        compute[34] = finish_in
        if scatter:
            fly = Butterfly(p, value, vland, vsend, vrecv)
        last = max(i for i, item in enumerate(program) if item[0] == "c")
        run(program[cut:last + 1], compute)
        tail = program[last + 1:]
        steps = 0
        for i, item in enumerate(tail):
            if scatter:
                ring.stage(*item)
                if i % 6 == 5 and steps < 4:
                    fly.take(steps)
                    if steps < 3:
                        fly.start(steps + 1)
                    steps += 1
        if scatter:
            for step in range(steps, 4):
                fly.take(step)
                if step < 3:
                    fly.start(step + 1)
            fly.drain()

    pl.run_scoped(attend_part, *[pltpu.VMEM(q_h.shape, BF16)] * 5, pltpu.VMEM(dm_h.shape, BF16),
                  pltpu.VMEM((2, SPAN, SPAN), F32), pltpu.VMEM((d, 3 * hw), BF16), pltpu.VMEM((hw, d), BF16))

    if scatter:
        for c in range(6):
            g2w[:, c * CW:(c + 1) * CW] = ring.own(c)[...]
            g1w[:, c * CW:(c + 1) * CW] = ring.own(6 + c)[...]
        for pair in range(3):
            at = slice(pair * 128, pair * 128 + 128)
            first, second = ring.own(12 + 2 * pair), ring.own(13 + 2 * pair)
            go[:, at] = first[:, 0:128]
            gq[:, at] = first[:, 128:256]
            gk[:, at] = second[:, 0:128]
            gv[:, at] = second[:, 128:256]
        o_qb, o_vb, o_ob, o_g1, o_s1, o_b1, o_b2, o_g2, o_s2 = small_outs
        for out, row in ((o_ob, 0), (o_g1, 1), (o_s1, 2), (o_b2, 3), (o_g2, 4), (o_s2, 5)):
            out[...] = value[4, row, 0:d]
        for half in range(2):
            o_b1[half * d:(half + 1) * d] = value[4, 6 + half, 0:d]
        for pair in range(3):
            o_qb[pair * 128:(pair + 1) * 128] = value[4, pair, d:d + 128]
            o_vb[pair * 128:(pair + 1) * 128] = value[4, 3 + pair, d:d + 128]
        for c in range(len(kinds)):
            ring.drain(c)
    else:
        wide = start(grad, wide_h, osem.at[1])
        small_out[...] = value[0]
        wide.wait()
    pltpu.make_async_copy(dz, grad_in_h, osem.at[0]).wait()


KINDS = ['yx', 'xy', 'xy', 'xy', 'yx', 'zxy', 'yx', 'xy', 'yx', 'zxy', 'yx', 'zyx', 'xy', 'xy', 'yx', 'yx', 'zyx', 'yx']

PROGRAM = [
    ("c", 0, 0), (0, 0), ("c", 0, 1), (1, 0), ("c", 0, 2), (2, 0), ("c", 0, 3), (3, 0), ("c", 0, 4), (4, 0),
    ("c", 0, 5), (5, 0), ("c", 0, 6), ("c", 0, 7), (6, 0), ("c", 0, 8), ("c", 0, 9), (7, 0), (0, 1), ("c", 0, 10),
    (1, 1), ("c", 0, 11), (8, 0), ("c", 0, 12), ("c", 0, 13), (9, 0), ("c", 0, 14), ("c", 0, 15), (10, 0),
    ("c", 0, 16), (4, 1), (5, 1), (2, 1), ("c", 0, 17), (11, 0), ("c", 0, 18), ("c", 0, 19), (6, 1), (3, 1),
    ("c", 0, 20), ("c", 0, 21), (5, 2), (1, 2), (9, 1), ("c", 0, 22), ("c", 0, 23), (12, 0), ("c", 0, 24), (13, 0),
    (7, 1), ("c", 0, 25), (5, 3), (8, 1), ("c", 0, 26), (0, 2), ("c", 0, 27), (14, 0), (9, 2), ("c", 0, 28), (15, 0),
    (11, 1), (4, 2), ("c", 0, 29), ("c", 0, 30), (1, 3), (10, 1), (6, 2), (9, 3), ("c", 0, 31), (16, 0), (0, 3),
    (2, 2), ("c", 0, 32), (17, 0), ("c", 0, 33), (4, 3), (11, 2), ("c", 0, 34), (3, 2), (1, 4), (6, 3), (12, 1),
    (0, 4), (7, 2), (4, 4), (11, 3), (1, 5), (6, 4), (0, 5), (4, 5), (13, 1), (6, 5), (5, 4), (14, 1), (16, 1),
    (8, 2), (2, 3), (3, 3), (10, 2), (15, 1), (9, 4), (7, 3), (16, 2), (2, 4), (8, 3), (14, 2), (3, 4), (16, 3),
    (10, 3), (17, 1), (7, 4), (2, 5), (15, 2), (3, 5), (8, 4), (14, 3), (7, 5), (12, 2), (10, 4), (8, 5), (17, 2),
    (15, 3), (11, 4), (14, 4), (10, 5), (12, 3), (11, 5), (14, 5), (15, 4), (13, 2), (5, 5), (17, 3), (9, 5), (15, 5),
    (12, 4), (16, 4), (13, 3), (12, 5), (17, 4), (16, 5), (17, 5), (13, 4), (13, 5),
]


def backward(scatter, tokens, bucket, lens, saved, student):
    wq, bq, wk, wv, bv, wo, bo, g1, s1, w1, b1, w2, b2, g2, s2 = student
    q, k, v, ctx, n1, r1, h1, f, dz, dm, sums = saved
    halves, span, d = dz.shape
    hw, fw = wq.shape[1], w1.shape[1]
    count = (2 * fw + 4 * hw) // CW
    kinds = KINDS
    program = PROGRAM
    hbm, vmem, smem = (pl.BlockSpec(memory_space=m) for m in (pl.ANY, pltpu.VMEM, pltpu.SMEM))
    def S(*shape, dtype=F32):
        return jax.ShapeDtypeStruct(shape, dtype)
    def V(*shape, dtype=F32):
        return pltpu.VMEM(shape, dtype)
    dma = pltpu.SemaphoreType.DMA
    if scatter:
        outs = (S(halves, span, d), S(ROWS, hw), S(ROWS, hw), S(ROWS, hw), S(ROWS, hw), S(ROWS, fw), S(ROWS, fw),
                S(hw), S(hw), S(d), S(d), S(d), S(fw), S(d), S(d), S(d))
        out_specs = (hbm,) + (vmem,) * 15
        rings = ring_scratch(kinds, count)
    else:
        outs = (S(halves, span, d), S(count, NZ, NY, NX, ROWS, CW), S(8, 896))
        out_specs = (hbm, hbm, vmem)
        rings = [V(count, NZ, NY, NX, ROWS, CW)]
    return pl.pallas_call(
        functools.partial(backward_kernel, scatter, kinds, program),
        out_shape=outs,
        in_specs=[smem, smem, vmem] + [hbm] * 19,
        out_specs=out_specs,
        scratch_shapes=[V(halves, span, d, dtype=BF16), V(halves, span, d), V(halves, span, d), V(halves, span, 128),
                        V(2, span, d), V(2, span, d), V(8, fw), V(8, d), V(5, 8, 896), V(4, 8, 896),
                        dma((11,)), dma((8,)), dma((2,)), dma((2,)), dma((2,)), pltpu.SemaphoreType.REGULAR, dma((4,)), dma((4,))] + rings,
        compiler_params=pltpu.CompilerParams(collective_id=2, has_side_effects=True, vmem_limit_bytes=VMEM_BYTES),
    )(bucket, lens, sums, tokens.reshape(halves, span, d), q, k, v, ctx, n1, r1, h1, f, dz, dm, wq, wk, wv, wo, w1, w2, b1, g1)


def shards(*args):
    tokens, row_bucket, row_lengths = args[:3]
    teacher, student = args[3:18], args[18:33]
    d = tokens.shape[1]
    count = lax.axis_size("dp")
    scatter = count == NZ * NY * NX
    out, *saved = forward(tokens, row_bucket, row_lengths, teacher, student)
    got = backward(scatter, tokens, row_bucket, row_lengths, saved, student)
    if scatter:
        grad_in, gq, gk, gv, go, g1, g2, qb, vb, ob, g1g, s1g, b1g, b2g, g2g, s2g = got
    else:
        grad_in, wide, small = got
        fw, hw = student[9].shape[1], student[0].shape[1]
        rows = wide.reshape(wide.shape[0], d, CW)
        side = lambda group: jnp.concatenate([rows[c] for c in group], axis=1)
        steps = fw // CW
        last = [2 * steps + i for i in range(2 * hw // 128)]
        first, second = ([rows[c] for c in last[i::2]] for i in (0, 1))
        mats = [
            jnp.concatenate([m[:, 128:] for m in first], axis=1),
            jnp.concatenate([m[:, :128] for m in second], axis=1),
            jnp.concatenate([m[:, 128:] for m in second], axis=1),
            jnp.concatenate([m[:, :128] for m in first], axis=1),
            side(range(steps, 2 * steps)),
            side(range(steps)),
        ]
        gq, gk, gv, go, g1, g2 = (lax.psum_scatter(m, "dp", scatter_dimension=0, tiled=True) for m in mats)
        small = lax.psum(small, "dp")
        qb, vb = small[0:3, d:].reshape(-1), small[3:6, d:].reshape(-1)
        ob, g1g, s1g, b2g, g2g, s2g = (small[i, :d] for i in range(6))
        b1g = small[6:8, :d].reshape(-1)
    toks = tokens.shape[0]
    return (
        out.reshape(toks, d), grad_in.reshape(toks, d), gq, qb, gk, gv, vb, go.T, ob, g1g, s1g, g1, b1g, g2.T, b2g, g2g, s2g
    )


def solution(mesh):
    placed = (
        P("dp", None),
        P("dp"),
        P("dp", None),
        P(None, "head"),
        P("head"),
        P(None, "head"),
        P(None, "head"),
        P("head"),
        P("head", None),
        P(),
        P(),
        P(),
        P(None, "head"),
        P("head"),
        P("head", None),
        P(),
        P(),
        P(),
        P(None, "head"),
        P("head"),
        P(None, "head"),
        P(None, "head"),
        P("head"),
        P("head", None),
        P(),
        P(),
        P(),
        P(None, "head"),
        P("head"),
        P("head", None),
        P(),
        P(),
        P(),
    )
    return jax.shard_map(
        shards,
        mesh=mesh,
        in_specs=placed,
        out_specs=(
            P("dp", None),
            P("dp", None),
            P("dp", "head"),
            P("head"),
            P("dp", "head"),
            P("dp", "head"),
            P("head"),
            P("head", "dp"),
            P(),
            P(),
            P(),
            P("dp", "head"),
            P("head"),
            P("head", "dp"),
            P(),
            P(),
            P(),
        ),
        check_vma=False,
    )
```

```python
import functools

import jax
import jax.numpy as jnp
from jax import lax
from jax.experimental import pallas as pl
from jax.experimental.pallas import tpu as pltpu
from jax.sharding import PartitionSpec as P

MESH = pl.DeviceIdType.MESH
HEAD_DIM = 64
SPAN = 512
NORM_EPS = 1e-12
SQRT_HALF = 0.7071067811865476
F32, BF16 = jnp.float32, jnp.bfloat16
VMEM_BYTES = 62 * 2**20


def nn(a, b):
    return jnp.dot(a, b, preferred_element_type=F32)


def nt(a, b):
    return lax.dot_general(a, b, (((1,), (1,)), ((), ())), preferred_element_type=F32)


def tn(a, b):
    return lax.dot_general(a, b, (((0,), (0,)), ((), ())), preferred_element_type=F32)


def row_layout(bucket, lens, slots):
    shift = jnp.where(bucket == 0, SPAN // 4, jnp.where(bucket == 1, SPAN // 2, SPAN))
    row = jnp.where(bucket == 0, slots // (SPAN // 4), jnp.where(bucket == 1, slots // (SPAN // 2), slots // SPAN))
    length = jnp.zeros_like(slots)
    for j in range(8):
        length = jnp.where(row == j, lens[0, j], length)
    return row, (slots - row * shift) < length


def fill_masks(bucket, lens, bias, valid):
    code = bucket[0]
    for b in range(bias.shape[0]):
        q = b * SPAN + lax.broadcasted_iota(jnp.int32, (SPAN, 1), 0)
        k = b * SPAN + lax.broadcasted_iota(jnp.int32, (1, SPAN), 1)
        q_row, q_ok = row_layout(code, lens, q)
        k_row, k_ok = row_layout(code, lens, k)
        k_row = jnp.where(k_ok, k_row, -1)
        bias[b] = jnp.where(q_row == k_row, 0.0, -1000000000.0)
        if valid is not None:
            valid[b] = jnp.broadcast_to(jnp.where(q_ok, 1.0, 0.0), valid.shape[1:])


def lane_half():
    return lax.broadcasted_iota(jnp.int32, (1, 128), 1) < HEAD_DIM


def attention(q, k, v, bias, ctx):
    low = lane_half()
    for pair in range(q.shape[1] // 128):
        cols = pl.ds(pair * 128, 128)
        q2, k2, v2 = q[:, cols], k[:, cols], v[:, cols]
        parts = []
        for side in (low, ~low):
            s = nt(jnp.where(side, q2, jnp.zeros_like(q2)), k2) + bias[...]
            e = jnp.exp(s - jnp.max(s, axis=1, keepdims=True))
            mass = jnp.sum(e, axis=1, keepdims=True)
            parts.append(nn(e.astype(BF16), v2) * (1.0 / mass))
        ctx[:, cols] = jnp.where(low, parts[0], parts[1]).astype(BF16)


def standardize(z):
    centred = z - jnp.mean(z, axis=-1, keepdims=True)
    inv = lax.rsqrt(jnp.mean(centred * centred, axis=-1, keepdims=True) + NORM_EPS)
    return centred * inv, inv


TILE = 128


def tiles(rows, body):
    for i in range(rows // TILE):
        body(pl.ds(i * TILE, TILE))


def forward_kernel(*refs):
    (bucket, lens, tokens_h, *rest) = refs
    th, rest = rest[:6], rest[6:]
    sh, rest = rest[:6], rest[6:]
    tb, rest = rest[:9], rest[9:]
    sb, rest = rest[:9], rest[9:]
    (out_h, q_h, k_h, v_h, ctx_h, n1_h, r1_h, h1_h, f_h, dz_h, dm_h, sums), rest = rest[:12], rest[12:]
    vecs, vsem, *rest = rest
    vectors = []
    for i, src in enumerate((*tb, *sb)):
        vectors.append(pltpu.make_async_copy(src, vecs.at[i, 0, pl.ds(0, src.shape[0])], vsem.at[i]))
    for item in vectors:
        item.start()
    tb, sb = ([vecs.at[base + i, :, pl.ds(0, src.shape[0])] for i, src in enumerate(group)]
              for base, group in ((0, tb), (9, sb)))
    (tok, t_qkv, t_o, t_1, t_2, s_qkv, s_o, s_1, s_2, q, k, v, ctx, n1, r1, h1, f, tq, tk, tv, tctx, th1b, tf,
     target, own, land, bias, valid, dm, wsem, osem, ssem, rsem) = rest
    dp, head = lax.axis_index("dp"), lax.axis_index("head")
    hw = q.shape[2]

    loads = [pltpu.make_async_copy(tokens_h, tok, wsem.at[0])]
    for base, src, qkv, o, one, two in ((1, th, t_qkv, t_o, t_1, t_2), (7, sh, s_qkv, s_o, s_1, s_2)):
        for j in range(3):
            loads.append(pltpu.make_async_copy(src[j], qkv.at[:, pl.ds(j * hw, hw)], wsem.at[base + j]))
        for j, dst in enumerate((o, one, two)):
            loads.append(pltpu.make_async_copy(src[3 + j], dst, wsem.at[base + 3 + j]))
    for item in loads:
        item.start()

    barrier = pltpu.get_barrier_semaphore()
    pl.semaphore_signal(barrier, inc=1, device_id=(dp, 1 - head), device_id_type=MESH)
    fill_masks(bucket, lens, bias, valid)
    sums[...] = jnp.zeros_like(sums)
    pl.semaphore_wait(barrier, 1)

    def swap(slot):
        return pltpu.make_async_remote_copy(
            src_ref=own.at[slot], dst_ref=land.at[slot], send_sem=ssem.at[slot], recv_sem=rsem.at[slot],
            device_id=(dp, 1 - head), device_id_type=MESH)

    def half(b):
        return pl.ds(pl.multiple_of(b * SPAN, SPAN), SPAN)

    def project(a, w, vectors, q, k, v):
        bq, bv = vectors
        q[...] = ((nn(a, w[:, 0:hw]) + bq[...]).astype(BF16).astype(F32) * (1.0 / 8.0)).astype(BF16)
        k[...] = nn(a, w[:, hw:2 * hw]).astype(BF16)
        v[...] = (nn(a, w[:, 2 * hw:3 * hw]) + bv[...]).astype(BF16)

    def feed(h1b, w1, b1, w2, f, slot):
        for j in range(w1.shape[1] // 256):
            cols = pl.ds(j * 256, 256)
            u = nn(h1b[...], w1[:, cols]) + b1[:, cols]
            f[:, cols] = (0.5 * u * (1.0 + lax.erf(u * SQRT_HALF))).astype(BF16)
        own[slot] = nn(f[...], w2[...])

    def whole(slot, rows, bias_vec, residual):
        return residual + ((own[slot, rows, :] + land[slot, rows, :]) + bias_vec[...])

    def teach_attend(b, carry):
        project(tok[half(b), :], t_qkv, tb[:2], tq, tk, tv)
        attention(tq, tk, tv, bias.at[b], tctx)
        own[b] = nn(tctx[...], t_o[...])
        swap(b).start()
        return carry

    def teach_feed(b, carry):
        swap(b).wait()

        def norm(rows):
            at = pl.ds(pl.multiple_of(b * SPAN + rows.start, TILE), TILE)
            n, _ = standardize(whole(b, rows, tb[2], tok[at, :].astype(F32)))
            h = n * tb[3][...] + tb[4][...]
            target[b, rows, :] = h
            th1b[rows, :] = h.astype(BF16)
        tiles(SPAN, norm)
        feed(th1b, t_1, tb[5], t_2, tf, 2 + b)
        swap(2 + b).start()
        return carry

    def study_attend(b, carry):
        swap(2 + b).wait()

        def norm(rows):
            n, _ = standardize(whole(2 + b, rows, tb[6], target[b, rows, :]))
            target[b, rows, :] = n * tb[7][...] + tb[8][...]
        tiles(SPAN, norm)
        project(tok[half(b), :], s_qkv, sb[:2], q.at[b], k.at[b], v.at[b])
        attention(q.at[b], k.at[b], v.at[b], bias.at[b], ctx.at[b])
        own[b] = nn(ctx[b], s_o[...])
        swap(b).start()
        return carry

    def study_feed(b, carry):
        @pl.when(b == 0)
        def _():
            swap(0).wait()

        def norm(rows):
            at = pl.ds(pl.multiple_of(b * SPAN + rows.start, TILE), TILE)
            n, r = standardize(whole(b, rows, sb[2], tok[at, :].astype(F32)))
            n1[b, rows, :] = n
            r1[b, rows, :] = jnp.broadcast_to(r, (TILE, 128))
            h1[b, rows, :] = (n * sb[3][...] + sb[4][...]).astype(BF16)
        tiles(SPAN, norm)
        feed(h1.at[b], s_1, sb[5], s_2, f.at[b], 2 + b)

        @pl.when(b == 0)
        def _():
            swap(1).wait()
        swap(2 + b).start()
        return carry

    def study_end(b, carry):
        swap(2 + b).wait()

        def norm(rows):
            residual = n1[b, rows, :] * sb[3][...] + sb[4][...]
            n2, r2 = standardize(whole(2 + b, rows, sb[6], residual))
            result = n2 * sb[7][...] + sb[8][...]
            dy = (result - target[b, rows, :]) * valid[b, rows, 0:1]
            target[b, rows, :] = result
            scaled = dy * sb[7][...]
            dz = r2 * (scaled - jnp.mean(scaled, axis=-1, keepdims=True) - n2 * jnp.mean(scaled * n2, axis=-1, keepdims=True))
            own[b, rows, :] = dz
            low = dz.astype(BF16)
            dm[b, rows, :] = low
            sums[0:1, :] += jnp.sum(low.astype(F32), axis=0, keepdims=True)
            sums[1:2, :] += jnp.sum(dy * n2, axis=0, keepdims=True)
            sums[2:3, :] += jnp.sum(dy, axis=0, keepdims=True)
        tiles(SPAN, norm)
        return carry

    for item in vectors:
        item.wait()
    for item in loads[0:4]:
        item.wait()
    loads[4].wait()
    lax.fori_loop(0, 2, teach_attend, 0)
    for item in loads[5:7]:
        item.wait()
    lax.fori_loop(0, 2, teach_feed, 0)
    for item in loads[7:11]:
        item.wait()
    lax.fori_loop(0, 2, study_attend, 0)
    stores = []

    def store(src, dst):
        copy = pltpu.make_async_copy(src, dst, osem.at[len(stores)])
        copy.start()
        stores.append(copy)
    for src, dst in ((q, q_h), (k, k_h), (v, v_h), (ctx, ctx_h)):
        store(src, dst)
    for item in loads[11:13]:
        item.wait()
    lax.fori_loop(0, 2, study_feed, 0)
    for src, dst in ((n1, n1_h), (r1, r1_h), (h1, h1_h), (f, f_h)):
        store(src, dst)
    lax.fori_loop(0, 2, study_end, 0)
    store(dm, dm_h)
    store(own.at[pl.ds(0, 2)], dz_h)
    store(target, out_h)
    for item in stores:
        item.wait()


def forward(tokens, bucket, lens, teacher, student):
    def cut(layer):
        wq, bq, wk, wv, bv, wo, bo, g1, s1, w1, b1, w2, b2, g2, s2 = layer
        return [wq, wk, wv, wo, w1, w2], [bq, bv, bo, g1, s1, b1, b2, g2, s2]
    tw, tv = cut(teacher)
    sw, sv = cut(student)
    toks, d = tokens.shape
    hw, fw = tw[0].shape[1], tw[4].shape[1]
    halves = toks // SPAN
    hbm, vmem, smem = (pl.BlockSpec(memory_space=m) for m in (pl.ANY, pltpu.VMEM, pltpu.SMEM))
    def S(*shape, dtype=F32):
        return jax.ShapeDtypeStruct(shape, dtype)
    def V(*shape, dtype=F32):
        return pltpu.VMEM(shape, dtype)
    b = BF16
    outs = (S(halves, SPAN, d), S(halves, SPAN, hw, dtype=b), S(halves, SPAN, hw, dtype=b), S(halves, SPAN, hw, dtype=b),
            S(halves, SPAN, hw, dtype=b), S(halves, SPAN, d), S(halves, SPAN, 128), S(halves, SPAN, d, dtype=b),
            S(halves, SPAN, fw, dtype=b), S(halves, SPAN, d), S(halves, SPAN, d, dtype=b), S(8, d))
    weights = [V(d, 3 * hw, dtype=b), V(hw, d, dtype=b), V(d, fw, dtype=b), V(fw, d, dtype=b)]
    return pl.pallas_call(
        forward_kernel,
        out_shape=outs,
        in_specs=[smem, smem, hbm] + [hbm] * 30,
        out_specs=(hbm,) * 11 + (vmem,),
        scratch_shapes=[V(18, 1, fw), pltpu.SemaphoreType.DMA((18,)), V(toks, d, dtype=b)] + weights + weights
        + [V(halves, SPAN, hw, dtype=b)] * 4 + [V(halves, SPAN, d), V(halves, SPAN, 128), V(halves, SPAN, d, dtype=b), V(halves, SPAN, fw, dtype=b)]
        + [V(SPAN, hw, dtype=b)] * 4 + [V(SPAN, d, dtype=b), V(SPAN, fw, dtype=b)]
        + [V(halves, SPAN, d), V(4, SPAN, d), V(4, SPAN, d), V(halves, SPAN, SPAN), V(halves, SPAN, 128), V(halves, SPAN, d, dtype=b)]
        + [pltpu.SemaphoreType.DMA((13,)), pltpu.SemaphoreType.DMA((11,)), pltpu.SemaphoreType.DMA((4,)), pltpu.SemaphoreType.DMA((4,))],
        compiler_params=pltpu.CompilerParams(collective_id=1, has_side_effects=True, vmem_limit_bytes=VMEM_BYTES),
    )(bucket, lens, tokens, *tw, *sw, *tv, *sv)


CW = 256
NZ, NY, NX = 4, 2, 2
ROWS = 48


class Place:
    def __init__(self):
        self.dp = lax.axis_index("dp")
        self.head = lax.axis_index("head")
        self.z = self.dp // 4
        self.y = lax.rem(self.dp // 2, 2)
        self.x = lax.rem(self.dp, 2)

    def at(self, dz=0, y=None, x=None):
        y = self.y if y is None else y
        x = self.x if x is None else x
        return ((self.z + dz) * 4 + y * 2 + x, self.head)


class Ring:
    def __init__(self, place, kinds, grad, pair_a, pair_b, path, zpath, zpair_a, zpair_b, send, recv, slot=None):
        self.p = place
        self.kinds = kinds
        self.grad, self.pair_a, self.pair_b, self.path = grad, pair_a, pair_b, path
        self.zpath, self.zpair_a, self.zpair_b = zpath, zpair_a, zpair_b
        self.send, self.recv = send, recv
        self.slot = slot or list(range(len(kinds)))
        flat = [c for c, k in enumerate(kinds) if not k.startswith("z")]
        deep = [c for c, k in enumerate(kinds) if k.startswith("z")]
        self.place_of = {c: i for i, c in enumerate(flat)} | {c: i for i, c in enumerate(deep)}

    def _pair(self, c, step):
        kind, p, i = self.kinds[c], self.p, self.place_of[c]
        g = self.grad.at[self.slot[c]]
        if kind.startswith("z"):
            axis = kind[1 + step]
            land = (self.zpair_a if step == 0 else self.zpair_b).at[i]
            view = g.at[p.z]
            if step == 0:
                pick = (lambda j: view.at[:, j]) if axis == "x" else (lambda j: view.at[j])
            else:
                pick = (lambda j: view.at[p.y, j]) if axis == "x" else (lambda j: view.at[j, p.x])
        else:
            axis = kind[step]
            land = (self.pair_a if step == 0 else self.pair_b).at[i]
            if step == 0:
                pick = (lambda j: g.at[:, :, j]) if axis == "x" else (lambda j: g.at[:, j])
            else:
                pick = (lambda j: g.at[:, p.y, j]) if axis == "x" else (lambda j: g.at[:, j, p.x])
        mine = p.x if axis == "x" else p.y
        to = p.at(x=1 - p.x) if axis == "x" else p.at(y=1 - p.y)
        copy = pltpu.make_async_remote_copy(
            src_ref=pick(1 - mine), dst_ref=land, send_sem=self.send.at[c, step], recv_sem=self.recv.at[c, step],
            device_id=to, device_id_type=MESH)
        return copy, pick(mine), land

    def pair_send(self, c, step):
        self._pair(c, step)[0].start()

    def pair_take(self, c, step):
        copy, mine, land = self._pair(c, step)
        copy.wait_recv()
        mine[...] += land[...]

    def _path_refs(self, c):
        kind, p, i = self.kinds[c], self.p, self.place_of[c]
        g = self.grad.at[self.slot[c]]
        if kind.startswith("z"):
            return (lambda lo, n: g.at[pl.ds(lo, n)]), self.zpath.at[i]
        return (lambda lo, n: g.at[pl.ds(lo, n), p.y, p.x]), self.path.at[i]

    def _hop(self, c, z, up):
        blocks, land = self._path_refs(c)
        if up:
            src, dst, k, dz = blocks(z + 1, 3 - z), land.at[pl.ds(0, 3 - z)], 2, 1
        else:
            src, dst, k, dz = blocks(0, z), land.at[pl.ds(5 - z, z)], 3, -1
        return pltpu.make_async_remote_copy(
            src_ref=src, dst_ref=dst, send_sem=self.send.at[c, k], recv_sem=self.recv.at[c, k],
            device_id=self.p.at(dz=dz), device_id_type=MESH)

    def path_start(self, c):
        @pl.when(self.p.z == 0)
        def _():
            self._hop(c, 0, True).start()

        @pl.when(self.p.z == 3)
        def _():
            self._hop(c, 3, False).start()

    def path_mid(self, c, first):
        blocks, land = self._path_refs(c)
        for z in (1, 2):
            up = (z == 1) == first

            @pl.when(self.p.z == z)
            def _(z=z, up=up):
                if up:
                    self._hop(c, z - 1, True).wait_recv()
                    own = blocks(z + 1, 3 - z)
                    own[...] += land[pl.ds(1, 3 - z)]
                    self._hop(c, z, True).start()
                else:
                    self._hop(c, z + 1, False).wait_recv()
                    own = blocks(0, z)
                    own[...] += land[pl.ds(4 - z, z)]
                    self._hop(c, z, False).start()

    def path_end(self, c):
        blocks, land = self._path_refs(c)
        for z in range(NZ):
            @pl.when(self.p.z == z)
            def _(z=z):
                if z == 0:
                    self._hop(c, 1, False).wait_recv()
                if z == 3:
                    self._hop(c, 2, True).wait_recv()
                own = blocks(z, 1)
                total = own[...]
                if z > 0:
                    total = total + land[pl.ds(0, 1)]
                if z < 3:
                    total = total + land[pl.ds(4, 1)]
                own[...] = total

    def drain(self, c):
        for step in (0, 1):
            self._pair(c, step)[0].wait_send()
        for z in range(NZ):
            @pl.when(self.p.z == z)
            def _(z=z):
                if z < 3:
                    self._hop(c, z, True).wait_send()
                if z > 0:
                    self._hop(c, z, False).wait_send()

    def stage(self, c, s):
        deep = self.kinds[c].startswith("z")
        if deep:
            if s == 0: self.path_start(c)
            elif s == 1: self.path_mid(c, True)
            elif s == 2: self.path_mid(c, False)
            elif s == 3: self.path_end(c); self.pair_send(c, 0)
            elif s == 4: self.pair_take(c, 0); self.pair_send(c, 1)
            elif s == 5: self.pair_take(c, 1)
        else:
            if s == 0: self.pair_send(c, 0)
            elif s == 1: self.pair_take(c, 0); self.pair_send(c, 1)
            elif s == 2: self.pair_take(c, 1); self.path_start(c)
            elif s == 3: self.path_mid(c, True)
            elif s == 4: self.path_mid(c, False)
            elif s == 5: self.path_end(c)

    def own(self, c):
        p = self.p
        return self.grad.at[self.slot[c], p.z, p.y, p.x]


def ring_scratch(kinds, slots):
    flat = sum(not k.startswith("z") for k in kinds)
    deep = len(kinds) - flat
    f = jnp.float32
    return [
        pltpu.VMEM((slots, NZ, NY, NX, ROWS, CW), f),
        pltpu.VMEM((flat, NZ, 2, ROWS, CW), f),
        pltpu.VMEM((flat, NZ, ROWS, CW), f),
        pltpu.VMEM((flat, 5, ROWS, CW), f),
        pltpu.VMEM((max(deep, 1), 5, NY, NX, ROWS, CW), f),
        pltpu.VMEM((max(deep, 1), 2, ROWS, CW), f),
        pltpu.VMEM((max(deep, 1), ROWS, CW), f),
        pltpu.SemaphoreType.DMA((len(kinds), 4)),
        pltpu.SemaphoreType.DMA((len(kinds), 4)),
    ]


INV_SQRT_2PI = 0.3989422804014327


class Butterfly:
    def __init__(self, place, value, land, send, recv):
        self.p, self.value, self.land, self.send, self.recv = place, value, land, send, recv

    def partner(self, step):
        p = self.p
        if step == 0:
            return p.at(x=1 - p.x)
        if step == 1:
            return p.at(y=1 - p.y)
        if step == 2:
            return p.at(dz=1 - 2 * lax.rem(p.z, 2))
        return p.at(dz=2 - 4 * (p.z // 2))

    def _copy(self, step):
        return pltpu.make_async_remote_copy(
            src_ref=self.value.at[step], dst_ref=self.land.at[step], send_sem=self.send.at[step],
            recv_sem=self.recv.at[step], device_id=self.partner(step), device_id_type=MESH)

    def start(self, step):
        self._copy(step).start()

    def take(self, step):
        self._copy(step).wait_recv()
        self.value[step + 1] = self.value[step] + self.land[step]

    def drain(self):
        for step in range(4):
            self._copy(step).wait_send()


def greet_all(p, scatter):
    barrier = pltpu.get_barrier_semaphore()

    def hello(to):
        pl.semaphore_signal(barrier, inc=1, device_id=to, device_id_type=MESH)
    hello((p.dp, 1 - p.head))
    if not scatter:
        return lambda: pl.semaphore_wait(barrier, 1)
    hello(p.at(x=1 - p.x))
    hello(p.at(y=1 - p.y))
    for dz in (1, -1):
        @pl.when((p.z + dz >= 0) & (p.z + dz < NZ))
        def _(dz=dz):
            hello(p.at(dz=dz))
    hello(p.at(dz=2 - 4 * (p.z // 2)))

    def wait():
        inner = (p.z == 1) | (p.z == 2)

        @pl.when(inner)
        def _():
            pl.semaphore_wait(barrier, 6)

        @pl.when(~inner)
        def _():
            pl.semaphore_wait(barrier, 5)
    return wait


def gelu_slope(u):
    return 0.5 * (1.0 + lax.erf(u * SQRT_HALF)) + u * (INV_SQRT_2PI * jnp.exp(-0.5 * u * u))


def backward_kernel(scatter, kinds, program, *refs):
    (bucket, lens, sums, tokens_h, q_h, k_h, v_h, ctx_h, n1_h, r1_h, h1_h, f_h, dz_h, dm_h,
     wq_h, wk_h, wv_h, wo_h, w1_h, w2_h, b1_h, g1_h), rest = refs[:22], refs[22:]
    if scatter:
        (grad_in_h, wide, small_out), rest = rest[:3], rest[3:]
    else:
        (grad_in_h, wide_h, small_out), rest = rest[:3], rest[3:]
    (tok, dz, n1, r1, own, land, b1, g1, value, vland, lsem, asem, osem, ssem, rsem, credit, vsend, vrecv, *ring_refs) = rest
    p = Place()
    dp, head = p.dp, p.head
    grad = ring_refs[0]
    ready = greet_all(p, scatter)
    hw = q_h.shape[2]
    d = dz.shape[2]
    fw = w1_h.shape[1]

    def start(src, dst, sem):
        copy = pltpu.make_async_copy(src, dst, sem)
        copy.start()
        return copy

    def swap(slot):
        return pltpu.make_async_remote_copy(
            src_ref=own.at[slot], dst_ref=land.at[slot], send_sem=ssem.at[slot], recv_sem=rsem.at[slot],
            device_id=(dp, 1 - head), device_id_type=MESH)

    def put(c, cols, block):
        g = grad.at[ring.slot[c]] if scatter else grad.at[c]
        for i in range(NZ * NY * NX):
            z, y, x = i // 4, i // 2 % 2, i % 2
            g[z, y, x, :, cols] = block[i * ROWS:(i + 1) * ROWS]

    if scatter:
        ring = Ring(p, kinds, *ring_refs)
    all_cols = pl.ds(0, CW)

    def run(items, compute):
        for item in items:
            if item[0] == "c":
                compute[item[2]]()
            elif scatter:
                ring.stage(*item)

    cut = next(i for i, item in enumerate(program) if item[0] == "c" and item[2] == 19)

    def feed_part(f, dm, h1, w1, w2):
        got = {}
        for i, (name, src, dst) in enumerate((
                ("dm", dm_h, dm), ("f", f_h, f), ("h1", h1_h, h1), ("w2", w2_h, w2), ("w1", w1_h, w1), ("b1", b1_h, b1.at[0]),
                ("dz", dz_h, dz), ("n1", n1_h, n1), ("r1", r1_h, r1), ("g1", g1_h, g1.at[0]), ("tok", tokens_h, tok))):
            got[name] = start(src, dst, lsem.at[i])
        value[...] = jnp.zeros_like(value)

        def need(*names):
            for name in names:
                got.pop(name).wait() if name in got else None
        compute = {}

        def return_grad(c):
            need("dm", "f")
            cols = pl.ds(c * CW, CW)
            left, right = dm[...].reshape(-1, d), f[:, :, cols].reshape(-1, CW)
            put(c, all_cols, tn(left, right))
            if c == 0:
                ready()
        for c in range(6):
            compute[c] = functools.partial(return_grad, c)

        def slope(j):
            need("h1", "w2", "w1", "b1")
            cols = pl.ds(j * CW, CW)

            def half(b, total):
                u = nn(h1[b], w1[:, cols]) + b1[0:1, cols]
                g = nt(dm[b], w2[cols, :])
                du = (g * gelu_slope(u)).astype(BF16)
                f[b, :, cols] = du
                return total + jnp.sum(du.astype(F32), axis=0, keepdims=True)
            total = lax.fori_loop(0, 2, half, jnp.zeros((1, CW), F32))
            value[0, 6 + j // 3:7 + j // 3, pl.ds(j % 3 * CW, CW)] = total

        def hidden_grad(j):
            cols = pl.ds(j * CW, CW)
            put(6 + j, all_cols, tn(h1[...].reshape(-1, d), f[:, :, cols].reshape(-1, CW)))
        for j in range(6):
            compute[6 + 2 * j] = functools.partial(slope, j)
            compute[7 + 2 * j] = functools.partial(hidden_grad, j)

        def back_first():
            def half(b, carry):
                own[b] = nt(f[b], w1[...])
                swap(b).start()
                return carry
            lax.fori_loop(0, 2, half, 0)
            need(*list(got))
        compute[18] = back_first
        run(program[:cut], compute)

    pl.run_scoped(feed_part, pltpu.VMEM(f_h.shape, BF16), pltpu.VMEM(dm_h.shape, BF16), pltpu.VMEM(h1_h.shape, BF16),
                  pltpu.VMEM(w1_h.shape, BF16), pltpu.VMEM(w2_h.shape, BF16))

    def attend_part(q, k, v, ctx, dctx, do, bias, wqkv, wo):
        got = {}
        for i, (name, src, dst) in enumerate((
                ("wo", wo_h, wo), ("q", q_h, q), ("k", k_h, k), ("v", v_h, v), ("ctx", ctx_h, ctx),
                ("wq", wq_h, wqkv.at[:, pl.ds(0, hw)]), ("wk", wk_h, wqkv.at[:, pl.ds(hw, hw)]),
                ("wv", wv_h, wqkv.at[:, pl.ds(2 * hw, hw)]))):
            got[name] = start(src, dst, asem.at[i])
        fill_masks(bucket, lens, bias, None)
        compute = {}

        def norm_back():
            def half(b, carry):
                swap(b).wait()

                def tile(rows):
                    up = dz[b, rows, :] + (own[b, rows, :] + land[b, rows, :])
                    n = n1[b, rows, :]
                    scaled = up * g1[0:1, :]
                    out = r1[b, rows, 0:1] * (scaled - jnp.mean(scaled, axis=-1, keepdims=True)
                                              - n * jnp.mean(scaled * n, axis=-1, keepdims=True))
                    dz[b, rows, :] = out
                    low = out.astype(BF16)
                    do[b, rows, :] = low
                    value[0, 0:1, 0:d] += jnp.sum(low.astype(F32), axis=0, keepdims=True)
                    value[0, 1:2, 0:d] += jnp.sum(up * n, axis=0, keepdims=True)
                    value[0, 2:3, 0:d] += jnp.sum(up, axis=0, keepdims=True)
                tiles(SPAN, tile)
                return carry
            lax.fori_loop(0, 2, half, 0)
            pl.semaphore_signal(credit, inc=1, device_id=(dp, 1 - head), device_id_type=MESH)
            value[0, 3:6, 0:d] = sums[0:3, :]
        compute[19] = norm_back

        def context_grad():
            got["wo"].wait()

            def half(b, carry):
                dctx[b] = nt(do[b], wo[...]).astype(BF16)
                return carry
            lax.fori_loop(0, 2, half, 0)
            for name in ("q", "k", "v", "ctx"):
                got[name].wait()
        compute[20] = context_grad

        def attend_back(pair, b):
            low_side = lane_half()
            cols = pl.ds(pair * 128, 128)
            q2, k2, v2, dc2 = q[b, :, cols], k[b, :, cols], v[b, :, cols], dctx[b, :, cols]
            parts = []
            for side in (low_side, ~low_side):
                zero = jnp.zeros_like(q2)
                s = nt(jnp.where(side, q2, zero), k2) + bias[b]
                e = jnp.exp(s - jnp.max(s, axis=1, keepdims=True))
                probs = e * (1.0 / jnp.sum(e, axis=1, keepdims=True))
                dprob = nt(jnp.where(side, dc2, zero), v2)
                ds = (probs * (dprob - jnp.sum(probs * dprob, axis=1, keepdims=True))).astype(BF16)
                parts.append((nn(ds, k2), tn(ds, q2), tn(probs.astype(BF16), dc2)))
            dq = (jnp.where(low_side, parts[0][0], parts[1][0]) * (1.0 / 8.0)).astype(BF16)
            dk = jnp.where(low_side, parts[0][1], parts[1][1]).astype(BF16)
            dv = jnp.where(low_side, parts[0][2], parts[1][2]).astype(BF16)
            q[b, :, cols], k[b, :, cols], v[b, :, cols] = dq, dk, dv
            extra = pl.ds(d, 128)
            value[0, pair:pair + 1, extra] += jnp.sum(dq.astype(F32), axis=0, keepdims=True)
            value[0, 3 + pair:4 + pair, extra] += jnp.sum(dv.astype(F32), axis=0, keepdims=True)

        def attend_grad(pair, second):
            cols = pl.ds(pair * 128, 128)
            a = tok[...].reshape(-1, d)
            c = 12 + 2 * pair + second
            if second:
                put(c, pl.ds(0, 128), tn(a, k[:, :, cols].reshape(-1, 128)))
                put(c, pl.ds(128, 128), tn(a, v[:, :, cols].reshape(-1, 128)))
            else:
                put(c, pl.ds(0, 128), tn(do[...].reshape(-1, d), ctx[:, :, cols].reshape(-1, 128)))
                put(c, pl.ds(128, 128), tn(a, q[:, :, cols].reshape(-1, 128)))
        for pair in range(3):
            compute[21 + 4 * pair] = functools.partial(attend_back, pair, 0)
            compute[22 + 4 * pair] = functools.partial(attend_back, pair, 1)
            compute[23 + 4 * pair] = functools.partial(attend_grad, pair, 0)
            compute[24 + 4 * pair] = functools.partial(attend_grad, pair, 1)

        def back_in():
            for name in ("wq", "wk", "wv"):
                got[name].wait()
            pl.semaphore_wait(credit, 1)

            def half(b, carry):
                own[b] = (nt(q[b], wqkv[:, 0:hw]) + nt(k[b], wqkv[:, hw:2 * hw])) + nt(v[b], wqkv[:, 2 * hw:3 * hw])
                swap(b).start()
                return carry
            lax.fori_loop(0, 2, half, 0)
            if scatter:
                fly.start(0)
        compute[33] = back_in

        def finish_in():
            def half(b, carry):
                swap(b).wait()

                def tile(rows):
                    dz[b, rows, :] += own[b, rows, :] + land[b, rows, :]
                tiles(SPAN, tile)
                return carry
            lax.fori_loop(0, 2, half, 0)
            start(dz, grad_in_h, osem.at[0])
        compute[34] = finish_in
        if scatter:
            fly = Butterfly(p, value, vland, vsend, vrecv)
        last = max(i for i, item in enumerate(program) if item[0] == "c")
        run(program[cut:last + 1], compute)
        tail = program[last + 1:]
        steps = 0
        for i, item in enumerate(tail):
            if scatter:
                ring.stage(*item)
                if i % 6 == 5 and steps < 4:
                    fly.take(steps)
                    if steps < 3:
                        fly.start(steps + 1)
                    steps += 1
        if scatter:
            for step in range(steps, 4):
                fly.take(step)
                if step < 3:
                    fly.start(step + 1)
            fly.drain()

    pl.run_scoped(attend_part, *[pltpu.VMEM(q_h.shape, BF16)] * 5, pltpu.VMEM(dm_h.shape, BF16),
                  pltpu.VMEM((2, SPAN, SPAN), F32), pltpu.VMEM((d, 3 * hw), BF16), pltpu.VMEM((hw, d), BF16))

    if scatter:
        for c in range(len(kinds)):
            wide[:, c * CW:(c + 1) * CW] = ring.own(c)[...]
        small_out[...] = value[4]
        for c in range(len(kinds)):
            ring.drain(c)
    else:
        wide = start(grad, wide_h, osem.at[1])
        small_out[...] = value[0]
        wide.wait()
    pltpu.make_async_copy(dz, grad_in_h, osem.at[0]).wait()


KINDS = ['yx', 'xy', 'xy', 'zxy', 'yx', 'zyx', 'yx', 'yx', 'yx', 'yx', 'xy', 'xy', 'zyx', 'xy', 'yx', 'xy', 'xy', 'zyx']

PROGRAM = [
    ("c", 0, 0), (0, 0), ("c", 0, 1), (1, 0), ("c", 0, 2), ("c", 0, 3), (3, 0), ("c", 0, 4), ("c", 0, 5), ("c", 0, 6),
    (4, 0), (2, 0), ("c", 0, 7), ("c", 0, 8), ("c", 0, 9), ("c", 0, 10), (0, 1), (1, 1), ("c", 0, 11), (5, 0),
    ("c", 0, 12), ("c", 0, 13), ("c", 0, 14), ("c", 0, 15), ("c", 0, 16), (3, 1), (6, 0), (4, 1), ("c", 0, 17),
    (2, 1), ("c", 0, 18), (1, 2), (10, 0), (0, 2), ("c", 0, 19), (4, 2), (3, 2), (5, 1), (7, 0), (6, 1), ("c", 0, 20),
    ("c", 0, 21), (1, 3), (2, 2), (11, 0), (3, 3), (0, 3), (10, 1), ("c", 0, 22), (4, 3), ("c", 0, 23), (12, 0),
    (5, 2), (6, 2), ("c", 0, 24), (2, 3), (1, 4), (8, 0), (7, 1), (0, 4), ("c", 0, 25), (4, 4), (5, 3), (10, 2),
    (1, 5), (2, 4), (11, 1), (0, 5), ("c", 0, 26), (13, 0), (4, 5), (3, 4), (2, 5), ("c", 0, 27), ("c", 0, 28),
    (12, 1), (7, 2), (8, 1), ("c", 0, 29), (6, 3), (5, 4), (9, 0), ("c", 0, 30), (10, 3), (11, 2), (3, 5), (13, 1),
    (15, 0), (7, 3), ("c", 0, 31), (12, 2), ("c", 0, 32), (17, 0), (8, 2), (6, 4), (11, 3), (5, 5), ("c", 0, 33),
    (10, 4), (14, 0), (9, 1), (12, 3), (7, 4), (6, 5), (11, 4), ("c", 0, 34), (10, 5), (13, 2), (16, 0), (7, 5),
    (15, 1), (11, 5), (9, 2), (17, 1), (14, 1), (8, 3), (12, 4), (13, 3), (16, 1), (15, 2), (9, 3), (17, 2), (14, 2),
    (8, 4), (12, 5), (15, 3), (16, 2), (13, 4), (17, 3), (9, 4), (14, 3), (8, 5), (13, 5), (15, 4), (9, 5), (17, 4),
    (16, 3), (14, 4), (15, 5), (17, 5), (14, 5), (16, 4), (16, 5),
]


def backward(scatter, tokens, bucket, lens, saved, student):
    wq, bq, wk, wv, bv, wo, bo, g1, s1, w1, b1, w2, b2, g2, s2 = student
    q, k, v, ctx, n1, r1, h1, f, dz, dm, sums = saved
    halves, span, d = dz.shape
    hw, fw = wq.shape[1], w1.shape[1]
    count = (2 * fw + 4 * hw) // CW
    kinds = KINDS
    program = PROGRAM
    hbm, vmem, smem = (pl.BlockSpec(memory_space=m) for m in (pl.ANY, pltpu.VMEM, pltpu.SMEM))
    def S(*shape, dtype=F32):
        return jax.ShapeDtypeStruct(shape, dtype)
    def V(*shape, dtype=F32):
        return pltpu.VMEM(shape, dtype)
    dma = pltpu.SemaphoreType.DMA
    if scatter:
        outs = (S(halves, span, d), S(ROWS, count * CW), S(8, 896))
        out_specs = (hbm, vmem, vmem)
        rings = ring_scratch(kinds, count)
    else:
        outs = (S(halves, span, d), S(count, NZ, NY, NX, ROWS, CW), S(8, 896))
        out_specs = (hbm, hbm, vmem)
        rings = [V(count, NZ, NY, NX, ROWS, CW)]
    return pl.pallas_call(
        functools.partial(backward_kernel, scatter, kinds, program),
        out_shape=outs,
        in_specs=[smem, smem, vmem] + [hbm] * 19,
        out_specs=out_specs,
        scratch_shapes=[V(halves, span, d, dtype=BF16), V(halves, span, d), V(halves, span, d), V(halves, span, 128),
                        V(2, span, d), V(2, span, d), V(8, fw), V(8, d), V(5, 8, 896), V(4, 8, 896),
                        dma((11,)), dma((8,)), dma((2,)), dma((2,)), dma((2,)), pltpu.SemaphoreType.REGULAR, dma((4,)), dma((4,))] + rings,
        compiler_params=pltpu.CompilerParams(collective_id=2, has_side_effects=True, vmem_limit_bytes=VMEM_BYTES),
    )(bucket, lens, sums, tokens.reshape(halves, span, d), q, k, v, ctx, n1, r1, h1, f, dz, dm, wq, wk, wv, wo, w1, w2, b1, g1)


def finish_kernel(out_h, gin_h, wide, small, out, gin, gq, gk, gv, go, g1w, g2w, *rest):
    small_outs, (sem,) = rest[:9], rest[9:]
    copies = [pltpu.make_async_copy(src, dst, sem.at[i]) for i, (src, dst) in enumerate(((out_h, out), (gin_h, gin)))]
    for item in copies:
        item.start()
    d = out.shape[2]
    fw, hw = g1w.shape[1], gq.shape[1]
    g2w[...] = wide[:, 0:fw]
    g1w[...] = wide[:, fw:2 * fw]
    first = 2 * fw
    for pair in range(hw // 128):
        at = slice(pair * 128, pair * 128 + 128)
        base = first + pair * 512
        go[:, at] = wide[:, base:base + 128]
        gq[:, at] = wide[:, base + 128:base + 256]
        gk[:, at] = wide[:, base + 256:base + 384]
        gv[:, at] = wide[:, base + 384:base + 512]
    o_qb, o_vb, o_ob, o_g1, o_s1, o_b1, o_b2, o_g2, o_s2 = small_outs
    for dst, row in ((o_ob, 0), (o_g1, 1), (o_s1, 2), (o_b2, 3), (o_g2, 4), (o_s2, 5)):
        dst[...] = small[row, 0:d]
    for half in range(2):
        o_b1[half * d:(half + 1) * d] = small[6 + half, 0:d]
    for pair in range(hw // 128):
        o_qb[pair * 128:(pair + 1) * 128] = small[pair, d:d + 128]
        o_vb[pair * 128:(pair + 1) * 128] = small[3 + pair, d:d + 128]
    for item in copies:
        item.wait()


def finish(out_raw, gin_raw, wide, small, hw, fw):
    d = out_raw.shape[2]
    def S(*shape):
        return jax.ShapeDtypeStruct(shape, F32)
    hbm, vmem = (pl.BlockSpec(memory_space=m) for m in (pl.ANY, pltpu.VMEM))
    return pl.pallas_call(
        finish_kernel,
        out_shape=(S(*out_raw.shape), S(*gin_raw.shape), S(ROWS, hw), S(ROWS, hw), S(ROWS, hw), S(ROWS, hw), S(ROWS, fw), S(ROWS, fw),
                   S(hw), S(hw), S(d), S(d), S(d), S(fw), S(d), S(d), S(d)),
        in_specs=[hbm, hbm, vmem, vmem],
        out_specs=(hbm, hbm) + (vmem,) * 15,
        scratch_shapes=[pltpu.SemaphoreType.DMA((2,))],
        compiler_params=pltpu.CompilerParams(vmem_limit_bytes=32 * 2**20),
    )(out_raw, gin_raw, wide, small)


def shards(*args):
    tokens, row_bucket, row_lengths = args[:3]
    teacher, student = args[3:18], args[18:33]
    d = tokens.shape[1]
    count = lax.axis_size("dp")
    scatter = count == NZ * NY * NX
    out, *saved = forward(tokens, row_bucket, row_lengths, teacher, student)
    got = backward(scatter, tokens, row_bucket, row_lengths, saved, student)
    if scatter:
        fw, hw = student[9].shape[1], student[0].shape[1]
        out, grad_in, gq, gk, gv, go, g1, g2, qb, vb, ob, g1g, s1g, b1g, b2g, g2g, s2g = finish(out, *got, hw, fw)
    else:
        grad_in, wide, small = got
        fw, hw = student[9].shape[1], student[0].shape[1]
        rows = wide.reshape(wide.shape[0], d, CW)
        side = lambda group: jnp.concatenate([rows[c] for c in group], axis=1)
        steps = fw // CW
        last = [2 * steps + i for i in range(2 * hw // 128)]
        first, second = ([rows[c] for c in last[i::2]] for i in (0, 1))
        mats = [
            jnp.concatenate([m[:, 128:] for m in first], axis=1),
            jnp.concatenate([m[:, :128] for m in second], axis=1),
            jnp.concatenate([m[:, 128:] for m in second], axis=1),
            jnp.concatenate([m[:, :128] for m in first], axis=1),
            side(range(steps, 2 * steps)),
            side(range(steps)),
        ]
        gq, gk, gv, go, g1, g2 = (lax.psum_scatter(m, "dp", scatter_dimension=0, tiled=True) for m in mats)
        small = lax.psum(small, "dp")
        qb, vb = small[0:3, d:].reshape(-1), small[3:6, d:].reshape(-1)
        ob, g1g, s1g, b2g, g2g, s2g = (small[i, :d] for i in range(6))
        b1g = small[6:8, :d].reshape(-1)
    toks = tokens.shape[0]
    return (
        out.reshape(toks, d), grad_in.reshape(toks, d), gq, qb, gk, gv, vb, go.T, ob, g1g, s1g, g1, b1g, g2.T, b2g, g2g, s2g
    )


def solution(mesh):
    placed = (
        P("dp", None),
        P("dp"),
        P("dp", None),
        P(None, "head"),
        P("head"),
        P(None, "head"),
        P(None, "head"),
        P("head"),
        P("head", None),
        P(),
        P(),
        P(),
        P(None, "head"),
        P("head"),
        P("head", None),
        P(),
        P(),
        P(),
        P(None, "head"),
        P("head"),
        P(None, "head"),
        P(None, "head"),
        P("head"),
        P("head", None),
        P(),
        P(),
        P(),
        P(None, "head"),
        P("head"),
        P("head", None),
        P(),
        P(),
        P(),
    )
    return jax.shard_map(
        shards,
        mesh=mesh,
        in_specs=placed,
        out_specs=(
            P("dp", None),
            P("dp", None),
            P("dp", "head"),
            P("head"),
            P("dp", "head"),
            P("dp", "head"),
            P("head"),
            P("head", "dp"),
            P(),
            P(),
            P(),
            P("dp", "head"),
            P("head"),
            P("head", "dp"),
            P(),
            P(),
            P(),
        ),
        check_vma=False,
    )
```

```python
import functools

import jax
import jax.numpy as jnp
from jax import lax
from jax.experimental import pallas as pl
from jax.experimental.pallas import tpu as pltpu
from jax.sharding import PartitionSpec as P

MESH = pl.DeviceIdType.MESH
HEAD_DIM = 64
SPAN = 512
NORM_EPS = 1e-12
SQRT_HALF = 0.7071067811865476
F32, BF16 = jnp.float32, jnp.bfloat16
VMEM_BYTES = 63 * 2**20 + 2**19


def nn(a, b):
    return jnp.dot(a, b, preferred_element_type=F32)


def nt(a, b):
    return lax.dot_general(a, b, (((1,), (1,)), ((), ())), preferred_element_type=F32)


def tn(a, b):
    return lax.dot_general(a, b, (((0,), (0,)), ((), ())), preferred_element_type=F32)


def row_layout(bucket, lens, slots):
    shift = jnp.where(bucket == 0, SPAN // 4, jnp.where(bucket == 1, SPAN // 2, SPAN))
    row = jnp.where(bucket == 0, slots // (SPAN // 4), jnp.where(bucket == 1, slots // (SPAN // 2), slots // SPAN))
    length = jnp.zeros_like(slots)
    for j in range(8):
        length = jnp.where(row == j, lens[0, j], length)
    return row, (slots - row * shift) < length


def fill_masks(bucket, lens, bias):
    code = bucket[0]
    for b in range(bias.shape[0]):
        q = b * SPAN + lax.broadcasted_iota(jnp.int32, (SPAN, 1), 0)
        k = b * SPAN + lax.broadcasted_iota(jnp.int32, (1, SPAN), 1)
        q_row, _ = row_layout(code, lens, q)
        k_row, k_ok = row_layout(code, lens, k)
        bias[b] = jnp.where(q_row == jnp.where(k_ok, k_row, -1), 0.0, -1000000000.0)


def lane_half():
    return lax.broadcasted_iota(jnp.int32, (1, 128), 1) < HEAD_DIM


def attention(q, k, v, bias, ctx):
    low = lane_half()
    for pair in range(q.shape[1] // 128):
        cols = pl.ds(pair * 128, 128)
        q2, k2, v2 = q[:, cols], k[:, cols], v[:, cols]
        parts = []
        for side in (low, ~low):
            s = nt(jnp.where(side, q2, jnp.zeros_like(q2)), k2) + bias[...]
            e = jnp.exp(s - jnp.max(s, axis=1, keepdims=True))
            mass = jnp.sum(e, axis=1, keepdims=True)
            parts.append(nn(e.astype(BF16), v2) * (1.0 / mass))
        ctx[:, cols] = jnp.where(low, parts[0], parts[1]).astype(BF16)


def standardize(z):
    centred = z - jnp.mean(z, axis=-1, keepdims=True)
    inv = lax.rsqrt(jnp.mean(centred * centred, axis=-1, keepdims=True) + NORM_EPS)
    return centred * inv, inv


TILE = 128


def tiles(rows, body):
    for i in range(rows // TILE):
        body(pl.ds(i * TILE, TILE))


CW = 256
NZ, NY, NX = 4, 2, 2
ROWS = 48


class Place:
    def __init__(self):
        self.dp = lax.axis_index("dp")
        self.head = lax.axis_index("head")
        self.z = self.dp // 4
        self.y = lax.rem(self.dp // 2, 2)
        self.x = lax.rem(self.dp, 2)

    def at(self, dz=0, y=None, x=None):
        y = self.y if y is None else y
        x = self.x if x is None else x
        return ((self.z + dz) * 4 + y * 2 + x, self.head)


class Ring:
    def __init__(self, place, kinds, grad, pair_a, pair_b, path, zpath, zpair_a, zpair_b, send, recv, slot=None):
        self.p = place
        self.kinds = kinds
        self.grad, self.pair_a, self.pair_b, self.path = grad, pair_a, pair_b, path
        self.zpath, self.zpair_a, self.zpair_b = zpath, zpair_a, zpair_b
        self.send, self.recv = send, recv
        self.slot = slot or list(range(len(kinds)))
        flat = [c for c, k in enumerate(kinds) if not k.startswith("z")]
        deep = [c for c, k in enumerate(kinds) if k.startswith("z")]
        self.place_of = {c: i for i, c in enumerate(flat)} | {c: i for i, c in enumerate(deep)}

    def _pair(self, c, step):
        kind, p, i = self.kinds[c], self.p, self.place_of[c]
        g = self.grad.at[self.slot[c]]
        if kind.startswith("z"):
            axis = kind[1 + step]
            land = (self.zpair_a if step == 0 else self.zpair_b).at[i]
            view = g.at[p.z]
            if step == 0:
                pick = (lambda j: view.at[:, j]) if axis == "x" else (lambda j: view.at[j])
            else:
                pick = (lambda j: view.at[p.y, j]) if axis == "x" else (lambda j: view.at[j, p.x])
        else:
            axis = kind[step]
            land = (self.pair_a if step == 0 else self.pair_b).at[i]
            if step == 0:
                pick = (lambda j: g.at[:, :, j]) if axis == "x" else (lambda j: g.at[:, j])
            else:
                pick = (lambda j: g.at[:, p.y, j]) if axis == "x" else (lambda j: g.at[:, j, p.x])
        mine = p.x if axis == "x" else p.y
        to = p.at(x=1 - p.x) if axis == "x" else p.at(y=1 - p.y)
        copy = pltpu.make_async_remote_copy(
            src_ref=pick(1 - mine), dst_ref=land, send_sem=self.send.at[c, step], recv_sem=self.recv.at[c, step],
            device_id=to, device_id_type=MESH)
        return copy, pick(mine), land

    def pair_send(self, c, step):
        self._pair(c, step)[0].start()

    def pair_take(self, c, step):
        copy, mine, land = self._pair(c, step)
        copy.wait_recv()
        mine[...] += land[...]

    def _path_refs(self, c):
        kind, p, i = self.kinds[c], self.p, self.place_of[c]
        g = self.grad.at[self.slot[c]]
        if kind.startswith("z"):
            return (lambda lo, n: g.at[pl.ds(lo, n)]), self.zpath.at[i]
        return (lambda lo, n: g.at[pl.ds(lo, n), p.y, p.x]), self.path.at[i]

    def _hop(self, c, z, up):
        blocks, land = self._path_refs(c)
        if up:
            src, dst, k, dz = blocks(z + 1, 3 - z), land.at[pl.ds(0, 3 - z)], 2, 1
        else:
            src, dst, k, dz = blocks(0, z), land.at[pl.ds(5 - z, z)], 3, -1
        return pltpu.make_async_remote_copy(
            src_ref=src, dst_ref=dst, send_sem=self.send.at[c, k], recv_sem=self.recv.at[c, k],
            device_id=self.p.at(dz=dz), device_id_type=MESH)

    def path_start(self, c):
        @pl.when(self.p.z == 0)
        def _():
            self._hop(c, 0, True).start()

        @pl.when(self.p.z == 3)
        def _():
            self._hop(c, 3, False).start()

    def path_mid(self, c, first):
        blocks, land = self._path_refs(c)
        for z in (1, 2):
            up = (z == 1) == first

            @pl.when(self.p.z == z)
            def _(z=z, up=up):
                if up:
                    self._hop(c, z - 1, True).wait_recv()
                    own = blocks(z + 1, 3 - z)
                    own[...] += land[pl.ds(1, 3 - z)]
                    self._hop(c, z, True).start()
                else:
                    self._hop(c, z + 1, False).wait_recv()
                    own = blocks(0, z)
                    own[...] += land[pl.ds(4 - z, z)]
                    self._hop(c, z, False).start()

    def path_end(self, c):
        blocks, land = self._path_refs(c)
        for z in range(NZ):
            @pl.when(self.p.z == z)
            def _(z=z):
                if z == 0:
                    self._hop(c, 1, False).wait_recv()
                if z == 3:
                    self._hop(c, 2, True).wait_recv()
                own = blocks(z, 1)
                total = own[...]
                if z > 0:
                    total = total + land[pl.ds(0, 1)]
                if z < 3:
                    total = total + land[pl.ds(4, 1)]
                own[...] = total

    def drain(self, c):
        for step in (0, 1):
            self._pair(c, step)[0].wait_send()
        for z in range(NZ):
            @pl.when(self.p.z == z)
            def _(z=z):
                if z < 3:
                    self._hop(c, z, True).wait_send()
                if z > 0:
                    self._hop(c, z, False).wait_send()

    def stage(self, c, s):
        deep = self.kinds[c].startswith("z")
        if deep:
            if s == 0: self.path_start(c)
            elif s == 1: self.path_mid(c, True)
            elif s == 2: self.path_mid(c, False)
            elif s == 3: self.path_end(c); self.pair_send(c, 0)
            elif s == 4: self.pair_take(c, 0); self.pair_send(c, 1)
            elif s == 5: self.pair_take(c, 1)
        else:
            if s == 0: self.pair_send(c, 0)
            elif s == 1: self.pair_take(c, 0); self.pair_send(c, 1)
            elif s == 2: self.pair_take(c, 1); self.path_start(c)
            elif s == 3: self.path_mid(c, True)
            elif s == 4: self.path_mid(c, False)
            elif s == 5: self.path_end(c)

    def own(self, c):
        p = self.p
        return self.grad.at[self.slot[c], p.z, p.y, p.x]


def ring_scratch(kinds, slots):
    flat = sum(not k.startswith("z") for k in kinds)
    deep = len(kinds) - flat
    f = jnp.float32
    return [
        pltpu.VMEM((slots, NZ, NY, NX, ROWS, CW), f),
        pltpu.VMEM((flat, NZ, 2, ROWS, CW), f),
        pltpu.VMEM((flat, NZ, ROWS, CW), f),
        pltpu.VMEM((flat, 5, ROWS, CW), f),
        pltpu.VMEM((max(deep, 1), 5, NY, NX, ROWS, CW), f),
        pltpu.VMEM((max(deep, 1), 2, ROWS, CW), f),
        pltpu.VMEM((max(deep, 1), ROWS, CW), f),
        pltpu.SemaphoreType.DMA((len(kinds), 4)),
        pltpu.SemaphoreType.DMA((len(kinds), 4)),
    ]


INV_SQRT_2PI = 0.3989422804014327


class Butterfly:
    def __init__(self, place, value, land, send, recv):
        self.p, self.value, self.land, self.send, self.recv = place, value, land, send, recv

    def partner(self, step):
        p = self.p
        if step == 0:
            return p.at(x=1 - p.x)
        if step == 1:
            return p.at(y=1 - p.y)
        if step == 2:
            return p.at(dz=1 - 2 * lax.rem(p.z, 2))
        return p.at(dz=2 - 4 * (p.z // 2))

    def _copy(self, step):
        return pltpu.make_async_remote_copy(
            src_ref=self.value.at[step], dst_ref=self.land.at[step], send_sem=self.send.at[step],
            recv_sem=self.recv.at[step], device_id=self.partner(step), device_id_type=MESH)

    def start(self, step):
        self._copy(step).start()

    def take(self, step):
        self._copy(step).wait_recv()
        self.value[step + 1] = self.value[step] + self.land[step]

    def drain(self):
        for step in range(4):
            self._copy(step).wait_send()


def greet_all(p, scatter):
    barrier = pltpu.get_barrier_semaphore()

    def hello(to):
        pl.semaphore_signal(barrier, inc=1, device_id=to, device_id_type=MESH)
    hello((p.dp, 1 - p.head))
    if not scatter:
        return lambda: pl.semaphore_wait(barrier, 1)
    hello(p.at(x=1 - p.x))
    hello(p.at(y=1 - p.y))
    for dz in (1, -1):
        @pl.when((p.z + dz >= 0) & (p.z + dz < NZ))
        def _(dz=dz):
            hello(p.at(dz=dz))
    hello(p.at(dz=2 - 4 * (p.z // 2)))

    def wait():
        inner = (p.z == 1) | (p.z == 2)

        @pl.when(inner)
        def _():
            pl.semaphore_wait(barrier, 6)

        @pl.when(~inner)
        def _():
            pl.semaphore_wait(barrier, 5)
    return wait


def gelu_slope(u):
    return 0.5 * (1.0 + lax.erf(u * SQRT_HALF)) + u * (INV_SQRT_2PI * jnp.exp(-0.5 * u * u))


KINDS = ['yx', 'xy', 'xy', 'zxy', 'yx', 'zyx', 'yx', 'yx', 'yx', 'yx', 'xy', 'xy', 'zyx', 'xy', 'yx', 'xy', 'xy', 'zyx']

PROGRAM = [
    ("c", 0, 0), (0, 0), ("c", 0, 1), (1, 0), ("c", 0, 2), ("c", 0, 3), (3, 0), ("c", 0, 4), ("c", 0, 5), ("c", 0, 6),
    (4, 0), (2, 0), ("c", 0, 7), ("c", 0, 8), ("c", 0, 9), ("c", 0, 10), (0, 1), (1, 1), ("c", 0, 11), (5, 0),
    ("c", 0, 12), ("c", 0, 13), ("c", 0, 14), ("c", 0, 15), ("c", 0, 16), (3, 1), (6, 0), (4, 1), ("c", 0, 17),
    (2, 1), ("c", 0, 18), (1, 2), (10, 0), (0, 2), ("c", 0, 19), (4, 2), (3, 2), (5, 1), (7, 0), (6, 1), ("c", 0, 20),
    ("c", 0, 21), (1, 3), (2, 2), (11, 0), (3, 3), (0, 3), (10, 1), ("c", 0, 22), (4, 3), ("c", 0, 23), (12, 0),
    (5, 2), (6, 2), ("c", 0, 24), (2, 3), (1, 4), (8, 0), (7, 1), (0, 4), ("c", 0, 25), (4, 4), (5, 3), (10, 2),
    (1, 5), (2, 4), (11, 1), (0, 5), ("c", 0, 26), (13, 0), (4, 5), (3, 4), (2, 5), ("c", 0, 27), ("c", 0, 28),
    (12, 1), (7, 2), (8, 1), ("c", 0, 29), (6, 3), (5, 4), (9, 0), ("c", 0, 30), (10, 3), (11, 2), (3, 5), (13, 1),
    (15, 0), (7, 3), ("c", 0, 31), (12, 2), ("c", 0, 32), (17, 0), (8, 2), (6, 4), (11, 3), (5, 5), ("c", 0, 33),
    (10, 4), (14, 0), (9, 1), (12, 3), (7, 4), (6, 5), (11, 4), ("c", 0, 34), (10, 5), (13, 2), (16, 0), (7, 5),
    (15, 1), (11, 5), (9, 2), (17, 1), (14, 1), (8, 3), (12, 4), (13, 3), (16, 1), (15, 2), (9, 3), (17, 2), (14, 2),
    (8, 4), (12, 5), (15, 3), (16, 2), (13, 4), (17, 3), (9, 4), (14, 3), (8, 5), (13, 5), (15, 4), (9, 5), (17, 4),
    (16, 3), (14, 4), (15, 5), (17, 5), (14, 5), (16, 4), (16, 5),
]


def step_kernel(scatter, kinds, program, *refs):
    (bucket, lens, tokens_h), rest = refs[:3], refs[3:]
    th, rest = rest[:6], rest[6:]
    sh, rest = rest[:6], rest[6:]
    tb, rest = rest[:9], rest[9:]
    sb, rest = rest[:9], rest[9:]
    (out_h, grad_in_h, wide, small_out, q_h, k_h, v_h, ctx_h), rest = rest[:8], rest[8:]
    (tok, w1, w2, f, h1, dm, dz, n1, r1, own, land, vecs, value, vland,
     vsem, wsem, osem, ssem, rsem, bsem, vsend, vrecv, gsem, *ring_refs) = rest
    p = Place()
    dp, head = p.dp, p.head
    d, fw = w1.shape
    hw = q_h.shape[2]
    ready = greet_all(p, scatter)

    def copy(src, dst, sem):
        item = pltpu.make_async_copy(src, dst, sem)
        item.start()
        return item

    vectors = [copy(src, vecs.at[i, 0, pl.ds(0, src.shape[0])], vsem.at[i]) for i, src in enumerate((*tb, *sb))]
    tb, sb = ([vecs.at[base + i, :, pl.ds(0, src.shape[0])] for i, src in enumerate(group)]
              for base, group in ((0, tb), (9, sb)))

    def swap(slot, src):
        return pltpu.make_async_remote_copy(
            src_ref=src, dst_ref=land.at[slot], send_sem=ssem.at[slot], recv_sem=rsem.at[slot],
            device_id=(dp, 1 - head), device_id_type=MESH)

    def both(body):
        def step(b, carry):
            body(b)
            return carry
        lax.fori_loop(0, 2, step, 0)

    def forward_part(wqkv, wo, q, k, v, ctx, target, bias):
        own2 = dz
        def attend_weights(src):
            return [copy(src[j], wqkv.at[:, pl.ds(j * hw, hw)], wsem.at[1 + j]) for j in range(3)] + [copy(src[3], wo, wsem.at[4])]

        def feed_weights(src):
            return [copy(src[4], w1, wsem.at[5]), copy(src[5], w2, wsem.at[6])]

        def wait(items):
            for item in items:
                item.wait()
        tokens_in = copy(tokens_h, tok, wsem.at[0])
        attend_in = attend_weights(th)
        feed_in = feed_weights(th)
        fill_masks(bucket, lens, bias)
        value[...] = jnp.zeros_like(value)

        def attend(b, vectors):
            a = tok[b]
            q[b] = ((nn(a, wqkv[:, 0:hw]) + vectors[0][...]).astype(BF16).astype(F32) * (1.0 / 8.0)).astype(BF16)
            k[b] = nn(a, wqkv[:, hw:2 * hw]).astype(BF16)
            v[b] = (nn(a, wqkv[:, 2 * hw:3 * hw]) + vectors[1][...]).astype(BF16)
            attention(q.at[b], k.at[b], v.at[b], bias.at[b], ctx.at[b])
            own[b] = nn(ctx[b], wo[...])

        def feed(b, vectors):
            for j in range(fw // CW):
                cols = pl.ds(j * CW, CW)
                u = nn(h1[b], w1[:, cols]) + vectors[5][:, cols]
                f[b, :, cols] = (0.5 * u * (1.0 + lax.erf(u * SQRT_HALF))).astype(BF16)
            own2[b] = nn(f[b], w2[...])

        def first_sum(b, rows, vectors):
            return tok[b, rows, :].astype(F32) + ((own[b, rows, :] + land[b, rows, :]) + vectors[2][...])

        def second_sum(b, rows, vectors, residual):
            return residual + ((own2[b, rows, :] + land[2 + b, rows, :]) + vectors[6][...])

        def teach_attend(b):
            attend(b, tb)
            swap(b, own.at[b]).start()

        def teach_feed(b):
            swap(b, own.at[b]).wait()

            def norm(rows):
                n, _ = standardize(first_sum(b, rows, tb))
                h = n * tb[3][...] + tb[4][...]
                target[b, rows, :] = h
                h1[b, rows, :] = h.astype(BF16)
            tiles(SPAN, norm)
            feed(b, tb)
            swap(2 + b, own2.at[b]).start()

        def study_attend(b):
            swap(2 + b, own2.at[b]).wait()

            def norm(rows):
                n, _ = standardize(second_sum(b, rows, tb, target[b, rows, :]))
                target[b, rows, :] = n * tb[7][...] + tb[8][...]
            tiles(SPAN, norm)
            attend(b, sb)
            swap(b, own.at[b]).start()

        def study_feed(b):
            @pl.when(b == 0)
            def _():
                swap(0, own.at[0]).wait()

            def norm(rows):
                n, r = standardize(first_sum(b, rows, sb))
                n1[b, rows, :] = n
                slots = b * SPAN + rows.start + lax.broadcasted_iota(jnp.int32, (TILE, 1), 0)
                real = jnp.where(row_layout(bucket[0], lens, slots)[1], 1.0, 0.0)
                r1[b, rows, :] = jnp.where(lane_half(), r, real)
                h1[b, rows, :] = (n * sb[3][...] + sb[4][...]).astype(BF16)
            tiles(SPAN, norm)
            feed(b, sb)

            @pl.when(b == 0)
            def _():
                swap(1, own.at[1]).wait()
            swap(2 + b, own2.at[b]).start()

        def study_end(b):
            swap(2 + b, own2.at[b]).wait()
            total = [jnp.zeros((1, d), F32)] * 3

            def norm(rows):
                residual = n1[b, rows, :] * sb[3][...] + sb[4][...]
                n2, r2 = standardize(second_sum(b, rows, sb, residual))
                result = n2 * sb[7][...] + sb[8][...]
                dy = (result - target[b, rows, :]) * r1[b, rows, HEAD_DIM:HEAD_DIM + 1]
                own[b, rows, :] = result
                scaled = dy * sb[7][...]
                out = r2 * (scaled - jnp.mean(scaled, axis=-1, keepdims=True) - n2 * jnp.mean(scaled * n2, axis=-1, keepdims=True))
                dz[b, rows, :] = out
                low = out.astype(BF16)
                dm[b, rows, :] = low
                for i, item in enumerate((low.astype(F32), dy * n2, dy)):
                    total[i] = total[i] + jnp.sum(item, axis=0, keepdims=True)
            tiles(SPAN, norm)
            for i in range(3):
                value[0, 3 + i:4 + i, 0:d] += total[i]

        wait(vectors)
        wait([tokens_in] + attend_in)
        ready()
        both(teach_attend)
        attend_in = attend_weights(sh)
        wait(feed_in)
        both(teach_feed)
        feed_in = feed_weights(sh)
        wait(attend_in)
        both(study_attend)
        spills = [copy(src, dst, osem.at[i]) for i, (src, dst) in enumerate(((q, q_h), (k, k_h), (v, v_h), (ctx, ctx_h)))]
        wait(feed_in)
        both(study_feed)
        both(study_end)
        copy(own, out_h, osem.at[4])
        wait(spills)
    return_out = pltpu.make_async_copy(own, out_h, osem.at[4])

    def V(*shape, dtype=F32):
        return pltpu.VMEM(shape, dtype)
    pl.run_scoped(forward_part, V(d, 3 * hw, dtype=BF16), V(hw, d, dtype=BF16), *[V(2, SPAN, hw, dtype=BF16)] * 4,
                  V(2, SPAN, d), V(2, SPAN, SPAN))

    def backward_part(grad):
        ring = Ring(p, kinds, grad, *ring_refs) if scatter else None
        fly = Butterfly(p, value, vland, vsend, vrecv) if scatter else None
        all_cols = pl.ds(0, CW)
        compute, got = {}, {}

        def put(c, cols, block):
            for i in range(NZ * NY * NX):
                grad[c, i // 4, i // 2 % 2, i % 2, :, cols] = block[i * ROWS:(i + 1) * ROWS]

        def return_grad(c):
            cols = pl.ds(c * CW, CW)
            put(c, all_cols, tn(dm[...].reshape(-1, d), f[:, :, cols].reshape(-1, CW)))

        def slope(j):
            cols = pl.ds(j * CW, CW)

            def half(b, total):
                u = nn(h1[b], w1[:, cols]) + sb[5][:, cols]
                g = nt(dm[b], w2[cols, :])
                du = (g * gelu_slope(u)).astype(BF16)
                f[b, :, cols] = du
                return total + jnp.sum(du.astype(F32), axis=0, keepdims=True)
            total = lax.fori_loop(0, 2, half, jnp.zeros((1, CW), F32))
            value[0, 6 + j // 3:7 + j // 3, pl.ds(j % 3 * CW, CW)] = total

        def hidden_grad(j):
            cols = pl.ds(j * CW, CW)
            put(6 + j, all_cols, tn(h1[...].reshape(-1, d), f[:, :, cols].reshape(-1, CW)))

        def back_first():
            return_out.wait()

            def half(b):
                own[b] = nt(f[b], w1[...])
                swap(b, own.at[b]).start()
            both(half)
            for i, (name, src, dst) in enumerate((
                    ("wo", sh[3], wo), ("q", q_h, q), ("k", k_h, k), ("v", v_h, v), ("ctx", ctx_h, ctx),
                    ("wq", sh[0], wqkv.at[:, pl.ds(0, hw)]), ("wk", sh[1], wqkv.at[:, pl.ds(hw, hw)]),
                    ("wv", sh[2], wqkv.at[:, pl.ds(2 * hw, hw)]))):
                got[name] = copy(src, dst, bsem.at[i])
        q, k, v, ctx = (f.at[:, :, pl.ds(i * hw, hw)] for i in range(4))
        dctx = h1.at[:, :, pl.ds(0, hw)]
        do = dm
        wqkv = w1.at[:, pl.ds(0, 3 * hw)]
        wo = w2.at[pl.ds(0, hw)]
        bias = n1.at[:, :, pl.ds(0, SPAN)]

        def norm_back():
            def half(b):
                swap(b, own.at[b]).wait()
                total = [jnp.zeros((1, d), F32)] * 3

                def tile(rows):
                    up = dz[b, rows, :] + (own[b, rows, :] + land[b, rows, :])
                    n = n1[b, rows, :]
                    scaled = up * sb[3][...]
                    out = r1[b, rows, 0:1] * (scaled - jnp.mean(scaled, axis=-1, keepdims=True)
                                              - n * jnp.mean(scaled * n, axis=-1, keepdims=True))
                    dz[b, rows, :] = out
                    low = out.astype(BF16)
                    do[b, rows, :] = low
                    for i, item in enumerate((low.astype(F32), up * n, up)):
                        total[i] = total[i] + jnp.sum(item, axis=0, keepdims=True)
                tiles(SPAN, tile)
                for i in range(3):
                    value[0, i:i + 1, 0:d] += total[i]
            both(half)
            fill_masks(bucket, lens, bias)

        def context_grad():
            got["wo"].wait()

            def half(b):
                dctx[b] = nt(do[b], wo[...]).astype(BF16)
            both(half)
            for name in ("q", "k", "v", "ctx"):
                got[name].wait()

        def attend_back(pair, b):
            low_side = lane_half()
            cols = pl.ds(pair * 128, 128)
            q2, k2, v2, dc2 = q[b, :, cols], k[b, :, cols], v[b, :, cols], dctx[b, :, cols]
            parts = []
            for side in (low_side, ~low_side):
                zero = jnp.zeros_like(q2)
                s = nt(jnp.where(side, q2, zero), k2) + bias[b]
                e = jnp.exp(s - jnp.max(s, axis=1, keepdims=True))
                probs = e * (1.0 / jnp.sum(e, axis=1, keepdims=True))
                dprob = nt(jnp.where(side, dc2, zero), v2)
                ds = (probs * (dprob - jnp.sum(probs * dprob, axis=1, keepdims=True))).astype(BF16)
                parts.append((nn(ds, k2), tn(ds, q2), tn(probs.astype(BF16), dc2)))
            dq = (jnp.where(low_side, parts[0][0], parts[1][0]) * (1.0 / 8.0)).astype(BF16)
            dk = jnp.where(low_side, parts[0][1], parts[1][1]).astype(BF16)
            dv = jnp.where(low_side, parts[0][2], parts[1][2]).astype(BF16)
            q[b, :, cols], k[b, :, cols], v[b, :, cols] = dq, dk, dv
            extra = pl.ds(d, 128)
            value[0, pair:pair + 1, extra] += jnp.sum(dq.astype(F32), axis=0, keepdims=True)
            value[0, 3 + pair:4 + pair, extra] += jnp.sum(dv.astype(F32), axis=0, keepdims=True)

        def attend_grad(pair, second):
            cols = pl.ds(pair * 128, 128)
            a = tok[...].reshape(-1, d)
            c = 12 + 2 * pair + second
            if second:
                put(c, pl.ds(0, 128), tn(a, k[:, :, cols].reshape(-1, 128)))
                put(c, pl.ds(128, 128), tn(a, v[:, :, cols].reshape(-1, 128)))
            else:
                put(c, pl.ds(0, 128), tn(do[...].reshape(-1, d), ctx[:, :, cols].reshape(-1, 128)))
                put(c, pl.ds(128, 128), tn(a, q[:, :, cols].reshape(-1, 128)))

        def back_in():
            for name in ("wq", "wk", "wv"):
                got[name].wait()

            def half(b):
                own[b] = (nt(q[b], wqkv[:, 0:hw]) + nt(k[b], wqkv[:, hw:2 * hw])) + nt(v[b], wqkv[:, 2 * hw:3 * hw])
                swap(2 + b, own.at[b]).start()
            both(half)
            if scatter:
                fly.start(0)

        def finish_in():
            def half(b):
                swap(2 + b, own.at[b]).wait()

                def tile(rows):
                    dz[b, rows, :] += own[b, rows, :] + land[2 + b, rows, :]
                tiles(SPAN, tile)
            both(half)
            copy(dz, grad_in_h, osem.at[5])

        for c in range(6):
            compute[c] = functools.partial(return_grad, c)
            compute[6 + 2 * c] = functools.partial(slope, c)
            compute[7 + 2 * c] = functools.partial(hidden_grad, c)
        compute[18], compute[19], compute[20], compute[33], compute[34] = back_first, norm_back, context_grad, back_in, finish_in
        for pair in range(3):
            compute[21 + 4 * pair] = functools.partial(attend_back, pair, 0)
            compute[22 + 4 * pair] = functools.partial(attend_back, pair, 1)
            compute[23 + 4 * pair] = functools.partial(attend_grad, pair, 0)
            compute[24 + 4 * pair] = functools.partial(attend_grad, pair, 1)

        def owned(c):
            return pltpu.make_async_copy(ring.own(c), wide.at[:, pl.ds(c * CW, CW)], gsem.at[c])

        after, steps = 0, 0
        for item in program:
            if item[0] == "c":
                compute[item[2]]()
                after = -6 if item[2] == 33 else after
            elif scatter:
                ring.stage(*item)
                if item[1] == 5:
                    owned(item[0]).start()
            if scatter and after < 0:
                after += 1
                if after == 0 and steps < 4:
                    fly.take(steps)
                    steps += 1
                    if steps < 4:
                        fly.start(steps)
                        after = -6
        if scatter:
            for step in range(steps, 4):
                fly.take(step)
                if step < 3:
                    fly.start(step + 1)
            small_out[...] = value[4]
            for c in range(len(kinds)):
                ring.drain(c)
                owned(c).wait()
            fly.drain()
        else:
            rows = copy(grad, wide, osem.at[6])
            small_out[...] = value[0]
            rows.wait()
        pltpu.make_async_copy(dz, grad_in_h, osem.at[5]).wait()

    count = (2 * fw + 4 * hw) // CW
    pl.run_scoped(backward_part, V(count, NZ, NY, NX, ROWS, CW))


def distill(scatter, tokens, bucket, lens, teacher, student):
    def cut(layer):
        wq, bq, wk, wv, bv, wo, bo, g1, s1, w1, b1, w2, b2, g2, s2 = layer
        return [wq, wk, wv, wo, w1, w2], [bq, bv, bo, g1, s1, b1, b2, g2, s2]
    tw, tv = cut(teacher)
    sw, sv = cut(student)
    toks, d = tokens.shape
    hw, fw = tw[0].shape[1], tw[4].shape[1]
    count = (2 * fw + 4 * hw) // CW
    halves, b = toks // SPAN, BF16
    kinds = KINDS
    program = PROGRAM
    hbm, vmem, smem = (pl.BlockSpec(memory_space=m) for m in (pl.ANY, pltpu.VMEM, pltpu.SMEM))
    def S(*shape, dtype=F32):
        return jax.ShapeDtypeStruct(shape, dtype)
    def V(*shape, dtype=F32):
        return pltpu.VMEM(shape, dtype)
    dma = pltpu.SemaphoreType.DMA
    wide = S(ROWS, count * CW) if scatter else S(count, NZ, NY, NX, ROWS, CW)
    outs = (S(halves, SPAN, d), S(halves, SPAN, d), wide, S(8, 896)) + (S(halves, SPAN, hw, dtype=b),) * 4
    return pl.pallas_call(
        functools.partial(step_kernel, scatter, kinds, program),
        out_shape=outs,
        in_specs=[smem, smem] + [hbm] * 31,
        out_specs=(hbm, hbm, hbm, vmem) + (hbm,) * 4,
        scratch_shapes=[
            V(halves, SPAN, d, dtype=b), V(d, fw, dtype=b), V(fw, d, dtype=b), V(halves, SPAN, fw, dtype=b), V(halves, SPAN, d, dtype=b),
            V(halves, SPAN, d, dtype=b), V(halves, SPAN, d), V(halves, SPAN, d), V(halves, SPAN, 128), V(2, SPAN, d), V(4, SPAN, d),
            V(18, 1, fw), V(5, 8, 896), V(4, 8, 896),
            dma((18,)), dma((7,)), dma((7,)), dma((4,)), dma((4,)), dma((8,)), dma((4,)), dma((4,)), dma((count,))]
        + (ring_scratch(kinds, count)[1:] if scatter else []),
        compiler_params=pltpu.CompilerParams(collective_id=1, has_side_effects=True, vmem_limit_bytes=VMEM_BYTES),
    )(bucket, lens, tokens.reshape(halves, SPAN, d), *tw, *sw, *tv, *sv)[:4]


def finish_kernel(out_h, gin_h, wide_h, small_h, out, gin, gq, gk, gv, go, g1w, g2w, *rest):
    small_outs, (wide, small, stage, sem_in, sem_out) = rest[:9], rest[9:]
    d = out.shape[2]
    fw, hw = g1w.shape[1], gq.shape[1]
    count = [0]

    def copy(src, dst):
        count[0] += 1
        return pltpu.make_async_copy(src, dst, sem_out.at[count[0] - 1])

    loads, stores = [(small_h, small), (wide_h, wide)], [[], []]
    for dst, row in zip((small_outs[i] for i in (2, 3, 4, 6, 7, 8)), range(6)):
        stores[0].append(copy(small.at[row, pl.ds(0, d)], dst))
    for half in range(2):
        stores[0].append(copy(small.at[6 + half, pl.ds(0, d)], small_outs[5].at[pl.ds(half * d, d)]))
    for pair in range(hw // 128):
        at, extra = pl.ds(pair * 128, 128), pl.ds(d, 128)
        stores[0].append(copy(small.at[pair, extra], small_outs[0].at[at]))
        stores[0].append(copy(small.at[3 + pair, extra], small_outs[1].at[at]))
        for i, dst in enumerate((go, gq, gk, gv)):
            stores[1].append(copy(wide.at[:, pl.ds(2 * fw + pair * 512 + i * 128, 128)], dst.at[:, at]))
    stores[1].append(copy(wide.at[:, pl.ds(0, fw)], g2w))
    stores[1].append(copy(wide.at[:, pl.ds(fw, fw)], g1w))
    for src, dst in ((out_h, out), (gin_h, gin)):
        for b in range(2):
            for rows in (pl.ds(0, SPAN // 2), pl.ds(SPAN // 2, SPAN // 2)):
                place = stage.at[len(loads) - 2]
                loads.append((src.at[b, rows], place))
                stores.append([copy(place, dst.at[b, rows])])
    loads = [pltpu.make_async_copy(src, dst, sem_in.at[i]) for i, (src, dst) in enumerate(loads)]
    for item in loads:
        item.start()
    for load, group in zip(loads, stores):
        load.wait()
        for item in group:
            item.start()
    for group in stores:
        for item in group:
            item.wait()


def finish(out_raw, gin_raw, wide, small, hw, fw):
    d = out_raw.shape[2]
    def S(*shape):
        return jax.ShapeDtypeStruct(shape, F32)
    hbm = pl.BlockSpec(memory_space=pl.ANY)
    return pl.pallas_call(
        finish_kernel,
        out_shape=(S(*out_raw.shape), S(*gin_raw.shape), S(ROWS, hw), S(ROWS, hw), S(ROWS, hw), S(ROWS, hw), S(ROWS, fw), S(ROWS, fw),
                   S(hw), S(hw), S(d), S(d), S(d), S(fw), S(d), S(d), S(d)),
        in_specs=[hbm] * 4,
        out_specs=(hbm,) * 17,
        scratch_shapes=[pltpu.VMEM(wide.shape, F32), pltpu.VMEM(small.shape, F32), pltpu.VMEM((8, SPAN // 2, d), F32),
                        pltpu.SemaphoreType.DMA((10,)), pltpu.SemaphoreType.DMA((48,))],
        compiler_params=pltpu.CompilerParams(vmem_limit_bytes=VMEM_BYTES),
    )(out_raw, gin_raw, wide, small)


def shards(*args):
    tokens, row_bucket, row_lengths = args[:3]
    teacher, student = args[3:18], args[18:33]
    d = tokens.shape[1]
    count = lax.axis_size("dp")
    scatter = count == NZ * NY * NX
    out, *got = distill(scatter, tokens, row_bucket, row_lengths, teacher, student)
    if scatter:
        fw, hw = student[9].shape[1], student[0].shape[1]
        out, grad_in, gq, gk, gv, go, g1, g2, qb, vb, ob, g1g, s1g, b1g, b2g, g2g, s2g = finish(out, *got, hw, fw)
    else:
        grad_in, wide, small = got
        fw, hw = student[9].shape[1], student[0].shape[1]
        rows = wide.reshape(wide.shape[0], d, CW)
        side = lambda group: jnp.concatenate([rows[c] for c in group], axis=1)
        steps = fw // CW
        last = [2 * steps + i for i in range(2 * hw // 128)]
        first, second = ([rows[c] for c in last[i::2]] for i in (0, 1))
        mats = [
            jnp.concatenate([m[:, 128:] for m in first], axis=1),
            jnp.concatenate([m[:, :128] for m in second], axis=1),
            jnp.concatenate([m[:, 128:] for m in second], axis=1),
            jnp.concatenate([m[:, :128] for m in first], axis=1),
            side(range(steps, 2 * steps)),
            side(range(steps)),
        ]
        gq, gk, gv, go, g1, g2 = (lax.psum_scatter(m, "dp", scatter_dimension=0, tiled=True) for m in mats)
        small = lax.psum(small, "dp")
        qb, vb = small[0:3, d:].reshape(-1), small[3:6, d:].reshape(-1)
        ob, g1g, s1g, b2g, g2g, s2g = (small[i, :d] for i in range(6))
        b1g = small[6:8, :d].reshape(-1)
    toks = tokens.shape[0]
    return (
        out.reshape(toks, d), grad_in.reshape(toks, d), gq, qb, gk, gv, vb, go.T, ob, g1g, s1g, g1, b1g, g2.T, b2g, g2g, s2g
    )


def solution(mesh):
    placed = (
        P("dp", None),
        P("dp"),
        P("dp", None),
        P(None, "head"),
        P("head"),
        P(None, "head"),
        P(None, "head"),
        P("head"),
        P("head", None),
        P(),
        P(),
        P(),
        P(None, "head"),
        P("head"),
        P("head", None),
        P(),
        P(),
        P(),
        P(None, "head"),
        P("head"),
        P(None, "head"),
        P(None, "head"),
        P("head"),
        P("head", None),
        P(),
        P(),
        P(),
        P(None, "head"),
        P("head"),
        P("head", None),
        P(),
        P(),
        P(),
    )
    return jax.shard_map(
        shards,
        mesh=mesh,
        in_specs=placed,
        out_specs=(
            P("dp", None),
            P("dp", None),
            P("dp", "head"),
            P("head"),
            P("dp", "head"),
            P("dp", "head"),
            P("head"),
            P("head", "dp"),
            P(),
            P(),
            P(),
            P("dp", "head"),
            P("head"),
            P("head", "dp"),
            P(),
            P(),
            P(),
        ),
        check_vma=False,
    )
```

```python
import functools

import jax
import jax.numpy as jnp
from jax import lax
from jax.experimental import pallas as pl
from jax.experimental.pallas import tpu as pltpu
from jax.sharding import PartitionSpec as P

MESH = pl.DeviceIdType.MESH
HEAD_DIM = 64
SPAN = 512
NORM_EPS = 1e-12
SQRT_HALF = 0.7071067811865476
F32, BF16 = jnp.float32, jnp.bfloat16
VMEM_BYTES = 63 * 2**20 + 2**19


def nn(a, b):
    return jnp.dot(a, b, preferred_element_type=F32)


def nt(a, b):
    return lax.dot_general(a, b, (((1,), (1,)), ((), ())), preferred_element_type=F32)


def tn(a, b):
    return lax.dot_general(a, b, (((0,), (0,)), ((), ())), preferred_element_type=F32)


def row_layout(bucket, lens, slots):
    shift = jnp.where(bucket == 0, SPAN // 4, jnp.where(bucket == 1, SPAN // 2, SPAN))
    row = jnp.where(bucket == 0, slots // (SPAN // 4), jnp.where(bucket == 1, slots // (SPAN // 2), slots // SPAN))
    length = jnp.zeros_like(slots)
    for j in range(8):
        length = jnp.where(row == j, lens[0, j], length)
    return row, (slots - row * shift) < length


def fill_masks(bucket, lens, bias):
    code = bucket[0]
    for b in range(bias.shape[0]):
        q = b * SPAN + lax.broadcasted_iota(jnp.int32, (SPAN, 1), 0)
        k = b * SPAN + lax.broadcasted_iota(jnp.int32, (1, SPAN), 1)
        q_row, _ = row_layout(code, lens, q)
        k_row, k_ok = row_layout(code, lens, k)
        bias[b] = jnp.where(q_row == jnp.where(k_ok, k_row, -1), 0.0, -1000000000.0)


def lane_half():
    return lax.broadcasted_iota(jnp.int32, (1, 128), 1) < HEAD_DIM


def attention(q, k, v, bias, ctx):
    low = lane_half()
    for pair in range(q.shape[1] // 128):
        cols = pl.ds(pair * 128, 128)
        q2, k2, v2 = q[:, cols], k[:, cols], v[:, cols]
        parts = []
        for side in (low, ~low):
            s = nt(jnp.where(side, q2, jnp.zeros_like(q2)), k2) + bias[...]
            e = jnp.exp(s - jnp.max(s, axis=1, keepdims=True))
            mass = jnp.sum(e, axis=1, keepdims=True)
            parts.append(nn(e.astype(BF16), v2) * (1.0 / mass))
        ctx[:, cols] = jnp.where(low, parts[0], parts[1]).astype(BF16)


def standardize(z):
    centred = z - jnp.mean(z, axis=-1, keepdims=True)
    inv = lax.rsqrt(jnp.mean(centred * centred, axis=-1, keepdims=True) + NORM_EPS)
    return centred * inv, inv


TILE = 128
PART = SPAN // 2


def tiles(rows, body, first=0):
    for i in range(rows // TILE):
        body(pl.ds(first + i * TILE, TILE))


CW = 256
NZ, NY, NX = 4, 2, 2
ROWS = 48


class Place:
    def __init__(self):
        self.dp = lax.axis_index("dp")
        self.head = lax.axis_index("head")
        self.z = self.dp // 4
        self.y = lax.rem(self.dp // 2, 2)
        self.x = lax.rem(self.dp, 2)

    def at(self, z=None, y=None, x=None):
        z, y, x = (mine if given is None else given for given, mine in ((z, self.z), (y, self.y), (x, self.x)))
        return (z * 4 + y * 2 + x, self.head)


def landing(pieces):
    places, used = [], {False: [], True: []}
    for kind, _, _, width in pieces:
        taken = used[kind[0] in "zd"]
        i = next((i for i, cols in enumerate(taken) if cols + width <= CW), len(taken))
        taken[i:i + 1] = [(taken[i] if i < len(taken) else 0) + width]
        places.append((i, taken[i] - width))
    return places, len(used[False]), len(used[True])


class Ring:
    def __init__(self, place, pieces, grad, pair_a, pair_b, path, zpath, zpair_a, zpair_b, send, recv):
        self.p, self.pieces, self.grad = place, pieces, grad
        self.lands = (pair_a, pair_b, path), (zpair_a, zpair_b, zpath)
        self.send, self.recv = send, recv
        self.places = landing(pieces)[0]

    def _refs(self, c, which):
        kind, chunk, col, width = self.pieces[c]
        deep = kind[0] in "zd"
        i, land_col = self.places[c]
        land = self.lands[deep][which]
        every = (slice(None),) * (len(land.shape) - 2)
        return deep, self.grad.at[chunk, :, :, :, :, pl.ds(col, width)], land.at[(i, *every, pl.ds(land_col, width))]

    def _pair(self, c, step):
        p = self.p
        deep, g, land = self._refs(c, step)
        axis = [a for a in self.pieces[c][0] if a in "xy"][step]
        if deep:
            view = g.at[p.z]
            if step == 0:
                pick = (lambda j: view.at[:, j]) if axis == "x" else (lambda j: view.at[j])
            else:
                pick = (lambda j: view.at[p.y, j]) if axis == "x" else (lambda j: view.at[j, p.x])
        elif step == 0:
            pick = (lambda j: g.at[:, :, j]) if axis == "x" else (lambda j: g.at[:, j])
        else:
            pick = (lambda j: g.at[:, p.y, j]) if axis == "x" else (lambda j: g.at[:, j, p.x])
        mine = p.x if axis == "x" else p.y
        to = p.at(x=1 - p.x) if axis == "x" else p.at(y=1 - p.y)
        copy = pltpu.make_async_remote_copy(
            src_ref=pick(1 - mine), dst_ref=land, send_sem=self.send.at[c], recv_sem=self.recv.at[c, step],
            device_id=to, device_id_type=MESH)
        return copy, pick(mine), land

    def pair_send(self, c, step):
        self._pair(c, step)[0].start()

    def pair_take(self, c, step):
        copy, mine, land = self._pair(c, step)
        copy.wait_recv()
        mine[...] += land[...]

    def _path_refs(self, c):
        p = self.p
        deep, g, land = self._refs(c, 2)
        if deep:
            return (lambda lo, n: g.at[pl.ds(lo, n)]), land
        return (lambda lo, n: g.at[pl.ds(lo, n), p.y, p.x]), land

    def _hop(self, c, z, up):
        blocks, land = self._path_refs(c)
        if up:
            src, dst, k, to = blocks(z + 1, 3 - z), land.at[pl.ds(0, 3 - z)], 2, self.p.z + 1
        else:
            src, dst, k, to = blocks(0, z), land.at[pl.ds(5 - z, z)], 3, self.p.z - 1
        return pltpu.make_async_remote_copy(
            src_ref=src, dst_ref=dst, send_sem=self.send.at[c], recv_sem=self.recv.at[c, k],
            device_id=self.p.at(z=to), device_id_type=MESH)

    def path_start(self, c):
        @pl.when(self.p.z == 0)
        def _():
            self._hop(c, 0, True).start()

        @pl.when(self.p.z == 3)
        def _():
            self._hop(c, 3, False).start()

    def path_mid(self, c, first):
        blocks, land = self._path_refs(c)
        for z in (1, 2):
            up = (z == 1) == first

            @pl.when(self.p.z == z)
            def _(z=z, up=up):
                if up:
                    self._hop(c, z - 1, True).wait_recv()
                    own = blocks(z + 1, 3 - z)
                    own[...] += land[pl.ds(1, 3 - z)]
                    self._hop(c, z, True).start()
                else:
                    self._hop(c, z + 1, False).wait_recv()
                    own = blocks(0, z)
                    own[...] += land[pl.ds(4 - z, z)]
                    self._hop(c, z, False).start()

    def path_end(self, c):
        blocks, land = self._path_refs(c)
        for z in range(NZ):
            @pl.when(self.p.z == z)
            def _(z=z):
                if z == 0:
                    self._hop(c, 1, False).wait_recv()
                if z == 3:
                    self._hop(c, 2, True).wait_recv()
                own = blocks(z, 1)
                total = own[...]
                if z > 0:
                    total = total + land[pl.ds(0, 1)]
                if z < 3:
                    total = total + land[pl.ds(4, 1)]
                own[...] = total

    def _direct(self, c, j):
        blocks, land = self._path_refs(c)
        to = lax.rem(self.p.z + j, NZ)
        return pltpu.make_async_remote_copy(
            src_ref=blocks(to, 1), dst_ref=land.at[pl.ds(j - 1, 1)], send_sem=self.send.at[c], recv_sem=self.recv.at[c, 2],
            device_id=self.p.at(z=to), device_id_type=MESH)

    def direct_send(self, c):
        for j in (1, 2, 3):
            self._direct(c, j).start()

    def direct_take(self, c):
        blocks, land = self._path_refs(c)
        pltpu.make_async_copy(land.at[pl.ds(0, 3)], land.at[pl.ds(0, 3)], self.recv.at[c, 2]).wait()
        own = blocks(self.p.z, 1)
        own[...] += (land[pl.ds(0, 1)] + land[pl.ds(1, 1)]) + land[pl.ds(2, 1)]

    def drain(self, c):
        width = self.pieces[c][3]
        blocks = self.lands[False][2].at[pl.ds(0, 3), :, :, pl.ds(0, width)]
        pltpu.make_async_copy(blocks, blocks, self.send.at[c]).wait()

    def stages(self, c):
        take = lambda step: functools.partial(self.pair_take, c, step)
        send = lambda step: functools.partial(self.pair_send, c, step)
        if "d" in self.pieces[c][0]:
            column = [[functools.partial(self.direct_send, c)], [functools.partial(self.direct_take, c)]]
        else:
            column = [[functools.partial(self.path_start, c)], [functools.partial(self.path_mid, c, True)],
                      [functools.partial(self.path_mid, c, False)], [functools.partial(self.path_end, c)]]
        if self.pieces[c][0][0] in "zd":
            return column[:-1] + [column[-1] + [send(0)], [take(0), send(1)], [take(1)]]
        return [[send(0)], [take(0), send(1)], [take(1)] + column[0]] + column[1:]

    def stage(self, c, s):
        steps = self.stages(c)
        for step in steps[s]:
            step()
        return s == len(steps) - 1

    def own(self, c):
        p = self.p
        _, chunk, col, width = self.pieces[c]
        return self.grad.at[chunk, p.z, p.y, p.x, :, pl.ds(col, width)], pl.ds(chunk * CW + col, width)


def ring_scratch(pieces):
    _, flat, deep = landing(pieces)
    f = jnp.float32
    return [
        pltpu.VMEM((flat, NZ, 2, ROWS, CW), f),
        pltpu.VMEM((flat, NZ, ROWS, CW), f),
        pltpu.VMEM((flat, 5, ROWS, CW), f),
        pltpu.VMEM((deep, 5, NY, NX, ROWS, CW), f),
        pltpu.VMEM((deep, 2, ROWS, CW), f),
        pltpu.VMEM((deep, ROWS, CW), f),
        pltpu.SemaphoreType.DMA((len(pieces),)),
        pltpu.SemaphoreType.DMA((len(pieces), 4)),
    ]


def greet(place, scatter):
    barrier = pltpu.get_barrier_semaphore()
    p = place
    others = [(p.dp, 1 - p.head)]
    if scatter:
        others += [p.at(x=1 - p.x), p.at(y=1 - p.y), p.at(x=1 - p.x, y=1 - p.y)] + [p.at(z=lax.rem(p.z + j, NZ)) for j in (1, 2, 3)]
    for to in others:
        pl.semaphore_signal(barrier, inc=1, device_id=to, device_id_type=MESH)
    return lambda: pl.semaphore_wait(barrier, len(others))


PIECES = [
    ("dxy", 0, 0, 256), ("xy", 1, 0, 256), ("yxd", 2, 0, 256), ("xy", 3, 0, 256), ("zyx", 4, 0, 256),
    ("yx", 5, 0, 256), ("xy", 6, 0, 256), ("yx", 7, 0, 256), ("dxy", 8, 0, 256), ("xy", 9, 0, 256),
    ("xy", 10, 0, 256), ("yx", 11, 0, 256), ("zyx", 12, 0, 256), ("yx", 13, 0, 256), ("xyd", 14, 0, 256),
    ("yxd", 15, 0, 256), ("xyd", 16, 0, 128), ("xyd", 16, 128, 128), ("xyd", 17, 0, 128), ("yxd", 17, 128, 128),
]
PROGRAM = [
    ("c", 0, 0), (0, 0), ("c", 0, 1), (1, 0), ("c", 0, 2), (2, 0), ("c", 0, 3), (3, 0), ("c", 0, 4), ("c", 0, 5),
    (5, 0), ("c", 0, 6), (4, 0), ("c", 0, 8), ("c", 0, 10), ("c", 0, 12), ("c", 0, 14), ("c", 0, 16), ("c", 0, 18),
    (1, 1), (2, 1), ("c", 0, 7), (6, 0), ("c", 0, 9), (7, 0), ("c", 0, 11), ("c", 0, 13), (8, 0), ("c", 0, 15),
    ("c", 0, 17), ("c", 0, 19), (3, 1), (0, 1), (5, 1), ("c", 0, 20), ("c", 0, 21), (2, 2), ("c", 0, 22), (1, 2),
    (11, 0), (9, 0), (4, 1), ("c", 0, 23), ("c", 0, 24), ("c", 0, 25), ("c", 0, 26), (6, 1), (7, 1), (0, 2), (12, 0),
    ("c", 0, 27), ("c", 0, 28), ("c", 0, 29), (3, 2), (5, 2), (13, 0), (10, 0), ("c", 0, 30), ("c", 0, 33), (8, 1),
    ("c", 0, 31), (11, 1), (1, 3), (9, 1), ("c", 0, 32), ("c", 0, 34), (2, 3), (6, 2), (0, 3), (7, 2), (15, 0),
    (14, 0), (4, 2), (12, 1), (1, 4), (13, 1), (10, 1), (8, 2), (3, 3), (4, 3), (9, 2), (1, 5), (5, 3), ("f", 0, 0),
    (11, 2), (6, 3), (12, 2), (16, 0), (19, 0), (3, 4), (7, 3), (15, 1), (5, 4), (14, 1), (9, 3), (12, 3), (6, 4),
    (3, 5), (10, 2), (5, 5), (7, 4), (8, 3), (17, 0), (11, 3), (6, 5), (13, 2), (9, 4), (4, 4), (7, 5), (10, 3),
    (11, 4), (9, 5), (18, 0), (16, 1), (19, 1), ("f", 0, 1), (13, 3), (11, 5), (10, 4), (15, 2), (10, 5), (14, 2),
    (13, 4), (12, 4), (17, 1), (16, 2), (4, 5), (15, 3), (17, 2), (18, 1), (14, 3), (19, 2), (13, 5), (12, 5),
    (18, 2), (16, 3), (17, 3), (19, 3), (18, 3),
]


INV_SQRT_2PI = 0.3989422804014327


class SmallSum:
    def __init__(self, place, value, land, send, recv):
        self.p, self.value, self.land, self.send, self.recv = place, value, land, send, recv

    def _copies(self, step):
        p = self.p
        if step == 0:
            mine = p.y * 2 + p.x
            others = [p.at(x=1 - p.x), p.at(y=1 - p.y), p.at(x=1 - p.x, y=1 - p.y)]
        else:
            mine = p.z
            others = [p.at(z=lax.rem(p.z + j, NZ)) for j in (1, 2, 3)]
        return mine, [pltpu.make_async_remote_copy(
            src_ref=self.value.at[step], dst_ref=self.land.at[step, mine], send_sem=self.send.at[step],
            recv_sem=self.recv.at[step], device_id=to, device_id_type=MESH) for to in others]

    def start(self, step):
        mine, copies = self._copies(step)
        self.land[step, mine] = self.value[step]
        for copy in copies:
            copy.start()

    def _three(self, step):
        return self.land.at[step, pl.ds(0, 3)]

    def take(self, step):
        pltpu.make_async_copy(self._three(step), self._three(step), self.recv.at[step]).wait()
        land = self.land
        self.value[step + 1] = (land[step, 0] + land[step, 1]) + (land[step, 2] + land[step, 3])

    def drain(self):
        for step in range(2):
            pltpu.make_async_copy(self._three(step), self._three(step), self.send.at[step]).wait()


def gelu_slope(u):
    return 0.5 * (1.0 + lax.erf(u * SQRT_HALF)) + u * (INV_SQRT_2PI * jnp.exp(-0.5 * u * u))


def step_kernel(scatter, pieces, program, *refs):
    (bucket_h, lens_h, tokens_h), rest = refs[:3], refs[3:]
    th, rest = rest[:6], rest[6:]
    sh, rest = rest[:6], rest[6:]
    tb, rest = rest[:9], rest[9:]
    sb, rest = rest[:9], rest[9:]
    (out_h, grad_in_h, wide, small_out, q_h, k_h, v_h, ctx_h), rest = rest[:8], rest[8:]
    (tok, w1, w2, f, h1, dm, dz, n1, r1, own, land, vecs, value, vland,
     vsem, wsem, osem, ssem, rsem, bsem, vsend, vrecv, gsem, bucket, lens, *ring_refs) = rest
    p = Place()
    dp, head = p.dp, p.head
    d, fw = w1.shape
    hw = q_h.shape[2]
    ready = greet(p, scatter)

    def copy(src, dst, sem):
        item = pltpu.make_async_copy(src, dst, sem)
        item.start()
        return item

    vectors = [copy(src, vecs.at[i, 0, pl.ds(0, src.shape[0])], vsem.at[0]) for i, src in enumerate((*tb, *sb))]
    tb, sb = ([vecs.at[base + i, :, pl.ds(0, src.shape[0])] for i, src in enumerate(group)]
              for base, group in ((0, tb), (9, sb)))

    def swap(slot, src, part):
        rows = pl.ds(part * PART, PART)
        return pltpu.make_async_remote_copy(
            src_ref=src.at[rows], dst_ref=land.at[slot, rows], send_sem=ssem.at[slot, part], recv_sem=rsem.at[slot, part],
            device_id=(dp, 1 - head), device_id_type=MESH)

    def swap_start(slot, src):
        for part in range(2):
            swap(slot, src, part).start()

    def swap_wait(slot, src):
        for part in range(2):
            swap(slot, src, part).wait()

    def both(body):
        def step(b, carry):
            body(b)
            return carry
        lax.fori_loop(0, 2, step, 0)

    def forward_part(wqkv, wo, q, k, v, ctx, target, bias):
        own2 = dz
        def attend_weights(src):
            return [copy(src[j], wqkv.at[:, pl.ds(j * hw, hw)], wsem.at[1 + j]) for j in range(3)] + [copy(src[3], wo, wsem.at[4])]

        def feed_weights(src):
            return [copy(src[4], w1, wsem.at[5]), copy(src[5], w2, wsem.at[6])]

        def wait(items):
            for item in items:
                item.wait()
        layout_in = [copy(bucket_h, bucket, wsem.at[7]), copy(lens_h, lens, wsem.at[8])]
        tokens_in = [copy(tokens_h.at[0], tok.at[0], wsem.at[0])]
        attend_in = attend_weights(th)
        tokens_in.append(copy(tokens_h.at[1], tok.at[1], wsem.at[9]))
        wait(layout_in)
        fill_masks(bucket, lens, bias)
        value[...] = jnp.zeros_like(value)

        def attend(b, vectors):
            mixed = nn(tok[b], wqkv[...])
            q[b] = ((mixed[:, 0:hw] + vectors[0][...]).astype(BF16).astype(F32) * (1.0 / 8.0)).astype(BF16)
            k[b] = mixed[:, hw:2 * hw].astype(BF16)
            v[b] = (mixed[:, 2 * hw:3 * hw] + vectors[1][...]).astype(BF16)
            attention(q.at[b], k.at[b], v.at[b], bias.at[b], ctx.at[b])
            own[b] = nn(ctx[b], wo[...])

        def feed(b, part, vectors):
            rows = pl.ds(part * PART, PART)
            for j in range(fw // CW):
                cols = pl.ds(j * CW, CW)
                u = nn(h1[b, rows, :], w1[:, cols]) + vectors[5][:, cols]
                f[b, rows, cols] = (0.5 * u * (1.0 + lax.erf(u * SQRT_HALF))).astype(BF16)
            own2[b, rows, :] = nn(f[b, rows, :], w2[...])

        def first_sum(b, rows, vectors):
            return tok[b, rows, :].astype(F32) + ((own[b, rows, :] + land[b, rows, :]) + vectors[2][...])

        def second_sum(b, rows, vectors, residual):
            return residual + ((own2[b, rows, :] + land[2 + b, rows, :]) + vectors[6][...])

        def teach_attend(b):
            @pl.when(b == 1)
            def _():
                wait(tokens_in[1:])
            attend(b, tb)
            swap_start(b, own.at[b])

        def teach_feed(b):
            swap_wait(b, own.at[b])

            def norm(rows):
                n, _ = standardize(first_sum(b, rows, tb))
                h = n * tb[3][...] + tb[4][...]
                target[b, rows, :] = h
                h1[b, rows, :] = h.astype(BF16)
            tiles(SPAN, norm)
            for part in range(2):
                feed(b, part, tb)
                swap(2 + b, own2.at[b], part).start()

        def study_attend(b):
            swap_wait(2 + b, own2.at[b])

            def norm(rows):
                n, _ = standardize(second_sum(b, rows, tb, target[b, rows, :]))
                target[b, rows, :] = n * tb[7][...] + tb[8][...]
            tiles(SPAN, norm)
            attend(b, sb)
            swap_start(b, own.at[b])

        def study_feed(b):
            @pl.when(b == 0)
            def _():
                swap_wait(0, own.at[0])

            def norm(rows):
                n, r = standardize(first_sum(b, rows, sb))
                n1[b, rows, :] = n
                slots = b * SPAN + rows.start + lax.broadcasted_iota(jnp.int32, (TILE, 1), 0)
                real = jnp.where(row_layout(bucket[0], lens, slots)[1], 1.0, 0.0)
                r1[b, rows, :] = jnp.where(lane_half(), r, real)
                h1[b, rows, :] = (n * sb[3][...] + sb[4][...]).astype(BF16)
            tiles(SPAN, norm)
            feed(b, 0, sb)

            @pl.when(b == 1)
            def _():
                swap(2 + b, own2.at[b], 0).start()
            feed(b, 1, sb)

            @pl.when(b == 0)
            def _():
                swap_wait(1, own.at[1])
                swap(2 + b, own2.at[b], 0).start()
            swap(2 + b, own2.at[b], 1).start()

        def study_end(b):
            total = [jnp.zeros((1, d), F32)] * 3

            def norm(rows):
                residual = n1[b, rows, :] * sb[3][...] + sb[4][...]
                n2, r2 = standardize(second_sum(b, rows, sb, residual))
                result = n2 * sb[7][...] + sb[8][...]
                dy = (result - target[b, rows, :]) * r1[b, rows, HEAD_DIM:HEAD_DIM + 1]
                own[b, rows, :] = result
                scaled = dy * sb[7][...]
                out = r2 * (scaled - jnp.mean(scaled, axis=-1, keepdims=True) - n2 * jnp.mean(scaled * n2, axis=-1, keepdims=True))
                dz[b, rows, :] = out
                low = out.astype(BF16)
                dm[b, rows, :] = low
                for i, item in enumerate((low.astype(F32), dy * n2, dy)):
                    total[i] = total[i] + jnp.sum(item, axis=0, keepdims=True)
            for part in range(2):
                swap(2 + b, own2.at[b], part).wait()
                tiles(PART, norm, part * PART)
            for i in range(3):
                value[0, 3 + i:4 + i, 0:d] += total[i]

        all_vectors = vecs.at[:, 0, pl.ds(0, d)]
        pltpu.make_async_copy(all_vectors, all_vectors, vsem.at[0]).wait()
        wait(tokens_in[:1] + attend_in)
        feed_in = feed_weights(th)
        ready()
        both(teach_attend)
        attend_in = attend_weights(sh)
        wait(feed_in)
        both(teach_feed)
        feed_in = feed_weights(sh)
        wait(attend_in)
        both(study_attend)
        spills = [copy(src, dst, osem.at[i]) for i, (src, dst) in enumerate(((q, q_h), (k, k_h), (v, v_h), (ctx, ctx_h)))]
        wait(feed_in)
        both(study_feed)
        both(study_end)
        copy(own, out_h, osem.at[4])
        wait(spills)
    return_out = pltpu.make_async_copy(own, out_h, osem.at[4])

    def V(*shape, dtype=F32):
        return pltpu.VMEM(shape, dtype)
    pl.run_scoped(forward_part, V(d, 3 * hw, dtype=BF16), V(hw, d, dtype=BF16), *[V(2, SPAN, hw, dtype=BF16)] * 4,
                  V(2, SPAN, d), V(2, SPAN, SPAN))

    def backward_part(grad):
        ring = Ring(p, pieces, grad, *ring_refs) if scatter else None
        fly = SmallSum(p, value, vland, vsend, vrecv) if scatter else None
        all_cols = pl.ds(0, CW)
        compute, got = {}, {}

        def put(c, cols, block):
            for i in range(NZ * NY * NX):
                grad[c, i // 4, i // 2 % 2, i % 2, :, cols] = block[i * ROWS:(i + 1) * ROWS]

        def return_grad(c):
            cols = pl.ds(c * CW, CW)
            put(c, all_cols, tn(dm[...].reshape(-1, d), f[:, :, cols].reshape(-1, CW)))

        def slope(j):
            cols = pl.ds(j * CW, CW)

            def half(b, total):
                u = nn(h1[b], w1[:, cols]) + sb[5][:, cols]
                g = nt(dm[b], w2[cols, :])
                du = (g * gelu_slope(u)).astype(BF16)
                f[b, :, cols] = du
                return total + jnp.sum(du.astype(F32), axis=0, keepdims=True)
            total = lax.fori_loop(0, 2, half, jnp.zeros((1, CW), F32))
            value[0, 6 + j // 3:7 + j // 3, pl.ds(j % 3 * CW, CW)] = total

        def hidden_grad(j):
            cols = pl.ds(j * CW, CW)
            put(6 + j, all_cols, tn(h1[...].reshape(-1, d), f[:, :, cols].reshape(-1, CW)))

        def back_first():
            return_out.wait()

            def half(b):
                own[b] = nt(f[b], w1[...])
                swap_start(b, own.at[b])
            both(half)
            fetch(("wo", sh[3], wo), ("wq", sh[0], wqkv.at[:, pl.ds(0, hw)]), ("wk", sh[1], wqkv.at[:, pl.ds(hw, hw)]),
                  ("wv", sh[2], wqkv.at[:, pl.ds(2 * hw, hw)]))

        def fetch(*items):
            for name, src, dst in items:
                got[name] = copy(src, dst, bsem.at[len(got)])
        q, k, v, ctx = (f.at[:, :, pl.ds(i * hw, hw)] for i in range(4))
        dctx = h1.at[:, :, pl.ds(0, hw)]
        do = dm
        wqkv = w1.at[:, pl.ds(0, 3 * hw)]
        wo = w2.at[pl.ds(0, hw)]
        bias = n1.at[:, :, pl.ds(0, SPAN)]

        def norm_back():
            fetch(("q", q_h, q), ("k", k_h, k), ("v", v_h, v), ("ctx", ctx_h, ctx))

            def half(b):
                swap_wait(b, own.at[b])
                total = [jnp.zeros((1, d), F32)] * 3

                def tile(rows):
                    up = dz[b, rows, :] + (own[b, rows, :] + land[b, rows, :])
                    n = n1[b, rows, :]
                    scaled = up * sb[3][...]
                    out = r1[b, rows, 0:1] * (scaled - jnp.mean(scaled, axis=-1, keepdims=True)
                                              - n * jnp.mean(scaled * n, axis=-1, keepdims=True))
                    dz[b, rows, :] = out
                    low = out.astype(BF16)
                    do[b, rows, :] = low
                    for i, item in enumerate((low.astype(F32), up * n, up)):
                        total[i] = total[i] + jnp.sum(item, axis=0, keepdims=True)
                tiles(SPAN, tile)
                for i in range(3):
                    value[0, i:i + 1, 0:d] += total[i]
            both(half)
            fill_masks(bucket, lens, bias)

        def context_grad():
            got["wo"].wait()

            def half(b):
                dctx[b] = nt(do[b], wo[...]).astype(BF16)
            both(half)
            for name in ("q", "k", "v", "ctx"):
                got[name].wait()

        def attend_back(pair, b):
            low_side = lane_half()
            cols = pl.ds(pair * 128, 128)
            q2, k2, v2, dc2 = q[b, :, cols], k[b, :, cols], v[b, :, cols], dctx[b, :, cols]
            parts = []
            for side in (low_side, ~low_side):
                zero = jnp.zeros_like(q2)
                s = nt(jnp.where(side, q2, zero), k2) + bias[b]
                e = jnp.exp(s - jnp.max(s, axis=1, keepdims=True))
                probs = e * (1.0 / jnp.sum(e, axis=1, keepdims=True))
                dprob = nt(jnp.where(side, dc2, zero), v2)
                ds = (probs * (dprob - jnp.sum(probs * dprob, axis=1, keepdims=True))).astype(BF16)
                parts.append((nn(ds, k2), tn(ds, q2), tn(probs.astype(BF16), dc2)))
            dq = (jnp.where(low_side, parts[0][0], parts[1][0]) * (1.0 / 8.0)).astype(BF16)
            dk = jnp.where(low_side, parts[0][1], parts[1][1]).astype(BF16)
            dv = jnp.where(low_side, parts[0][2], parts[1][2]).astype(BF16)
            q[b, :, cols], k[b, :, cols], v[b, :, cols] = dq, dk, dv
            extra = pl.ds(d, 128)
            value[0, pair:pair + 1, extra] += jnp.sum(dq.astype(F32), axis=0, keepdims=True)
            value[0, 3 + pair:4 + pair, extra] += jnp.sum(dv.astype(F32), axis=0, keepdims=True)

        def attend_grad(pair, second):
            cols = pl.ds(pair * 128, 128)
            a = tok[...].reshape(-1, d)
            c = 12 + 2 * pair + second
            if second:
                put(c, pl.ds(0, 128), tn(a, k[:, :, cols].reshape(-1, 128)))
                put(c, pl.ds(128, 128), tn(a, v[:, :, cols].reshape(-1, 128)))
            else:
                put(c, pl.ds(0, 128), tn(do[...].reshape(-1, d), ctx[:, :, cols].reshape(-1, 128)))
                put(c, pl.ds(128, 128), tn(a, q[:, :, cols].reshape(-1, 128)))

        def back_in():
            for name in ("wq", "wk", "wv"):
                got[name].wait()

            def half(b):
                own[b] = (nt(q[b], wqkv[:, 0:hw]) + nt(k[b], wqkv[:, hw:2 * hw])) + nt(v[b], wqkv[:, 2 * hw:3 * hw])
                swap_start(2 + b, own.at[b])
            both(half)
            if scatter:
                fly.start(0)

        def finish_in():
            def half(b):
                swap_wait(2 + b, own.at[b])

                def tile(rows):
                    dz[b, rows, :] += own[b, rows, :] + land[2 + b, rows, :]
                tiles(SPAN, tile)
            both(half)
            copy(dz, grad_in_h, osem.at[5])

        for c in range(6):
            compute[c] = functools.partial(return_grad, c)
            compute[6 + 2 * c] = functools.partial(slope, c)
            compute[7 + 2 * c] = functools.partial(hidden_grad, c)
        compute[18], compute[19], compute[20], compute[33], compute[34] = back_first, norm_back, context_grad, back_in, finish_in
        for pair in range(3):
            compute[21 + 4 * pair] = functools.partial(attend_back, pair, 0)
            compute[22 + 4 * pair] = functools.partial(attend_back, pair, 1)
            compute[23 + 4 * pair] = functools.partial(attend_grad, pair, 0)
            compute[24 + 4 * pair] = functools.partial(attend_grad, pair, 1)

        def owned(c):
            mine, cols = ring.own(c)
            return pltpu.make_async_copy(mine, wide.at[:, cols], gsem.at[0])

        for item in program:
            if item[0] == "c":
                compute[item[2]]()
            elif scatter and item[0] == "f":
                fly.take(item[2])
                if item[2] == 0:
                    fly.start(1)
            elif scatter and ring.stage(*item):
                owned(item[0]).start()
        if scatter:
            small_out[...] = value[2]
            for c in range(len(pieces)):
                ring.drain(c)
            pltpu.make_async_copy(wide, wide, gsem.at[0]).wait()
            fly.drain()
        else:
            rows = copy(grad, wide, osem.at[6])
            small_out[...] = value[0]
            rows.wait()
        pltpu.make_async_copy(dz, grad_in_h, osem.at[5]).wait()

    count = (2 * fw + 4 * hw) // CW
    pl.run_scoped(backward_part, V(count, NZ, NY, NX, ROWS, CW))


def distill(scatter, tokens, bucket, lens, teacher, student):
    def cut(layer):
        wq, bq, wk, wv, bv, wo, bo, g1, s1, w1, b1, w2, b2, g2, s2 = layer
        return [wq, wk, wv, wo, w1, w2], [bq, bv, bo, g1, s1, b1, b2, g2, s2]
    tw, tv = cut(teacher)
    sw, sv = cut(student)
    toks, d = tokens.shape
    hw, fw = tw[0].shape[1], tw[4].shape[1]
    count = (2 * fw + 4 * hw) // CW
    halves, b = toks // SPAN, BF16
    pieces, program = PIECES, PROGRAM
    hbm, vmem = (pl.BlockSpec(memory_space=m) for m in (pl.ANY, pltpu.VMEM))
    def S(*shape, dtype=F32):
        return jax.ShapeDtypeStruct(shape, dtype)
    def V(*shape, dtype=F32):
        return pltpu.VMEM(shape, dtype)
    dma = pltpu.SemaphoreType.DMA
    wide = S(ROWS, count * CW) if scatter else S(count, NZ, NY, NX, ROWS, CW)
    outs = (S(halves, SPAN, d), S(halves, SPAN, d), wide, S(8, 896)) + (S(halves, SPAN, hw, dtype=b),) * 4
    return pl.pallas_call(
        functools.partial(step_kernel, scatter, pieces, program),
        out_shape=outs,
        in_specs=[hbm] * 33,
        out_specs=(hbm, hbm, hbm, vmem) + (hbm,) * 4,
        scratch_shapes=[
            V(halves, SPAN, d, dtype=b), V(d, fw, dtype=b), V(fw, d, dtype=b), V(halves, SPAN, fw, dtype=b), V(halves, SPAN, d, dtype=b),
            V(halves, SPAN, d, dtype=b), V(halves, SPAN, d), V(halves, SPAN, d), V(halves, SPAN, 128), V(2, SPAN, d), V(4, SPAN, d),
            V(18, 1, fw), V(3, 8, 896), V(2, 4, 8, 896),
            dma((1,)), dma((10,)), dma((7,)), dma((4, 2)), dma((4, 2)), dma((8,)), dma((2,)), dma((2,)), dma((1,)),
            pltpu.SMEM((1,), jnp.int32), pltpu.SMEM((1, 8), jnp.int32)]
        + (ring_scratch(pieces) if scatter else []),
        compiler_params=pltpu.CompilerParams(collective_id=1, has_side_effects=True, vmem_limit_bytes=VMEM_BYTES),
    )(bucket, lens, tokens.reshape(halves, SPAN, d), *tw, *sw, *tv, *sv)[:4]


def finish_kernel(out_h, gin_h, wide_h, small_h, out, gin, gq, gk, gv, go, g1w, g2w, *rest):
    small_outs, (wide, small, stage, sem_in, sem_out) = rest[:9], rest[9:]
    d = out.shape[2]
    fw, hw = g1w.shape[1], gq.shape[1]
    count = [0]

    def copy(src, dst):
        count[0] += 1
        return pltpu.make_async_copy(src, dst, sem_out.at[count[0] - 1])

    loads, stores = [(small_h, small), (wide_h, wide)], [[], []]
    for dst, row in zip((small_outs[i] for i in (2, 3, 4, 6, 7, 8)), range(6)):
        stores[0].append(copy(small.at[row, pl.ds(0, d)], dst))
    for half in range(2):
        stores[0].append(copy(small.at[6 + half, pl.ds(0, d)], small_outs[5].at[pl.ds(half * d, d)]))
    for pair in range(hw // 128):
        at, extra = pl.ds(pair * 128, 128), pl.ds(d, 128)
        stores[0].append(copy(small.at[pair, extra], small_outs[0].at[at]))
        stores[0].append(copy(small.at[3 + pair, extra], small_outs[1].at[at]))
        for i, dst in enumerate((go, gq, gk, gv)):
            stores[1].append(copy(wide.at[:, pl.ds(2 * fw + pair * 512 + i * 128, 128)], dst.at[:, at]))
    stores[1].append(copy(wide.at[:, pl.ds(0, fw)], g2w))
    stores[1].append(copy(wide.at[:, pl.ds(fw, fw)], g1w))
    for src, dst in ((out_h, out), (gin_h, gin)):
        for b in range(2):
            for rows in (pl.ds(0, SPAN // 2), pl.ds(SPAN // 2, SPAN // 2)):
                place = stage.at[len(loads) - 2]
                loads.append((src.at[b, rows], place))
                stores.append([copy(place, dst.at[b, rows])])
    loads = [pltpu.make_async_copy(src, dst, sem_in.at[i]) for i, (src, dst) in enumerate(loads)]
    for item in loads:
        item.start()
    for load, group in zip(loads, stores):
        load.wait()
        for item in group:
            item.start()
    for group in stores:
        for item in group:
            item.wait()


def finish(out_raw, gin_raw, wide, small, hw, fw):
    d = out_raw.shape[2]
    def S(*shape):
        return jax.ShapeDtypeStruct(shape, F32)
    hbm = pl.BlockSpec(memory_space=pl.ANY)
    return pl.pallas_call(
        finish_kernel,
        out_shape=(S(*out_raw.shape), S(*gin_raw.shape), S(ROWS, hw), S(ROWS, hw), S(ROWS, hw), S(ROWS, hw), S(ROWS, fw), S(ROWS, fw),
                   S(hw), S(hw), S(d), S(d), S(d), S(fw), S(d), S(d), S(d)),
        in_specs=[hbm] * 4,
        out_specs=(hbm,) * 17,
        scratch_shapes=[pltpu.VMEM(wide.shape, F32), pltpu.VMEM(small.shape, F32), pltpu.VMEM((8, SPAN // 2, d), F32),
                        pltpu.SemaphoreType.DMA((10,)), pltpu.SemaphoreType.DMA((48,))],
        compiler_params=pltpu.CompilerParams(vmem_limit_bytes=VMEM_BYTES),
    )(out_raw, gin_raw, wide, small)


def shards(*args):
    tokens, row_bucket, row_lengths = args[:3]
    teacher, student = args[3:18], args[18:33]
    d = tokens.shape[1]
    hw, fw = student[0].shape[1], student[9].shape[1]
    scatter = lax.axis_size("dp") == NZ * NY * NX
    out, *got = distill(scatter, tokens, row_bucket, row_lengths, teacher, student)
    if scatter:
        out, grad_in, gq, gk, gv, go, g1, g2, qb, vb, ob, g1g, s1g, b1g, b2g, g2g, s2g = finish(out, *got, hw, fw)
    else:
        grad_in, wide, small = got
        rows = wide.reshape(wide.shape[0], d, CW)
        steps = fw // CW
        last = [2 * steps + i for i in range(2 * hw // 128)]
        first, second = ([rows[c] for c in last[i::2]] for i in (0, 1))
        mats = [
            jnp.concatenate([m[:, 128:] for m in first], axis=1),
            jnp.concatenate([m[:, :128] for m in second], axis=1),
            jnp.concatenate([m[:, 128:] for m in second], axis=1),
            jnp.concatenate([m[:, :128] for m in first], axis=1),
            jnp.concatenate([rows[c] for c in range(steps, 2 * steps)], axis=1),
            jnp.concatenate([rows[c] for c in range(steps)], axis=1),
        ]
        gq, gk, gv, go, g1, g2 = (lax.psum_scatter(m, "dp", scatter_dimension=0, tiled=True) for m in mats)
        small = lax.psum(small, "dp")
        qb, vb = small[0:3, d:].reshape(-1), small[3:6, d:].reshape(-1)
        ob, g1g, s1g, b2g, g2g, s2g = (small[i, :d] for i in range(6))
        b1g = small[6:8, :d].reshape(-1)
    toks = tokens.shape[0]
    return (
        out.reshape(toks, d), grad_in.reshape(toks, d), gq, qb, gk, gv, vb, go.T, ob, g1g, s1g, g1, b1g, g2.T, b2g, g2g, s2g
    )


def solution(mesh):
    placed = (
        P("dp", None),
        P("dp"),
        P("dp", None),
        P(None, "head"),
        P("head"),
        P(None, "head"),
        P(None, "head"),
        P("head"),
        P("head", None),
        P(),
        P(),
        P(),
        P(None, "head"),
        P("head"),
        P("head", None),
        P(),
        P(),
        P(),
        P(None, "head"),
        P("head"),
        P(None, "head"),
        P(None, "head"),
        P("head"),
        P("head", None),
        P(),
        P(),
        P(),
        P(None, "head"),
        P("head"),
        P("head", None),
        P(),
        P(),
        P(),
    )
    return jax.shard_map(
        shards,
        mesh=mesh,
        in_specs=placed,
        out_specs=(
            P("dp", None),
            P("dp", None),
            P("dp", "head"),
            P("head"),
            P("dp", "head"),
            P("dp", "head"),
            P("head"),
            P("head", "dp"),
            P(),
            P(),
            P(),
            P("dp", "head"),
            P("head"),
            P("head", "dp"),
            P(),
            P(),
            P(),
        ),
        check_vma=False,
    )
```

```python
import functools

import jax
import jax.numpy as jnp
from jax import lax
from jax.experimental import pallas as pl
from jax.experimental.pallas import tpu as pltpu
from jax.sharding import PartitionSpec as P

MESH = pl.DeviceIdType.MESH
HEAD_DIM = 64
SPAN = 512
NORM_EPS = 1e-12
SQRT_HALF = 0.7071067811865476
F32, BF16 = jnp.float32, jnp.bfloat16
VMEM_BYTES = 63 * 2**20 + 2**19


def nn(a, b):
    return jnp.dot(a, b, preferred_element_type=F32)


def nt(a, b):
    return lax.dot_general(a, b, (((1,), (1,)), ((), ())), preferred_element_type=F32)


def tn(a, b):
    return lax.dot_general(a, b, (((0,), (0,)), ((), ())), preferred_element_type=F32)


def row_layout(bucket, lens, slots):
    shift = jnp.where(bucket == 0, SPAN // 4, jnp.where(bucket == 1, SPAN // 2, SPAN))
    row = jnp.where(bucket == 0, slots // (SPAN // 4), jnp.where(bucket == 1, slots // (SPAN // 2), slots // SPAN))
    length = jnp.zeros_like(slots)
    for j in range(8):
        length = jnp.where(row == j, lens[0, j], length)
    return row, (slots - row * shift) < length


def fill_masks(bucket, lens, bias):
    code = bucket[0]
    for b in range(bias.shape[0]):
        q = b * SPAN + lax.broadcasted_iota(jnp.int32, (SPAN, 1), 0)
        k = b * SPAN + lax.broadcasted_iota(jnp.int32, (1, SPAN), 1)
        q_row, _ = row_layout(code, lens, q)
        k_row, k_ok = row_layout(code, lens, k)
        bias[b] = jnp.where(q_row == jnp.where(k_ok, k_row, -1), 0.0, -1000000000.0)


def lane_half():
    return lax.broadcasted_iota(jnp.int32, (1, 128), 1) < HEAD_DIM


def attention(q, k, v, bias, ctx):
    low = lane_half()
    for pair in range(q.shape[1] // 128):
        cols = pl.ds(pair * 128, 128)
        q2, k2, v2 = q[:, cols], k[:, cols], v[:, cols]
        parts = []
        for side in (low, ~low):
            s = nt(jnp.where(side, q2, jnp.zeros_like(q2)), k2) + bias[...]
            e = jnp.exp(s - jnp.max(s, axis=1, keepdims=True))
            mass = jnp.sum(e, axis=1, keepdims=True)
            parts.append(nn(e.astype(BF16), v2) * (1.0 / mass))
        ctx[:, cols] = jnp.where(low, parts[0], parts[1]).astype(BF16)


def standardize(z):
    centred = z - jnp.mean(z, axis=-1, keepdims=True)
    inv = lax.rsqrt(jnp.mean(centred * centred, axis=-1, keepdims=True) + NORM_EPS)
    return centred * inv, inv


TILE = 128
PART = SPAN // 2


def tiles(rows, body, first=0):
    for i in range(rows // TILE):
        body(pl.ds(first + i * TILE, TILE))


CW = 256
NZ, NY, NX = 4, 2, 2
ROWS = 48


class Place:
    def __init__(self):
        self.dp = lax.axis_index("dp")
        self.head = lax.axis_index("head")
        self.z = self.dp // 4
        self.y = lax.rem(self.dp // 2, 2)
        self.x = lax.rem(self.dp, 2)

    def at(self, z=None, y=None, x=None):
        z, y, x = (mine if given is None else given for given, mine in ((z, self.z), (y, self.y), (x, self.x)))
        return (z * 4 + y * 2 + x, self.head)


def landing(pieces):
    places, used = [], {False: [], True: []}
    for kind, _, _, width in pieces:
        taken = used[kind[0] in "zd"]
        i = next((i for i, cols in enumerate(taken) if cols + width <= CW), len(taken))
        taken[i:i + 1] = [(taken[i] if i < len(taken) else 0) + width]
        places.append((i, taken[i] - width))
    return places, len(used[False]), len(used[True])


class Ring:
    def __init__(self, place, pieces, grad, pair_a, pair_b, path, zpath, zpair_a, zpair_b, send, recv):
        self.p, self.pieces, self.grad = place, pieces, grad
        self.lands = (pair_a, pair_b, path), (zpair_a, zpair_b, zpath)
        self.send, self.recv = send, recv
        self.places = landing(pieces)[0]

    def _refs(self, c, which):
        kind, chunk, col, width = self.pieces[c]
        deep = kind[0] in "zd"
        i, land_col = self.places[c]
        land = self.lands[deep][which]
        every = (slice(None),) * (len(land.shape) - 2)
        return deep, self.grad.at[chunk, :, :, :, :, pl.ds(col, width)], land.at[(i, *every, pl.ds(land_col, width))]

    def _pair(self, c, step):
        p = self.p
        deep, g, land = self._refs(c, step)
        axis = [a for a in self.pieces[c][0] if a in "xy"][step]
        if deep:
            view = g.at[p.z]
            if step == 0:
                pick = (lambda j: view.at[:, j]) if axis == "x" else (lambda j: view.at[j])
            else:
                pick = (lambda j: view.at[p.y, j]) if axis == "x" else (lambda j: view.at[j, p.x])
        elif step == 0:
            pick = (lambda j: g.at[:, :, j]) if axis == "x" else (lambda j: g.at[:, j])
        else:
            pick = (lambda j: g.at[:, p.y, j]) if axis == "x" else (lambda j: g.at[:, j, p.x])
        mine = p.x if axis == "x" else p.y
        to = p.at(x=1 - p.x) if axis == "x" else p.at(y=1 - p.y)
        copy = pltpu.make_async_remote_copy(
            src_ref=pick(1 - mine), dst_ref=land, send_sem=self.send.at[c], recv_sem=self.recv.at[c, step],
            device_id=to, device_id_type=MESH)
        return copy, pick(mine), land

    def pair_send(self, c, step):
        self._pair(c, step)[0].start()

    def pair_take(self, c, step):
        copy, mine, land = self._pair(c, step)
        copy.wait_recv()
        mine[...] += land[...]

    def _path_refs(self, c):
        p = self.p
        deep, g, land = self._refs(c, 2)
        if deep:
            return (lambda lo, n: g.at[pl.ds(lo, n)]), land
        return (lambda lo, n: g.at[pl.ds(lo, n), p.y, p.x]), land

    def _hop(self, c, z, up):
        blocks, land = self._path_refs(c)
        if up:
            src, dst, k, to = blocks(z + 1, 3 - z), land.at[pl.ds(0, 3 - z)], 2, self.p.z + 1
        else:
            src, dst, k, to = blocks(0, z), land.at[pl.ds(5 - z, z)], 3, self.p.z - 1
        return pltpu.make_async_remote_copy(
            src_ref=src, dst_ref=dst, send_sem=self.send.at[c], recv_sem=self.recv.at[c, k],
            device_id=self.p.at(z=to), device_id_type=MESH)

    def path_start(self, c):
        @pl.when(self.p.z == 0)
        def _():
            self._hop(c, 0, True).start()

        @pl.when(self.p.z == 3)
        def _():
            self._hop(c, 3, False).start()

    def path_mid(self, c, first):
        blocks, land = self._path_refs(c)
        for z in (1, 2):
            up = (z == 1) == first

            @pl.when(self.p.z == z)
            def _(z=z, up=up):
                if up:
                    self._hop(c, z - 1, True).wait_recv()
                    own = blocks(z + 1, 3 - z)
                    own[...] += land[pl.ds(1, 3 - z)]
                    self._hop(c, z, True).start()
                else:
                    self._hop(c, z + 1, False).wait_recv()
                    own = blocks(0, z)
                    own[...] += land[pl.ds(4 - z, z)]
                    self._hop(c, z, False).start()

    def path_end(self, c):
        blocks, land = self._path_refs(c)
        for z in range(NZ):
            @pl.when(self.p.z == z)
            def _(z=z):
                if z == 0:
                    self._hop(c, 1, False).wait_recv()
                if z == 3:
                    self._hop(c, 2, True).wait_recv()
                own = blocks(z, 1)
                total = own[...]
                if z > 0:
                    total = total + land[pl.ds(0, 1)]
                if z < 3:
                    total = total + land[pl.ds(4, 1)]
                own[...] = total

    def _direct(self, c, j):
        blocks, land = self._path_refs(c)
        to = lax.rem(self.p.z + j, NZ)
        return pltpu.make_async_remote_copy(
            src_ref=blocks(to, 1), dst_ref=land.at[pl.ds(j - 1, 1)], send_sem=self.send.at[c], recv_sem=self.recv.at[c, 2],
            device_id=self.p.at(z=to), device_id_type=MESH)

    def direct_send(self, c):
        for j in (1, 2, 3):
            self._direct(c, j).start()

    def direct_take(self, c):
        blocks, land = self._path_refs(c)
        pltpu.make_async_copy(land.at[pl.ds(0, 3)], land.at[pl.ds(0, 3)], self.recv.at[c, 2]).wait()
        own = blocks(self.p.z, 1)
        own[...] += (land[pl.ds(0, 1)] + land[pl.ds(1, 1)]) + land[pl.ds(2, 1)]

    def drain(self, c):
        width = self.pieces[c][3]
        blocks = self.lands[False][2].at[pl.ds(0, 3), :, :, pl.ds(0, width)]
        pltpu.make_async_copy(blocks, blocks, self.send.at[c]).wait()

    def stages(self, c):
        take = lambda step: functools.partial(self.pair_take, c, step)
        send = lambda step: functools.partial(self.pair_send, c, step)
        if "d" in self.pieces[c][0]:
            column = [[functools.partial(self.direct_send, c)], [functools.partial(self.direct_take, c)]]
        else:
            column = [[functools.partial(self.path_start, c)], [functools.partial(self.path_mid, c, True)],
                      [functools.partial(self.path_mid, c, False)], [functools.partial(self.path_end, c)]]
        if self.pieces[c][0][0] in "zd":
            return column[:-1] + [column[-1] + [send(0)], [take(0), send(1)], [take(1)]]
        return [[send(0)], [take(0), send(1)], [take(1)] + column[0]] + column[1:]

    def stage(self, c, s):
        steps = self.stages(c)
        for step in steps[s]:
            step()
        return s == len(steps) - 1

    def own(self, c):
        p = self.p
        _, chunk, col, width = self.pieces[c]
        return self.grad.at[chunk, p.z, p.y, p.x, :, pl.ds(col, width)], pl.ds(chunk * CW + col, width)


def ring_scratch(pieces):
    _, flat, deep = landing(pieces)
    f = jnp.float32
    return [
        pltpu.VMEM((flat, NZ, 2, ROWS, CW), f),
        pltpu.VMEM((flat, NZ, ROWS, CW), f),
        pltpu.VMEM((flat, 5, ROWS, CW), f),
        pltpu.VMEM((deep, 5, NY, NX, ROWS, CW), f),
        pltpu.VMEM((deep, 2, ROWS, CW), f),
        pltpu.VMEM((deep, ROWS, CW), f),
        pltpu.SemaphoreType.DMA((len(pieces),)),
        pltpu.SemaphoreType.DMA((len(pieces), 4)),
    ]


def greet(place, scatter):
    barrier = pltpu.get_barrier_semaphore()
    p = place
    others = [(p.dp, 1 - p.head)]
    if scatter:
        others += [p.at(x=1 - p.x), p.at(y=1 - p.y), p.at(x=1 - p.x, y=1 - p.y)] + [p.at(z=lax.rem(p.z + j, NZ)) for j in (1, 2, 3)]
    for to in others:
        pl.semaphore_signal(barrier, inc=1, device_id=to, device_id_type=MESH)
    return lambda: pl.semaphore_wait(barrier, len(others))


PIECES = [
    ("yx", 0, 0, 128), ("zxy", 0, 128, 128), ("xyd", 1, 0, 256), ("dxy", 2, 0, 256), ("yxd", 3, 0, 256),
    ("yxd", 4, 0, 256), ("xy", 5, 0, 256), ("xy", 6, 0, 256), ("dxy", 7, 0, 256), ("yx", 8, 0, 256),
    ("yx", 9, 0, 256), ("yx", 10, 0, 256), ("zyx", 11, 0, 256), ("xy", 12, 0, 256), ("xy", 13, 0, 256),
    ("zyx", 14, 0, 128), ("xy", 14, 128, 128), ("yx", 15, 0, 128), ("yxd", 15, 128, 128), ("yxd", 16, 0, 128),
    ("xy", 16, 128, 128), ("xyd", 17, 0, 128), ("xyd", 17, 128, 128),
]
PROGRAM = [
    ("c", 0, 0), (0, 0), (1, 0), ("c", 0, 1), (2, 0), ("c", 0, 2), (3, 0), ("c", 0, 3), (4, 0), ("c", 0, 4),
    ("c", 0, 5), (6, 0), ("c", 0, 6), (5, 0), ("c", 0, 8), ("c", 0, 10), (0, 1), ("c", 0, 12), (1, 1), ("c", 0, 14),
    ("c", 0, 16), ("c", 0, 18), (2, 1), ("c", 0, 7), (7, 0), (4, 1), ("c", 0, 9), (8, 0), ("c", 0, 11), (9, 0),
    ("c", 0, 13), ("c", 0, 15), ("c", 0, 17), ("c", 0, 19), (6, 1), ("c", 0, 20), (0, 2), (5, 1), ("c", 0, 21),
    (12, 0), ("c", 0, 22), (3, 1), (2, 2), ("c", 0, 23), (10, 0), ("c", 0, 24), (13, 0), (1, 2), (7, 1), ("c", 0, 25),
    ("c", 0, 26), (4, 2), (0, 3), (9, 1), ("c", 0, 27), ("c", 0, 28), (5, 2), ("c", 0, 29), (6, 2), (3, 2),
    ("c", 0, 30), (11, 0), (14, 0), ("c", 0, 33), ("c", 0, 31), (8, 1), (12, 1), (10, 1), ("c", 0, 32), (13, 1),
    (15, 0), ("c", 0, 34), (7, 2), (2, 3), (3, 3), (9, 2), (1, 3), (17, 0), (0, 4), (4, 3), (16, 0), (6, 3), (18, 0),
    (11, 1), (14, 1), (5, 3), (0, 5), (8, 2), (13, 2), (15, 1), ("f", 0, 0), (20, 0), (10, 2), (1, 4), (7, 3),
    (17, 1), (12, 2), (19, 0), (6, 4), (9, 3), (16, 1), (18, 1), (13, 3), (12, 3), (21, 0), (15, 2), (6, 5), (11, 2),
    (14, 2), (7, 4), (10, 3), (8, 3), (1, 5), (22, 0), (15, 3), (9, 4), (20, 1), (7, 5), (11, 3), (13, 4), (17, 2),
    (9, 5), (19, 1), ("f", 0, 1), (10, 4), (14, 3), (13, 5), (18, 2), (16, 2), (11, 4), (17, 3), (10, 5), (12, 4),
    (14, 4), (15, 4), (21, 1), (16, 3), (20, 2), (18, 3), (17, 4), (11, 5), (16, 4), (21, 2), (14, 5), (22, 1),
    (17, 5), (20, 3), (16, 5), (19, 2), (12, 5), (15, 5), (22, 2), (21, 3), (20, 4), (19, 3), (22, 3), (20, 5),
]


INV_SQRT_2PI = 0.3989422804014327


class SmallSum:
    def __init__(self, place, value, land, send, recv):
        self.p, self.value, self.land, self.send, self.recv = place, value, land, send, recv

    def _copies(self, step):
        p = self.p
        if step == 0:
            mine = p.y * 2 + p.x
            others = [p.at(x=1 - p.x), p.at(y=1 - p.y), p.at(x=1 - p.x, y=1 - p.y)]
        else:
            mine = p.z
            others = [p.at(z=lax.rem(p.z + j, NZ)) for j in (1, 2, 3)]
        return mine, [pltpu.make_async_remote_copy(
            src_ref=self.value.at[step], dst_ref=self.land.at[step, mine], send_sem=self.send.at[step],
            recv_sem=self.recv.at[step], device_id=to, device_id_type=MESH) for to in others]

    def start(self, step):
        mine, copies = self._copies(step)
        self.land[step, mine] = self.value[step]
        for copy in copies:
            copy.start()

    def _three(self, step):
        return self.land.at[step, pl.ds(0, 3)]

    def take(self, step):
        pltpu.make_async_copy(self._three(step), self._three(step), self.recv.at[step]).wait()
        land = self.land
        self.value[step + 1] = (land[step, 0] + land[step, 1]) + (land[step, 2] + land[step, 3])

    def drain(self):
        for step in range(2):
            pltpu.make_async_copy(self._three(step), self._three(step), self.send.at[step]).wait()


def gelu_slope(u):
    return 0.5 * (1.0 + lax.erf(u * SQRT_HALF)) + u * (INV_SQRT_2PI * jnp.exp(-0.5 * u * u))


def step_kernel(scatter, pieces, program, *refs):
    (bucket_h, lens_h, tokens_h), rest = refs[:3], refs[3:]
    th, rest = rest[:6], rest[6:]
    sh, rest = rest[:6], rest[6:]
    tb, rest = rest[:9], rest[9:]
    sb, rest = rest[:9], rest[9:]
    (out_h, grad_in_h, wide, small_out, q_h, k_h, v_h, ctx_h), rest = rest[:8], rest[8:]
    (tok, w1, w2, f, h1, dm, dz, n1, r1, own, land, vecs, value, vland,
     vsem, wsem, osem, ssem, rsem, bsem, vsend, vrecv, gsem, bucket, lens, *ring_refs) = rest
    p = Place()
    dp, head = p.dp, p.head
    d, fw = w1.shape
    hw = q_h.shape[2]
    ready = greet(p, scatter)

    def copy(src, dst, sem):
        item = pltpu.make_async_copy(src, dst, sem)
        item.start()
        return item

    vectors = [copy(src, vecs.at[i, 0, pl.ds(0, src.shape[0])], vsem.at[0]) for i, src in enumerate((*tb, *sb))]
    tb, sb = ([vecs.at[base + i, :, pl.ds(0, src.shape[0])] for i, src in enumerate(group)]
              for base, group in ((0, tb), (9, sb)))

    def swap(slot, src, part):
        rows = pl.ds(part * PART, PART)
        return pltpu.make_async_remote_copy(
            src_ref=src.at[rows], dst_ref=land.at[slot, rows], send_sem=ssem.at[slot, part], recv_sem=rsem.at[slot, part],
            device_id=(dp, 1 - head), device_id_type=MESH)

    def swap_start(slot, src):
        for part in range(2):
            swap(slot, src, part).start()

    def swap_wait(slot, src):
        for part in range(2):
            swap(slot, src, part).wait()

    def both(body):
        def step(b, carry):
            body(b)
            return carry
        lax.fori_loop(0, 2, step, 0)

    def forward_part(wqkv, wo, q, k, v, ctx, target, bias):
        own2 = dz
        def attend_weights(src):
            return [copy(src[j], wqkv.at[:, pl.ds(j * hw, hw)], wsem.at[1 + j]) for j in range(3)] + [copy(src[3], wo, wsem.at[4])]

        def feed_weights(src):
            return [copy(src[4], w1, wsem.at[5]), copy(src[5], w2, wsem.at[6])]

        def wait(items):
            for item in items:
                item.wait()
        layout_in = [copy(bucket_h, bucket, wsem.at[7]), copy(lens_h, lens, wsem.at[8])]
        tokens_in = [copy(tokens_h.at[0], tok.at[0], wsem.at[0])]
        attend_in = attend_weights(th)
        tokens_in.append(copy(tokens_h.at[1], tok.at[1], wsem.at[9]))
        wait(layout_in)
        fill_masks(bucket, lens, bias)
        value[...] = jnp.zeros_like(value)

        def attend(b, vectors):
            mixed = nn(tok[b], wqkv[...])
            q[b] = ((mixed[:, 0:hw] + vectors[0][...]).astype(BF16).astype(F32) * (1.0 / 8.0)).astype(BF16)
            k[b] = mixed[:, hw:2 * hw].astype(BF16)
            v[b] = (mixed[:, 2 * hw:3 * hw] + vectors[1][...]).astype(BF16)
            attention(q.at[b], k.at[b], v.at[b], bias.at[b], ctx.at[b])
            own[b] = nn(ctx[b], wo[...])

        def feed(b, part, vectors):
            rows = pl.ds(part * PART, PART)
            for j in range(fw // CW):
                cols = pl.ds(j * CW, CW)
                u = nn(h1[b, rows, :], w1[:, cols]) + vectors[5][:, cols]
                f[b, rows, cols] = (0.5 * u * (1.0 + lax.erf(u * SQRT_HALF))).astype(BF16)
            own2[b, rows, :] = nn(f[b, rows, :], w2[...])

        def first_sum(b, rows, vectors):
            return tok[b, rows, :].astype(F32) + ((own[b, rows, :] + land[b, rows, :]) + vectors[2][...])

        def second_sum(b, rows, vectors, residual):
            return residual + ((own2[b, rows, :] + land[2 + b, rows, :]) + vectors[6][...])

        def teach_attend(b):
            @pl.when(b == 1)
            def _():
                wait(tokens_in[1:])
            attend(b, tb)
            swap_start(b, own.at[b])

        def teach_feed(b):
            swap_wait(b, own.at[b])

            def norm(rows):
                n, _ = standardize(first_sum(b, rows, tb))
                h = n * tb[3][...] + tb[4][...]
                target[b, rows, :] = h
                h1[b, rows, :] = h.astype(BF16)
            tiles(SPAN, norm)
            for part in range(2):
                feed(b, part, tb)
                swap(2 + b, own2.at[b], part).start()

        def study_attend(b):
            swap_wait(2 + b, own2.at[b])

            def norm(rows):
                n, _ = standardize(second_sum(b, rows, tb, target[b, rows, :]))
                target[b, rows, :] = n * tb[7][...] + tb[8][...]
            tiles(SPAN, norm)
            attend(b, sb)
            swap_start(b, own.at[b])

        def study_feed(b):
            @pl.when(b == 0)
            def _():
                swap_wait(0, own.at[0])

            def norm(rows):
                n, r = standardize(first_sum(b, rows, sb))
                n1[b, rows, :] = n
                slots = b * SPAN + rows.start + lax.broadcasted_iota(jnp.int32, (TILE, 1), 0)
                real = jnp.where(row_layout(bucket[0], lens, slots)[1], 1.0, 0.0)
                r1[b, rows, :] = jnp.where(lane_half(), r, real)
                h1[b, rows, :] = (n * sb[3][...] + sb[4][...]).astype(BF16)
            tiles(SPAN, norm)
            feed(b, 0, sb)

            @pl.when(b == 1)
            def _():
                swap(2 + b, own2.at[b], 0).start()
            feed(b, 1, sb)

            @pl.when(b == 0)
            def _():
                swap_wait(1, own.at[1])
                swap(2 + b, own2.at[b], 0).start()
            swap(2 + b, own2.at[b], 1).start()

        def study_end(b):
            total = [jnp.zeros((1, d), F32)] * 3

            def norm(rows):
                residual = n1[b, rows, :] * sb[3][...] + sb[4][...]
                n2, r2 = standardize(second_sum(b, rows, sb, residual))
                result = n2 * sb[7][...] + sb[8][...]
                dy = (result - target[b, rows, :]) * r1[b, rows, HEAD_DIM:HEAD_DIM + 1]
                own[b, rows, :] = result
                scaled = dy * sb[7][...]
                out = r2 * (scaled - jnp.mean(scaled, axis=-1, keepdims=True) - n2 * jnp.mean(scaled * n2, axis=-1, keepdims=True))
                dz[b, rows, :] = out
                low = out.astype(BF16)
                dm[b, rows, :] = low
                for i, item in enumerate((low.astype(F32), dy * n2, dy)):
                    total[i] = total[i] + jnp.sum(item, axis=0, keepdims=True)
            for part in range(2):
                swap(2 + b, own2.at[b], part).wait()
                tiles(PART, norm, part * PART)
            for i in range(3):
                value[0, 3 + i:4 + i, 0:d] += total[i]

        all_vectors = vecs.at[:, 0, pl.ds(0, d)]
        pltpu.make_async_copy(all_vectors, all_vectors, vsem.at[0]).wait()
        wait(tokens_in[:1] + attend_in)
        feed_in = feed_weights(th)
        ready()
        both(teach_attend)
        attend_in = attend_weights(sh)
        wait(feed_in)
        both(teach_feed)
        feed_in = feed_weights(sh)
        wait(attend_in)
        both(study_attend)
        spills = [copy(src, dst, osem.at[i]) for i, (src, dst) in enumerate(((q, q_h), (k, k_h), (v, v_h), (ctx, ctx_h)))]
        wait(feed_in)
        both(study_feed)
        both(study_end)
        copy(own, out_h, osem.at[4])
        wait(spills)
    return_out = pltpu.make_async_copy(own, out_h, osem.at[4])

    def V(*shape, dtype=F32):
        return pltpu.VMEM(shape, dtype)
    pl.run_scoped(forward_part, V(d, 3 * hw, dtype=BF16), V(hw, d, dtype=BF16), *[V(2, SPAN, hw, dtype=BF16)] * 4,
                  V(2, SPAN, d), V(2, SPAN, SPAN))

    def backward_part(grad):
        ring = Ring(p, pieces, grad, *ring_refs) if scatter else None
        fly = SmallSum(p, value, vland, vsend, vrecv) if scatter else None
        all_cols = pl.ds(0, CW)
        compute, got = {}, {}

        def put(c, cols, block):
            for i in range(NZ * NY * NX):
                grad[c, i // 4, i // 2 % 2, i % 2, :, cols] = block[i * ROWS:(i + 1) * ROWS]

        def return_grad(c):
            cols = pl.ds(c * CW, CW)
            put(c, all_cols, tn(dm[...].reshape(-1, d), f[:, :, cols].reshape(-1, CW)))

        def slope(j):
            cols = pl.ds(j * CW, CW)

            def half(b, total):
                u = nn(h1[b], w1[:, cols]) + sb[5][:, cols]
                g = nt(dm[b], w2[cols, :])
                du = (g * gelu_slope(u)).astype(BF16)
                f[b, :, cols] = du
                return total + jnp.sum(du.astype(F32), axis=0, keepdims=True)
            total = lax.fori_loop(0, 2, half, jnp.zeros((1, CW), F32))
            value[0, 6 + j // 3:7 + j // 3, pl.ds(j % 3 * CW, CW)] = total

        def hidden_grad(j):
            cols = pl.ds(j * CW, CW)
            put(6 + j, all_cols, tn(h1[...].reshape(-1, d), f[:, :, cols].reshape(-1, CW)))

        def back_first():
            return_out.wait()

            def half(b):
                own[b] = nt(f[b], w1[...])
                swap_start(b, own.at[b])
            both(half)
            fetch(("wo", sh[3], wo), ("wq", sh[0], wqkv.at[:, pl.ds(0, hw)]), ("wk", sh[1], wqkv.at[:, pl.ds(hw, hw)]),
                  ("wv", sh[2], wqkv.at[:, pl.ds(2 * hw, hw)]))

        def fetch(*items):
            for name, src, dst in items:
                got[name] = copy(src, dst, bsem.at[len(got)])
        q, k, v, ctx = (f.at[:, :, pl.ds(i * hw, hw)] for i in range(4))
        dctx = h1.at[:, :, pl.ds(0, hw)]
        do = dm
        wqkv = w1.at[:, pl.ds(0, 3 * hw)]
        wo = w2.at[pl.ds(0, hw)]
        bias = n1.at[:, :, pl.ds(0, SPAN)]

        def norm_back():
            fetch(("q", q_h, q), ("k", k_h, k), ("v", v_h, v), ("ctx", ctx_h, ctx))

            def half(b):
                swap_wait(b, own.at[b])
                total = [jnp.zeros((1, d), F32)] * 3

                def tile(rows):
                    up = dz[b, rows, :] + (own[b, rows, :] + land[b, rows, :])
                    n = n1[b, rows, :]
                    scaled = up * sb[3][...]
                    out = r1[b, rows, 0:1] * (scaled - jnp.mean(scaled, axis=-1, keepdims=True)
                                              - n * jnp.mean(scaled * n, axis=-1, keepdims=True))
                    dz[b, rows, :] = out
                    low = out.astype(BF16)
                    do[b, rows, :] = low
                    for i, item in enumerate((low.astype(F32), up * n, up)):
                        total[i] = total[i] + jnp.sum(item, axis=0, keepdims=True)
                tiles(SPAN, tile)
                for i in range(3):
                    value[0, i:i + 1, 0:d] += total[i]
            both(half)
            fill_masks(bucket, lens, bias)

        def context_grad():
            got["wo"].wait()

            def half(b):
                dctx[b] = nt(do[b], wo[...]).astype(BF16)
            both(half)
            for name in ("q", "k", "v", "ctx"):
                got[name].wait()

        def attend_back(pair, b):
            low_side = lane_half()
            cols = pl.ds(pair * 128, 128)
            q2, k2, v2, dc2 = q[b, :, cols], k[b, :, cols], v[b, :, cols], dctx[b, :, cols]
            parts = []
            for side in (low_side, ~low_side):
                zero = jnp.zeros_like(q2)
                s = nt(jnp.where(side, q2, zero), k2) + bias[b]
                e = jnp.exp(s - jnp.max(s, axis=1, keepdims=True))
                probs = e * (1.0 / jnp.sum(e, axis=1, keepdims=True))
                dprob = nt(jnp.where(side, dc2, zero), v2)
                ds = (probs * (dprob - jnp.sum(probs * dprob, axis=1, keepdims=True))).astype(BF16)
                parts.append((nn(ds, k2), tn(ds, q2), tn(probs.astype(BF16), dc2)))
            dq = (jnp.where(low_side, parts[0][0], parts[1][0]) * (1.0 / 8.0)).astype(BF16)
            dk = jnp.where(low_side, parts[0][1], parts[1][1]).astype(BF16)
            dv = jnp.where(low_side, parts[0][2], parts[1][2]).astype(BF16)
            q[b, :, cols], k[b, :, cols], v[b, :, cols] = dq, dk, dv
            extra = pl.ds(d, 128)
            value[0, pair:pair + 1, extra] += jnp.sum(dq.astype(F32), axis=0, keepdims=True)
            value[0, 3 + pair:4 + pair, extra] += jnp.sum(dv.astype(F32), axis=0, keepdims=True)

        def attend_grad(pair, second):
            cols = pl.ds(pair * 128, 128)
            a = tok[...].reshape(-1, d)
            c = 12 + 2 * pair + second
            if second:
                put(c, pl.ds(0, 128), tn(a, k[:, :, cols].reshape(-1, 128)))
                put(c, pl.ds(128, 128), tn(a, v[:, :, cols].reshape(-1, 128)))
            else:
                put(c, pl.ds(0, 128), tn(do[...].reshape(-1, d), ctx[:, :, cols].reshape(-1, 128)))
                put(c, pl.ds(128, 128), tn(a, q[:, :, cols].reshape(-1, 128)))

        def back_in():
            for name in ("wq", "wk", "wv"):
                got[name].wait()

            def half(b):
                own[b] = (nt(q[b], wqkv[:, 0:hw]) + nt(k[b], wqkv[:, hw:2 * hw])) + nt(v[b], wqkv[:, 2 * hw:3 * hw])
                swap_start(2 + b, own.at[b])
            both(half)
            if scatter:
                fly.start(0)

        def finish_in():
            def half(b):
                swap_wait(2 + b, own.at[b])

                def tile(rows):
                    dz[b, rows, :] += own[b, rows, :] + land[2 + b, rows, :]
                tiles(SPAN, tile)
            both(half)
            copy(dz, grad_in_h, osem.at[5])

        for c in range(6):
            compute[c] = functools.partial(return_grad, c)
            compute[6 + 2 * c] = functools.partial(slope, c)
            compute[7 + 2 * c] = functools.partial(hidden_grad, c)
        compute[18], compute[19], compute[20], compute[33], compute[34] = back_first, norm_back, context_grad, back_in, finish_in
        for pair in range(3):
            compute[21 + 4 * pair] = functools.partial(attend_back, pair, 0)
            compute[22 + 4 * pair] = functools.partial(attend_back, pair, 1)
            compute[23 + 4 * pair] = functools.partial(attend_grad, pair, 0)
            compute[24 + 4 * pair] = functools.partial(attend_grad, pair, 1)

        def owned(c):
            mine, cols = ring.own(c)
            return pltpu.make_async_copy(mine, wide.at[:, cols], gsem.at[0])

        for item in program:
            if item[0] == "c":
                compute[item[2]]()
            elif scatter and item[0] == "f":
                fly.take(item[2])
                if item[2] == 0:
                    fly.start(1)
            elif scatter and ring.stage(*item):
                owned(item[0]).start()
        if scatter:
            small_out[...] = value[2]
            for c in range(len(pieces)):
                ring.drain(c)
            pltpu.make_async_copy(wide, wide, gsem.at[0]).wait()
            fly.drain()
        else:
            rows = copy(grad, wide, osem.at[6])
            small_out[...] = value[0]
            rows.wait()
        pltpu.make_async_copy(dz, grad_in_h, osem.at[5]).wait()

    count = (2 * fw + 4 * hw) // CW
    pl.run_scoped(backward_part, V(count, NZ, NY, NX, ROWS, CW))


def distill(scatter, tokens, bucket, lens, teacher, student):
    def cut(layer):
        wq, bq, wk, wv, bv, wo, bo, g1, s1, w1, b1, w2, b2, g2, s2 = layer
        return [wq, wk, wv, wo, w1, w2], [bq, bv, bo, g1, s1, b1, b2, g2, s2]
    tw, tv = cut(teacher)
    sw, sv = cut(student)
    toks, d = tokens.shape
    hw, fw = tw[0].shape[1], tw[4].shape[1]
    count = (2 * fw + 4 * hw) // CW
    halves, b = toks // SPAN, BF16
    pieces, program = PIECES, PROGRAM
    hbm, vmem = (pl.BlockSpec(memory_space=m) for m in (pl.ANY, pltpu.VMEM))
    def S(*shape, dtype=F32):
        return jax.ShapeDtypeStruct(shape, dtype)
    def V(*shape, dtype=F32):
        return pltpu.VMEM(shape, dtype)
    dma = pltpu.SemaphoreType.DMA
    wide = S(ROWS, count * CW) if scatter else S(count, NZ, NY, NX, ROWS, CW)
    outs = (S(halves, SPAN, d), S(halves, SPAN, d), wide, S(8, 896)) + (S(halves, SPAN, hw, dtype=b),) * 4
    return pl.pallas_call(
        functools.partial(step_kernel, scatter, pieces, program),
        out_shape=outs,
        in_specs=[hbm] * 33,
        out_specs=(hbm, hbm, hbm, vmem) + (hbm,) * 4,
        scratch_shapes=[
            V(halves, SPAN, d, dtype=b), V(d, fw, dtype=b), V(fw, d, dtype=b), V(halves, SPAN, fw, dtype=b), V(halves, SPAN, d, dtype=b),
            V(halves, SPAN, d, dtype=b), V(halves, SPAN, d), V(halves, SPAN, d), V(halves, SPAN, 128), V(2, SPAN, d), V(4, SPAN, d),
            V(18, 1, fw), V(3, 8, 896), V(2, 4, 8, 896),
            dma((1,)), dma((10,)), dma((7,)), dma((4, 2)), dma((4, 2)), dma((8,)), dma((2,)), dma((2,)), dma((1,)),
            pltpu.SMEM((1,), jnp.int32), pltpu.SMEM((1, 8), jnp.int32)]
        + (ring_scratch(pieces) if scatter else []),
        compiler_params=pltpu.CompilerParams(collective_id=1, has_side_effects=True, vmem_limit_bytes=VMEM_BYTES),
    )(bucket, lens, tokens.reshape(halves, SPAN, d), *tw, *sw, *tv, *sv)[:4]


def finish_kernel(out_h, gin_h, wide_h, small_h, out, gin, gq, gk, gv, go, g1w, g2w, *rest):
    small_outs, (wide, small, stage, sem_in, sem_out) = rest[:9], rest[9:]
    d = out.shape[2]
    fw, hw = g1w.shape[1], gq.shape[1]
    count = [0]

    def copy(src, dst):
        count[0] += 1
        return pltpu.make_async_copy(src, dst, sem_out.at[count[0] - 1])

    loads, stores = [(small_h, small), (wide_h, wide)], [[], []]
    for dst, row in zip((small_outs[i] for i in (2, 3, 4, 6, 7, 8)), range(6)):
        stores[0].append(copy(small.at[row, pl.ds(0, d)], dst))
    for half in range(2):
        stores[0].append(copy(small.at[6 + half, pl.ds(0, d)], small_outs[5].at[pl.ds(half * d, d)]))
    for pair in range(hw // 128):
        at, extra = pl.ds(pair * 128, 128), pl.ds(d, 128)
        stores[0].append(copy(small.at[pair, extra], small_outs[0].at[at]))
        stores[0].append(copy(small.at[3 + pair, extra], small_outs[1].at[at]))
        for i, dst in enumerate((go, gq, gk, gv)):
            stores[1].append(copy(wide.at[:, pl.ds(2 * fw + pair * 512 + i * 128, 128)], dst.at[:, at]))
    stores[1].append(copy(wide.at[:, pl.ds(0, fw)], g2w))
    stores[1].append(copy(wide.at[:, pl.ds(fw, fw)], g1w))
    for src, dst in ((out_h, out), (gin_h, gin)):
        for b in range(2):
            for rows in (pl.ds(0, SPAN // 2), pl.ds(SPAN // 2, SPAN // 2)):
                place = stage.at[len(loads) - 2]
                loads.append((src.at[b, rows], place))
                stores.append([copy(place, dst.at[b, rows])])
    loads = [pltpu.make_async_copy(src, dst, sem_in.at[i]) for i, (src, dst) in enumerate(loads)]
    for item in loads:
        item.start()
    for load, group in zip(loads, stores):
        load.wait()
        for item in group:
            item.start()
    for group in stores:
        for item in group:
            item.wait()


def finish(out_raw, gin_raw, wide, small, hw, fw):
    d = out_raw.shape[2]
    def S(*shape):
        return jax.ShapeDtypeStruct(shape, F32)
    hbm = pl.BlockSpec(memory_space=pl.ANY)
    return pl.pallas_call(
        finish_kernel,
        out_shape=(S(*out_raw.shape), S(*gin_raw.shape), S(ROWS, hw), S(ROWS, hw), S(ROWS, hw), S(ROWS, hw), S(ROWS, fw), S(ROWS, fw),
                   S(hw), S(hw), S(d), S(d), S(d), S(fw), S(d), S(d), S(d)),
        in_specs=[hbm] * 4,
        out_specs=(hbm,) * 17,
        scratch_shapes=[pltpu.VMEM(wide.shape, F32), pltpu.VMEM(small.shape, F32), pltpu.VMEM((8, SPAN // 2, d), F32),
                        pltpu.SemaphoreType.DMA((10,)), pltpu.SemaphoreType.DMA((48,))],
        compiler_params=pltpu.CompilerParams(vmem_limit_bytes=VMEM_BYTES),
    )(out_raw, gin_raw, wide, small)


def shards(*args):
    tokens, row_bucket, row_lengths = args[:3]
    teacher, student = args[3:18], args[18:33]
    d = tokens.shape[1]
    hw, fw = student[0].shape[1], student[9].shape[1]
    scatter = lax.axis_size("dp") == NZ * NY * NX
    out, *got = distill(scatter, tokens, row_bucket, row_lengths, teacher, student)
    if scatter:
        out, grad_in, gq, gk, gv, go, g1, g2, qb, vb, ob, g1g, s1g, b1g, b2g, g2g, s2g = finish(out, *got, hw, fw)
    else:
        grad_in, wide, small = got
        rows = wide.reshape(wide.shape[0], d, CW)
        steps = fw // CW
        last = [2 * steps + i for i in range(2 * hw // 128)]
        first, second = ([rows[c] for c in last[i::2]] for i in (0, 1))
        mats = [
            jnp.concatenate([m[:, 128:] for m in first], axis=1),
            jnp.concatenate([m[:, :128] for m in second], axis=1),
            jnp.concatenate([m[:, 128:] for m in second], axis=1),
            jnp.concatenate([m[:, :128] for m in first], axis=1),
            jnp.concatenate([rows[c] for c in range(steps, 2 * steps)], axis=1),
            jnp.concatenate([rows[c] for c in range(steps)], axis=1),
        ]
        gq, gk, gv, go, g1, g2 = (lax.psum_scatter(m, "dp", scatter_dimension=0, tiled=True) for m in mats)
        small = lax.psum(small, "dp")
        qb, vb = small[0:3, d:].reshape(-1), small[3:6, d:].reshape(-1)
        ob, g1g, s1g, b2g, g2g, s2g = (small[i, :d] for i in range(6))
        b1g = small[6:8, :d].reshape(-1)
    toks = tokens.shape[0]
    return (
        out.reshape(toks, d), grad_in.reshape(toks, d), gq, qb, gk, gv, vb, go.T, ob, g1g, s1g, g1, b1g, g2.T, b2g, g2g, s2g
    )


def solution(mesh):
    placed = (
        P("dp", None),
        P("dp"),
        P("dp", None),
        P(None, "head"),
        P("head"),
        P(None, "head"),
        P(None, "head"),
        P("head"),
        P("head", None),
        P(),
        P(),
        P(),
        P(None, "head"),
        P("head"),
        P("head", None),
        P(),
        P(),
        P(),
        P(None, "head"),
        P("head"),
        P(None, "head"),
        P(None, "head"),
        P("head"),
        P("head", None),
        P(),
        P(),
        P(),
        P(None, "head"),
        P("head"),
        P("head", None),
        P(),
        P(),
        P(),
    )
    return jax.shard_map(
        shards,
        mesh=mesh,
        in_specs=placed,
        out_specs=(
            P("dp", None),
            P("dp", None),
            P("dp", "head"),
            P("head"),
            P("dp", "head"),
            P("dp", "head"),
            P("head"),
            P("head", "dp"),
            P(),
            P(),
            P(),
            P("dp", "head"),
            P("head"),
            P("head", "dp"),
            P(),
            P(),
            P(),
        ),
        check_vma=False,
    )
```

```python
import functools

import jax
import jax.numpy as jnp
from jax import lax
from jax.experimental import pallas as pl
from jax.experimental.pallas import tpu as pltpu
from jax.sharding import PartitionSpec as P

MESH = pl.DeviceIdType.MESH
HEAD_DIM = 64
SPAN = 512
NORM_EPS = 1e-12
SQRT_HALF = 0.7071067811865476
F32, BF16 = jnp.float32, jnp.bfloat16
VMEM_BYTES = 63 * 2**20 + 2**19


def nn(a, b):
    return jnp.dot(a, b, preferred_element_type=F32)


def nt(a, b):
    return lax.dot_general(a, b, (((1,), (1,)), ((), ())), preferred_element_type=F32)


def tn(a, b):
    return lax.dot_general(a, b, (((0,), (0,)), ((), ())), preferred_element_type=F32)


def row_layout(bucket, lens, slots):
    shift = jnp.where(bucket == 0, SPAN // 4, jnp.where(bucket == 1, SPAN // 2, SPAN))
    row = jnp.where(bucket == 0, slots // (SPAN // 4), jnp.where(bucket == 1, slots // (SPAN // 2), slots // SPAN))
    length = jnp.zeros_like(slots)
    for j in range(8):
        length = jnp.where(row == j, lens[0, j], length)
    return row, (slots - row * shift) < length


def fill_masks(bucket, lens, bias):
    code = bucket[0]
    for b in range(bias.shape[0]):
        q = b * SPAN + lax.broadcasted_iota(jnp.int32, (SPAN, 1), 0)
        k = b * SPAN + lax.broadcasted_iota(jnp.int32, (1, SPAN), 1)
        q_row, _ = row_layout(code, lens, q)
        k_row, k_ok = row_layout(code, lens, k)
        bias[b] = jnp.where(q_row == jnp.where(k_ok, k_row, -1), 0.0, -1000000000.0)


def lane_half():
    return lax.broadcasted_iota(jnp.int32, (1, 128), 1) < HEAD_DIM


def attention(q, k, v, bias, ctx):
    low = lane_half()
    for pair in range(q.shape[1] // 128):
        cols = pl.ds(pair * 128, 128)
        q2, k2, v2 = q[:, cols], k[:, cols], v[:, cols]
        parts = []
        for side in (low, ~low):
            s = nt(jnp.where(side, q2, jnp.zeros_like(q2)), k2) + bias[...]
            e = jnp.exp(s - jnp.max(s, axis=1, keepdims=True))
            mass = jnp.sum(e, axis=1, keepdims=True)
            parts.append(nn(e.astype(BF16), v2) * (1.0 / mass))
        ctx[:, cols] = jnp.where(low, parts[0], parts[1]).astype(BF16)


def standardize(z):
    centred = z - jnp.mean(z, axis=-1, keepdims=True)
    inv = lax.rsqrt(jnp.mean(centred * centred, axis=-1, keepdims=True) + NORM_EPS)
    return centred * inv, inv


TILE = 128
PART = SPAN // 2


def tiles(rows, body, first=0):
    for i in range(rows // TILE):
        body(pl.ds(first + i * TILE, TILE))


CW = 256
NZ, NY, NX = 4, 2, 2
ROWS = 48


class Place:
    def __init__(self):
        self.dp = lax.axis_index("dp")
        self.head = lax.axis_index("head")
        self.z = self.dp // 4
        self.y = lax.rem(self.dp // 2, 2)
        self.x = lax.rem(self.dp, 2)

    def at(self, z=None, y=None, x=None):
        z, y, x = (mine if given is None else given for given, mine in ((z, self.z), (y, self.y), (x, self.x)))
        return (z * 4 + y * 2 + x, self.head)


def landing(pieces):
    places, used = [], {False: [], True: []}
    for kind, _, _, width in pieces:
        taken = used[kind[0] in "zd"]
        i = next((i for i, cols in enumerate(taken) if cols + width <= CW), len(taken))
        taken[i:i + 1] = [(taken[i] if i < len(taken) else 0) + width]
        places.append((i, taken[i] - width))
    return places, len(used[False]), len(used[True])


class Ring:
    def __init__(self, place, pieces, grad, pair_a, pair_b, path, zpath, zpair_a, zpair_b, send, recv):
        self.p, self.pieces, self.grad = place, pieces, grad
        self.lands = (pair_a, pair_b, path), (zpair_a, zpair_b, zpath)
        self.send, self.recv = send, recv
        self.places = landing(pieces)[0]

    def _refs(self, c, which):
        kind, chunk, col, width = self.pieces[c]
        deep = kind[0] in "zd"
        i, land_col = self.places[c]
        land = self.lands[deep][which]
        every = (slice(None),) * (len(land.shape) - 2)
        return deep, self.grad.at[chunk, :, :, :, :, pl.ds(col, width)], land.at[(i, *every, pl.ds(land_col, width))]

    def _pair(self, c, step):
        p = self.p
        deep, g, land = self._refs(c, step)
        axis = [a for a in self.pieces[c][0] if a in "xy"][step]
        if deep:
            view = g.at[p.z]
            if step == 0:
                pick = (lambda j: view.at[:, j]) if axis == "x" else (lambda j: view.at[j])
            else:
                pick = (lambda j: view.at[p.y, j]) if axis == "x" else (lambda j: view.at[j, p.x])
        elif step == 0:
            pick = (lambda j: g.at[:, :, j]) if axis == "x" else (lambda j: g.at[:, j])
        else:
            pick = (lambda j: g.at[:, p.y, j]) if axis == "x" else (lambda j: g.at[:, j, p.x])
        mine = p.x if axis == "x" else p.y
        to = p.at(x=1 - p.x) if axis == "x" else p.at(y=1 - p.y)
        copy = pltpu.make_async_remote_copy(
            src_ref=pick(1 - mine), dst_ref=land, send_sem=self.send.at[c], recv_sem=self.recv.at[c, step],
            device_id=to, device_id_type=MESH)
        return copy, pick(mine), land

    def pair_send(self, c, step):
        self._pair(c, step)[0].start()

    def pair_take(self, c, step):
        copy, mine, land = self._pair(c, step)
        copy.wait_recv()
        mine[...] += land[...]

    def _path_refs(self, c):
        p = self.p
        deep, g, land = self._refs(c, 2)
        if deep:
            return (lambda lo, n: g.at[pl.ds(lo, n)]), land
        return (lambda lo, n: g.at[pl.ds(lo, n), p.y, p.x]), land

    def _hop(self, c, z, up):
        blocks, land = self._path_refs(c)
        if up:
            src, dst, k, to = blocks(z + 1, 3 - z), land.at[pl.ds(0, 3 - z)], 2, self.p.z + 1
        else:
            src, dst, k, to = blocks(0, z), land.at[pl.ds(5 - z, z)], 3, self.p.z - 1
        return pltpu.make_async_remote_copy(
            src_ref=src, dst_ref=dst, send_sem=self.send.at[c], recv_sem=self.recv.at[c, k],
            device_id=self.p.at(z=to), device_id_type=MESH)

    def path_start(self, c):
        @pl.when(self.p.z == 0)
        def _():
            self._hop(c, 0, True).start()

        @pl.when(self.p.z == 3)
        def _():
            self._hop(c, 3, False).start()

    def path_mid(self, c, first):
        blocks, land = self._path_refs(c)
        for z in (1, 2):
            up = (z == 1) == first

            @pl.when(self.p.z == z)
            def _(z=z, up=up):
                if up:
                    self._hop(c, z - 1, True).wait_recv()
                    own = blocks(z + 1, 3 - z)
                    own[...] += land[pl.ds(1, 3 - z)]
                    self._hop(c, z, True).start()
                else:
                    self._hop(c, z + 1, False).wait_recv()
                    own = blocks(0, z)
                    own[...] += land[pl.ds(4 - z, z)]
                    self._hop(c, z, False).start()

    def path_end(self, c):
        blocks, land = self._path_refs(c)
        for z in range(NZ):
            @pl.when(self.p.z == z)
            def _(z=z):
                if z == 0:
                    self._hop(c, 1, False).wait_recv()
                if z == 3:
                    self._hop(c, 2, True).wait_recv()
                own = blocks(z, 1)
                total = own[...]
                if z > 0:
                    total = total + land[pl.ds(0, 1)]
                if z < 3:
                    total = total + land[pl.ds(4, 1)]
                own[...] = total

    def _direct(self, c, j):
        blocks, land = self._path_refs(c)
        to = lax.rem(self.p.z + j, NZ)
        return pltpu.make_async_remote_copy(
            src_ref=blocks(to, 1), dst_ref=land.at[pl.ds(j - 1, 1)], send_sem=self.send.at[c], recv_sem=self.recv.at[c, 2],
            device_id=self.p.at(z=to), device_id_type=MESH)

    def direct_send(self, c):
        for j in (1, 2, 3):
            self._direct(c, j).start()

    def direct_take(self, c):
        blocks, land = self._path_refs(c)
        pltpu.make_async_copy(land.at[pl.ds(0, 3)], land.at[pl.ds(0, 3)], self.recv.at[c, 2]).wait()
        own = blocks(self.p.z, 1)
        own[...] += (land[pl.ds(0, 1)] + land[pl.ds(1, 1)]) + land[pl.ds(2, 1)]

    def drain(self, c):
        width = self.pieces[c][3]
        blocks = self.lands[False][2].at[pl.ds(0, 3), :, :, pl.ds(0, width)]
        pltpu.make_async_copy(blocks, blocks, self.send.at[c]).wait()

    def stages(self, c):
        take = lambda step: functools.partial(self.pair_take, c, step)
        send = lambda step: functools.partial(self.pair_send, c, step)
        if "d" in self.pieces[c][0]:
            column = [[functools.partial(self.direct_send, c)], [functools.partial(self.direct_take, c)]]
        else:
            column = [[functools.partial(self.path_start, c)], [functools.partial(self.path_mid, c, True)],
                      [functools.partial(self.path_mid, c, False)], [functools.partial(self.path_end, c)]]
        if self.pieces[c][0][0] in "zd":
            return column[:-1] + [column[-1] + [send(0)], [take(0), send(1)], [take(1)]]
        return [[send(0)], [take(0), send(1)], [take(1)] + column[0]] + column[1:]

    def stage(self, c, s):
        steps = self.stages(c)
        for step in steps[s]:
            step()
        return s == len(steps) - 1

    def own(self, c):
        p = self.p
        _, chunk, col, width = self.pieces[c]
        return self.grad.at[chunk, p.z, p.y, p.x, :, pl.ds(col, width)], pl.ds(chunk * CW + col, width)


def ring_scratch(pieces):
    _, flat, deep = landing(pieces)
    f = jnp.float32
    return [
        pltpu.VMEM((flat, NZ, 2, ROWS, CW), f),
        pltpu.VMEM((flat, NZ, ROWS, CW), f),
        pltpu.VMEM((flat, 5, ROWS, CW), f),
        pltpu.VMEM((deep, 5, NY, NX, ROWS, CW), f),
        pltpu.VMEM((deep, 2, ROWS, CW), f),
        pltpu.VMEM((deep, ROWS, CW), f),
        pltpu.SemaphoreType.DMA((len(pieces),)),
        pltpu.SemaphoreType.DMA((len(pieces), 4)),
    ]


def greet(place, scatter):
    barrier = pltpu.get_barrier_semaphore()
    p = place
    others = [(p.dp, 1 - p.head)]
    if scatter:
        others += [p.at(x=1 - p.x), p.at(y=1 - p.y), p.at(x=1 - p.x, y=1 - p.y)] + [p.at(z=lax.rem(p.z + j, NZ)) for j in (1, 2, 3)]
    for to in others:
        pl.semaphore_signal(barrier, inc=1, device_id=to, device_id_type=MESH)
    return lambda: pl.semaphore_wait(barrier, len(others))


PIECES = [
    ("yx", 0, 0, 128), ("zxy", 0, 128, 128), ("xyd", 1, 0, 256), ("dxy", 2, 0, 256), ("yxd", 3, 0, 256),
    ("yxd", 4, 0, 256), ("xy", 5, 0, 256), ("xy", 6, 0, 256), ("dxy", 7, 0, 256), ("yx", 8, 0, 256),
    ("yx", 9, 0, 256), ("yx", 10, 0, 256), ("zyx", 11, 0, 256), ("xy", 12, 0, 256), ("xy", 13, 0, 256),
    ("zyx", 14, 0, 128), ("xy", 14, 128, 128), ("yx", 15, 0, 128), ("yxd", 15, 128, 128), ("yxd", 16, 0, 128),
    ("xy", 16, 128, 128), ("xyd", 17, 0, 128), ("xyd", 17, 128, 128),
]
PROGRAM = [
    ("c", 0, 0), (0, 0), (1, 0), ("c", 0, 1), (2, 0), ("c", 0, 2), (3, 0), ("c", 0, 3), (4, 0), ("c", 0, 4),
    ("c", 0, 5), (6, 0), ("c", 0, 6), (5, 0), ("c", 0, 8), ("c", 0, 10), (0, 1), ("c", 0, 12), (1, 1), ("c", 0, 14),
    ("c", 0, 16), ("c", 0, 18), (2, 1), ("c", 0, 7), (7, 0), (4, 1), ("c", 0, 9), (8, 0), ("c", 0, 11), (9, 0),
    ("c", 0, 13), ("c", 0, 15), ("c", 0, 17), ("c", 0, 19), (6, 1), ("c", 0, 20), (0, 2), (5, 1), ("c", 0, 21),
    (12, 0), ("c", 0, 22), (3, 1), (2, 2), ("c", 0, 23), (10, 0), ("c", 0, 24), (13, 0), (1, 2), (7, 1), ("c", 0, 25),
    ("c", 0, 26), (4, 2), (0, 3), (9, 1), ("c", 0, 27), ("c", 0, 28), (5, 2), ("c", 0, 29), (6, 2), (3, 2),
    ("c", 0, 30), (11, 0), (14, 0), ("c", 0, 33), ("c", 0, 31), (8, 1), (12, 1), (10, 1), ("c", 0, 32), (13, 1),
    (15, 0), ("c", 0, 34), (7, 2), (2, 3), (3, 3), (9, 2), (1, 3), (17, 0), (0, 4), (4, 3), (16, 0), (6, 3), (18, 0),
    (11, 1), (14, 1), (5, 3), (0, 5), (8, 2), (13, 2), (15, 1), ("f", 0, 0), (20, 0), (10, 2), (1, 4), (7, 3),
    (17, 1), (12, 2), (19, 0), (6, 4), (9, 3), (16, 1), (18, 1), (13, 3), (12, 3), (21, 0), (15, 2), (6, 5), (11, 2),
    (14, 2), (7, 4), (10, 3), (8, 3), (1, 5), (22, 0), (15, 3), (9, 4), (20, 1), (7, 5), (11, 3), (13, 4), (17, 2),
    (9, 5), (19, 1), ("f", 0, 1), (10, 4), (14, 3), (13, 5), (18, 2), (16, 2), (11, 4), (17, 3), (10, 5), (12, 4),
    (14, 4), (15, 4), (21, 1), (16, 3), (20, 2), (18, 3), (17, 4), (11, 5), (16, 4), (21, 2), (14, 5), (22, 1),
    (17, 5), (20, 3), (16, 5), (19, 2), (12, 5), (15, 5), (22, 2), (21, 3), (20, 4), (19, 3), (22, 3), (20, 5),
]


INV_SQRT_2PI = 0.3989422804014327


class SmallSum:
    def __init__(self, place, value, land, send, recv):
        self.p, self.value, self.land, self.send, self.recv = place, value, land, send, recv

    def _copies(self, step):
        p = self.p
        if step == 0:
            mine = p.y * 2 + p.x
            others = [p.at(x=1 - p.x), p.at(y=1 - p.y), p.at(x=1 - p.x, y=1 - p.y)]
        else:
            mine = p.z
            others = [p.at(z=lax.rem(p.z + j, NZ)) for j in (1, 2, 3)]
        return mine, [pltpu.make_async_remote_copy(
            src_ref=self.value.at[step], dst_ref=self.land.at[step, mine], send_sem=self.send.at[step],
            recv_sem=self.recv.at[step], device_id=to, device_id_type=MESH) for to in others]

    def start(self, step):
        mine, copies = self._copies(step)
        self.land[step, mine] = self.value[step]
        for copy in copies:
            copy.start()

    def _three(self, step):
        return self.land.at[step, pl.ds(0, 3)]

    def take(self, step):
        pltpu.make_async_copy(self._three(step), self._three(step), self.recv.at[step]).wait()
        land = self.land
        self.value[step + 1] = (land[step, 0] + land[step, 1]) + (land[step, 2] + land[step, 3])

    def drain(self):
        for step in range(2):
            pltpu.make_async_copy(self._three(step), self._three(step), self.send.at[step]).wait()


def gelu_slope(u):
    return 0.5 * (1.0 + lax.erf(u * SQRT_HALF)) + u * (INV_SQRT_2PI * jnp.exp(-0.5 * u * u))


def step_kernel(scatter, pieces, program, *refs):
    (bucket_h, lens_h, tokens_h), rest = refs[:3], refs[3:]
    th, rest = rest[:6], rest[6:]
    sh, rest = rest[:6], rest[6:]
    tb, rest = rest[:9], rest[9:]
    sb, rest = rest[:9], rest[9:]
    (out_h, grad_in_h, wide, small_out, q_h, k_h, v_h, ctx_h), rest = rest[:8], rest[8:]
    (tok, w1, w2, f, h1, dm, dz, n1, r1, own, land, vecs, value, vland,
     vsem, wsem, osem, ssem, rsem, bsem, vsend, vrecv, gsem, bucket, lens, *ring_refs) = rest
    p = Place()
    dp, head = p.dp, p.head
    d, fw = w1.shape
    hw = q_h.shape[2]
    ready = greet(p, scatter)

    def copy(src, dst, sem):
        item = pltpu.make_async_copy(src, dst, sem)
        item.start()
        return item

    sources = (*tb, *sb)

    def fetch_vectors():
        for i, src in enumerate(sources):
            copy(src, vecs.at[i, 0, pl.ds(0, src.shape[0])], vsem.at[0])

    tb, sb = ([vecs.at[base + i, :, pl.ds(0, src.shape[0])] for i, src in enumerate(group)]
              for base, group in ((0, tb), (9, sb)))

    def swap(slot, src, part):
        rows = pl.ds(part * PART, PART)
        return pltpu.make_async_remote_copy(
            src_ref=src.at[rows], dst_ref=land.at[slot, rows], send_sem=ssem.at[slot, part], recv_sem=rsem.at[slot, part],
            device_id=(dp, 1 - head), device_id_type=MESH)

    def swap_start(slot, src):
        for part in range(2):
            swap(slot, src, part).start()

    def swap_wait(slot, src):
        for part in range(2):
            swap(slot, src, part).wait()

    def both(body):
        def step(b, carry):
            body(b)
            return carry
        lax.fori_loop(0, 2, step, 0)

    def forward_part(wqkv, wo, q, k, v, ctx, target, bias):
        own2 = dz
        def attend_weights(src):
            return [copy(src[j], wqkv.at[:, pl.ds(j * hw, hw)], wsem.at[1 + j]) for j in range(3)] + [copy(src[3], wo, wsem.at[4])]

        def feed_weights(src):
            return [copy(src[4], w1, wsem.at[5]), copy(src[5], w2, wsem.at[6])]

        def wait(items):
            for item in items:
                item.wait()
        layout_in = [copy(bucket_h, bucket, wsem.at[7]), copy(lens_h, lens, wsem.at[8])]
        tokens_in = [copy(tokens_h.at[0], tok.at[0], wsem.at[0])]
        attend_in = attend_weights(th)
        tokens_in.append(copy(tokens_h.at[1], tok.at[1], wsem.at[9]))
        fetch_vectors()
        wait(layout_in)
        fill_masks(bucket, lens, bias)
        value[...] = jnp.zeros_like(value)

        def attend(b, vectors):
            mixed = nn(tok[b], wqkv[...])
            q[b] = ((mixed[:, 0:hw] + vectors[0][...]).astype(BF16).astype(F32) * (1.0 / 8.0)).astype(BF16)
            k[b] = mixed[:, hw:2 * hw].astype(BF16)
            v[b] = (mixed[:, 2 * hw:3 * hw] + vectors[1][...]).astype(BF16)
            attention(q.at[b], k.at[b], v.at[b], bias.at[b], ctx.at[b])
            own[b] = nn(ctx[b], wo[...])

        def feed(b, part, vectors):
            rows = pl.ds(part * PART, PART)
            for j in range(fw // CW):
                cols = pl.ds(j * CW, CW)
                u = nn(h1[b, rows, :], w1[:, cols]) + vectors[5][:, cols]
                f[b, rows, cols] = (0.5 * u * (1.0 + lax.erf(u * SQRT_HALF))).astype(BF16)
            own2[b, rows, :] = nn(f[b, rows, :], w2[...])

        def first_sum(b, rows, vectors):
            return tok[b, rows, :].astype(F32) + ((own[b, rows, :] + land[b, rows, :]) + vectors[2][...])

        def second_sum(b, rows, vectors, residual):
            return residual + ((own2[b, rows, :] + land[2 + b, rows, :]) + vectors[6][...])

        def teach_attend(b):
            @pl.when(b == 1)
            def _():
                wait(tokens_in[1:])
            attend(b, tb)
            swap_start(b, own.at[b])

        def teach_feed(b):
            swap_wait(b, own.at[b])

            def norm(rows):
                n, _ = standardize(first_sum(b, rows, tb))
                h = n * tb[3][...] + tb[4][...]
                target[b, rows, :] = h
                h1[b, rows, :] = h.astype(BF16)
            tiles(SPAN, norm)
            for part in range(2):
                feed(b, part, tb)
                swap(2 + b, own2.at[b], part).start()

        def study_attend(b):
            swap_wait(2 + b, own2.at[b])

            def norm(rows):
                n, _ = standardize(second_sum(b, rows, tb, target[b, rows, :]))
                target[b, rows, :] = n * tb[7][...] + tb[8][...]
            tiles(SPAN, norm)
            attend(b, sb)
            swap_start(b, own.at[b])

        def study_feed(b):
            @pl.when(b == 0)
            def _():
                swap_wait(0, own.at[0])

            def norm(rows):
                n, r = standardize(first_sum(b, rows, sb))
                n1[b, rows, :] = n
                slots = b * SPAN + rows.start + lax.broadcasted_iota(jnp.int32, (TILE, 1), 0)
                real = jnp.where(row_layout(bucket[0], lens, slots)[1], 1.0, 0.0)
                r1[b, rows, :] = jnp.where(lane_half(), r, real)
                h1[b, rows, :] = (n * sb[3][...] + sb[4][...]).astype(BF16)
            tiles(SPAN, norm)
            feed(b, 0, sb)

            @pl.when(b == 1)
            def _():
                swap(2 + b, own2.at[b], 0).start()
            feed(b, 1, sb)

            @pl.when(b == 0)
            def _():
                swap_wait(1, own.at[1])
                swap(2 + b, own2.at[b], 0).start()
            swap(2 + b, own2.at[b], 1).start()

        def study_end(b):
            total = [jnp.zeros((1, d), F32)] * 3

            def norm(rows):
                residual = n1[b, rows, :] * sb[3][...] + sb[4][...]
                n2, r2 = standardize(second_sum(b, rows, sb, residual))
                result = n2 * sb[7][...] + sb[8][...]
                dy = (result - target[b, rows, :]) * r1[b, rows, HEAD_DIM:HEAD_DIM + 1]
                own[b, rows, :] = result
                scaled = dy * sb[7][...]
                out = r2 * (scaled - jnp.mean(scaled, axis=-1, keepdims=True) - n2 * jnp.mean(scaled * n2, axis=-1, keepdims=True))
                dz[b, rows, :] = out
                low = out.astype(BF16)
                dm[b, rows, :] = low
                for i, item in enumerate((low.astype(F32), dy * n2, dy)):
                    total[i] = total[i] + jnp.sum(item, axis=0, keepdims=True)
            for part in range(2):
                swap(2 + b, own2.at[b], part).wait()
                tiles(PART, norm, part * PART)
            for i in range(3):
                value[0, 3 + i:4 + i, 0:d] += total[i]

        all_vectors = vecs.at[:, 0, pl.ds(0, d)]
        pltpu.make_async_copy(all_vectors, all_vectors, vsem.at[0]).wait()
        wait(tokens_in[:1] + attend_in)
        feed_in = feed_weights(th)
        ready()
        both(teach_attend)
        attend_in = attend_weights(sh)
        wait(feed_in)
        both(teach_feed)
        feed_in = feed_weights(sh)
        wait(attend_in)
        both(study_attend)
        spills = [copy(src, dst, osem.at[i]) for i, (src, dst) in enumerate(((q, q_h), (k, k_h), (v, v_h), (ctx, ctx_h)))]
        wait(feed_in)
        both(study_feed)
        both(study_end)
        copy(own, out_h, osem.at[4])
        wait(spills)
    return_out = pltpu.make_async_copy(own, out_h, osem.at[4])

    def V(*shape, dtype=F32):
        return pltpu.VMEM(shape, dtype)
    pl.run_scoped(forward_part, V(d, 3 * hw, dtype=BF16), V(hw, d, dtype=BF16), *[V(2, SPAN, hw, dtype=BF16)] * 4,
                  V(2, SPAN, d), V(2, SPAN, SPAN))

    def backward_part(grad):
        ring = Ring(p, pieces, grad, *ring_refs) if scatter else None
        fly = SmallSum(p, value, vland, vsend, vrecv) if scatter else None
        all_cols = pl.ds(0, CW)
        compute, got = {}, {}

        def put(c, cols, block):
            for i in range(NZ * NY * NX):
                grad[c, i // 4, i // 2 % 2, i % 2, :, cols] = block[i * ROWS:(i + 1) * ROWS]

        def return_grad(c):
            cols = pl.ds(c * CW, CW)
            put(c, all_cols, tn(dm[...].reshape(-1, d), f[:, :, cols].reshape(-1, CW)))

        def slope(j):
            cols = pl.ds(j * CW, CW)

            def half(b, total):
                u = nn(h1[b], w1[:, cols]) + sb[5][:, cols]
                g = nt(dm[b], w2[cols, :])
                du = (g * gelu_slope(u)).astype(BF16)
                f[b, :, cols] = du
                return total + jnp.sum(du.astype(F32), axis=0, keepdims=True)
            total = lax.fori_loop(0, 2, half, jnp.zeros((1, CW), F32))
            value[0, 6 + j // 3:7 + j // 3, pl.ds(j % 3 * CW, CW)] = total

        def hidden_grad(j):
            cols = pl.ds(j * CW, CW)
            put(6 + j, all_cols, tn(h1[...].reshape(-1, d), f[:, :, cols].reshape(-1, CW)))

        def back_first():
            return_out.wait()

            def half(b):
                own[b] = nt(f[b], w1[...])
                swap_start(b, own.at[b])
            both(half)
            fetch(("wo", sh[3], wo), ("wq", sh[0], wqkv.at[:, pl.ds(0, hw)]), ("wk", sh[1], wqkv.at[:, pl.ds(hw, hw)]),
                  ("wv", sh[2], wqkv.at[:, pl.ds(2 * hw, hw)]))

        def fetch(*items):
            for name, src, dst in items:
                got[name] = copy(src, dst, bsem.at[len(got)])
        q, k, v, ctx = (f.at[:, :, pl.ds(i * hw, hw)] for i in range(4))
        dctx = h1.at[:, :, pl.ds(0, hw)]
        do = dm
        wqkv = w1.at[:, pl.ds(0, 3 * hw)]
        wo = w2.at[pl.ds(0, hw)]
        bias = n1.at[:, :, pl.ds(0, SPAN)]

        def norm_back():
            fetch(("q", q_h, q), ("k", k_h, k), ("v", v_h, v), ("ctx", ctx_h, ctx))

            def half(b):
                swap_wait(b, own.at[b])
                total = [jnp.zeros((1, d), F32)] * 3

                def tile(rows):
                    up = dz[b, rows, :] + (own[b, rows, :] + land[b, rows, :])
                    n = n1[b, rows, :]
                    scaled = up * sb[3][...]
                    out = r1[b, rows, 0:1] * (scaled - jnp.mean(scaled, axis=-1, keepdims=True)
                                              - n * jnp.mean(scaled * n, axis=-1, keepdims=True))
                    dz[b, rows, :] = out
                    low = out.astype(BF16)
                    do[b, rows, :] = low
                    for i, item in enumerate((low.astype(F32), up * n, up)):
                        total[i] = total[i] + jnp.sum(item, axis=0, keepdims=True)
                tiles(SPAN, tile)
                for i in range(3):
                    value[0, i:i + 1, 0:d] += total[i]
            both(half)
            fill_masks(bucket, lens, bias)

        def context_grad():
            got["wo"].wait()

            def half(b):
                dctx[b] = nt(do[b], wo[...]).astype(BF16)
            both(half)
            for name in ("q", "k", "v", "ctx"):
                got[name].wait()

        def attend_back(pair, b):
            low_side = lane_half()
            cols = pl.ds(pair * 128, 128)
            q2, k2, v2, dc2 = q[b, :, cols], k[b, :, cols], v[b, :, cols], dctx[b, :, cols]
            parts = []
            for side in (low_side, ~low_side):
                zero = jnp.zeros_like(q2)
                s = nt(jnp.where(side, q2, zero), k2) + bias[b]
                e = jnp.exp(s - jnp.max(s, axis=1, keepdims=True))
                probs = e * (1.0 / jnp.sum(e, axis=1, keepdims=True))
                dprob = nt(jnp.where(side, dc2, zero), v2)
                ds = (probs * (dprob - jnp.sum(probs * dprob, axis=1, keepdims=True))).astype(BF16)
                parts.append((nn(ds, k2), tn(ds, q2), tn(probs.astype(BF16), dc2)))
            dq = (jnp.where(low_side, parts[0][0], parts[1][0]) * (1.0 / 8.0)).astype(BF16)
            dk = jnp.where(low_side, parts[0][1], parts[1][1]).astype(BF16)
            dv = jnp.where(low_side, parts[0][2], parts[1][2]).astype(BF16)
            q[b, :, cols], k[b, :, cols], v[b, :, cols] = dq, dk, dv
            extra = pl.ds(d, 128)
            value[0, pair:pair + 1, extra] += jnp.sum(dq.astype(F32), axis=0, keepdims=True)
            value[0, 3 + pair:4 + pair, extra] += jnp.sum(dv.astype(F32), axis=0, keepdims=True)

        def attend_grad(pair, second):
            cols = pl.ds(pair * 128, 128)
            a = tok[...].reshape(-1, d)
            c = 12 + 2 * pair + second
            if second:
                put(c, pl.ds(0, 128), tn(a, k[:, :, cols].reshape(-1, 128)))
                put(c, pl.ds(128, 128), tn(a, v[:, :, cols].reshape(-1, 128)))
            else:
                put(c, pl.ds(0, 128), tn(do[...].reshape(-1, d), ctx[:, :, cols].reshape(-1, 128)))
                put(c, pl.ds(128, 128), tn(a, q[:, :, cols].reshape(-1, 128)))

        def back_in():
            for name in ("wq", "wk", "wv"):
                got[name].wait()

            def half(b):
                own[b] = (nt(q[b], wqkv[:, 0:hw]) + nt(k[b], wqkv[:, hw:2 * hw])) + nt(v[b], wqkv[:, 2 * hw:3 * hw])
                swap_start(2 + b, own.at[b])
            both(half)
            if scatter:
                fly.start(0)

        def finish_in():
            def half(b):
                swap_wait(2 + b, own.at[b])

                def tile(rows):
                    dz[b, rows, :] += own[b, rows, :] + land[2 + b, rows, :]
                tiles(SPAN, tile)
            both(half)
            copy(dz, grad_in_h, osem.at[5])

        for c in range(6):
            compute[c] = functools.partial(return_grad, c)
            compute[6 + 2 * c] = functools.partial(slope, c)
            compute[7 + 2 * c] = functools.partial(hidden_grad, c)
        compute[18], compute[19], compute[20], compute[33], compute[34] = back_first, norm_back, context_grad, back_in, finish_in
        for pair in range(3):
            compute[21 + 4 * pair] = functools.partial(attend_back, pair, 0)
            compute[22 + 4 * pair] = functools.partial(attend_back, pair, 1)
            compute[23 + 4 * pair] = functools.partial(attend_grad, pair, 0)
            compute[24 + 4 * pair] = functools.partial(attend_grad, pair, 1)

        def owned(c):
            mine, cols = ring.own(c)
            return pltpu.make_async_copy(mine, wide.at[:, cols], gsem.at[0])

        for item in program:
            if item[0] == "c":
                compute[item[2]]()
            elif scatter and item[0] == "f":
                fly.take(item[2])
                if item[2] == 0:
                    fly.start(1)
            elif scatter and ring.stage(*item):
                owned(item[0]).start()
        if scatter:
            small_out[...] = value[2]
            for c in range(len(pieces)):
                ring.drain(c)
            pltpu.make_async_copy(wide, wide, gsem.at[0]).wait()
            fly.drain()
        else:
            rows = copy(grad, wide, osem.at[6])
            small_out[...] = value[0]
            rows.wait()
        pltpu.make_async_copy(dz, grad_in_h, osem.at[5]).wait()

    count = (2 * fw + 4 * hw) // CW
    pl.run_scoped(backward_part, V(count, NZ, NY, NX, ROWS, CW))


def distill(scatter, tokens, bucket, lens, teacher, student):
    def cut(layer):
        wq, bq, wk, wv, bv, wo, bo, g1, s1, w1, b1, w2, b2, g2, s2 = layer
        return [wq, wk, wv, wo, w1, w2], [bq, bv, bo, g1, s1, b1, b2, g2, s2]
    tw, tv = cut(teacher)
    sw, sv = cut(student)
    toks, d = tokens.shape
    hw, fw = tw[0].shape[1], tw[4].shape[1]
    count = (2 * fw + 4 * hw) // CW
    halves, b = toks // SPAN, BF16
    pieces, program = PIECES, PROGRAM
    hbm, vmem = (pl.BlockSpec(memory_space=m) for m in (pl.ANY, pltpu.VMEM))
    def S(*shape, dtype=F32):
        return jax.ShapeDtypeStruct(shape, dtype)
    def V(*shape, dtype=F32):
        return pltpu.VMEM(shape, dtype)
    dma = pltpu.SemaphoreType.DMA
    wide = S(ROWS, count * CW) if scatter else S(count, NZ, NY, NX, ROWS, CW)
    outs = (S(halves, SPAN, d), S(halves, SPAN, d), wide, S(8, 896)) + (S(halves, SPAN, hw, dtype=b),) * 4
    return pl.pallas_call(
        functools.partial(step_kernel, scatter, pieces, program),
        out_shape=outs,
        in_specs=[hbm] * 33,
        out_specs=(hbm, hbm, hbm, vmem) + (hbm,) * 4,
        scratch_shapes=[
            V(halves, SPAN, d, dtype=b), V(d, fw, dtype=b), V(fw, d, dtype=b), V(halves, SPAN, fw, dtype=b), V(halves, SPAN, d, dtype=b),
            V(halves, SPAN, d, dtype=b), V(halves, SPAN, d), V(halves, SPAN, d), V(halves, SPAN, 128), V(2, SPAN, d), V(4, SPAN, d),
            V(18, 1, fw), V(3, 8, 896), V(2, 4, 8, 896),
            dma((1,)), dma((10,)), dma((7,)), dma((4, 2)), dma((4, 2)), dma((8,)), dma((2,)), dma((2,)), dma((1,)),
            pltpu.SMEM((1,), jnp.int32), pltpu.SMEM((1, 8), jnp.int32)]
        + (ring_scratch(pieces) if scatter else []),
        compiler_params=pltpu.CompilerParams(collective_id=1, has_side_effects=True, vmem_limit_bytes=VMEM_BYTES),
    )(bucket, lens, tokens.reshape(halves, SPAN, d), *tw, *sw, *tv, *sv)[:4]


def finish_kernel(out_h, gin_h, wide_h, small_h, out, gin, gq, gk, gv, go, g1w, g2w, *rest):
    small_outs, (wide, small, stage, sem_in, sem_out) = rest[:9], rest[9:]
    d = out.shape[2]
    fw, hw = g1w.shape[1], gq.shape[1]
    count = [0]

    def copy(src, dst):
        count[0] += 1
        return pltpu.make_async_copy(src, dst, sem_out.at[count[0] - 1])

    loads, stores = [(small_h, small), (wide_h, wide)], [[], []]
    for dst, row in zip((small_outs[i] for i in (2, 3, 4, 6, 7, 8)), range(6)):
        stores[0].append(copy(small.at[row, pl.ds(0, d)], dst))
    for half in range(2):
        stores[0].append(copy(small.at[6 + half, pl.ds(0, d)], small_outs[5].at[pl.ds(half * d, d)]))
    for pair in range(hw // 128):
        at, extra = pl.ds(pair * 128, 128), pl.ds(d, 128)
        stores[0].append(copy(small.at[pair, extra], small_outs[0].at[at]))
        stores[0].append(copy(small.at[3 + pair, extra], small_outs[1].at[at]))
        for i, dst in enumerate((go, gq, gk, gv)):
            stores[1].append(copy(wide.at[:, pl.ds(2 * fw + pair * 512 + i * 128, 128)], dst.at[:, at]))
    stores[1].append(copy(wide.at[:, pl.ds(0, fw)], g2w))
    stores[1].append(copy(wide.at[:, pl.ds(fw, fw)], g1w))
    for src, dst in ((out_h, out), (gin_h, gin)):
        for b in range(2):
            for rows in (pl.ds(0, SPAN // 2), pl.ds(SPAN // 2, SPAN // 2)):
                place = stage.at[len(loads) - 2]
                loads.append((src.at[b, rows], place))
                stores.append([copy(place, dst.at[b, rows])])
    loads = [pltpu.make_async_copy(src, dst, sem_in.at[i]) for i, (src, dst) in enumerate(loads)]
    for item in loads:
        item.start()
    for load, group in zip(loads, stores):
        load.wait()
        for item in group:
            item.start()
    for group in stores:
        for item in group:
            item.wait()


def finish(out_raw, gin_raw, wide, small, hw, fw):
    d = out_raw.shape[2]
    def S(*shape):
        return jax.ShapeDtypeStruct(shape, F32)
    hbm = pl.BlockSpec(memory_space=pl.ANY)
    return pl.pallas_call(
        finish_kernel,
        out_shape=(S(*out_raw.shape), S(*gin_raw.shape), S(ROWS, hw), S(ROWS, hw), S(ROWS, hw), S(ROWS, hw), S(ROWS, fw), S(ROWS, fw),
                   S(hw), S(hw), S(d), S(d), S(d), S(fw), S(d), S(d), S(d)),
        in_specs=[hbm] * 4,
        out_specs=(hbm,) * 17,
        scratch_shapes=[pltpu.VMEM(wide.shape, F32), pltpu.VMEM(small.shape, F32), pltpu.VMEM((8, SPAN // 2, d), F32),
                        pltpu.SemaphoreType.DMA((10,)), pltpu.SemaphoreType.DMA((48,))],
        compiler_params=pltpu.CompilerParams(vmem_limit_bytes=VMEM_BYTES),
    )(out_raw, gin_raw, wide, small)


def shards(*args):
    tokens, row_bucket, row_lengths = args[:3]
    teacher, student = args[3:18], args[18:33]
    d = tokens.shape[1]
    hw, fw = student[0].shape[1], student[9].shape[1]
    scatter = lax.axis_size("dp") == NZ * NY * NX
    out, *got = distill(scatter, tokens, row_bucket, row_lengths, teacher, student)
    if scatter:
        out, grad_in, gq, gk, gv, go, g1, g2, qb, vb, ob, g1g, s1g, b1g, b2g, g2g, s2g = finish(out, *got, hw, fw)
    else:
        grad_in, wide, small = got
        rows = wide.reshape(wide.shape[0], d, CW)
        steps = fw // CW
        last = [2 * steps + i for i in range(2 * hw // 128)]
        first, second = ([rows[c] for c in last[i::2]] for i in (0, 1))
        mats = [
            jnp.concatenate([m[:, 128:] for m in first], axis=1),
            jnp.concatenate([m[:, :128] for m in second], axis=1),
            jnp.concatenate([m[:, 128:] for m in second], axis=1),
            jnp.concatenate([m[:, :128] for m in first], axis=1),
            jnp.concatenate([rows[c] for c in range(steps, 2 * steps)], axis=1),
            jnp.concatenate([rows[c] for c in range(steps)], axis=1),
        ]
        gq, gk, gv, go, g1, g2 = (lax.psum_scatter(m, "dp", scatter_dimension=0, tiled=True) for m in mats)
        small = lax.psum(small, "dp")
        qb, vb = small[0:3, d:].reshape(-1), small[3:6, d:].reshape(-1)
        ob, g1g, s1g, b2g, g2g, s2g = (small[i, :d] for i in range(6))
        b1g = small[6:8, :d].reshape(-1)
    toks = tokens.shape[0]
    return (
        out.reshape(toks, d), grad_in.reshape(toks, d), gq, qb, gk, gv, vb, go.T, ob, g1g, s1g, g1, b1g, g2.T, b2g, g2g, s2g
    )


def solution(mesh):
    placed = (
        P("dp", None),
        P("dp"),
        P("dp", None),
        P(None, "head"),
        P("head"),
        P(None, "head"),
        P(None, "head"),
        P("head"),
        P("head", None),
        P(),
        P(),
        P(),
        P(None, "head"),
        P("head"),
        P("head", None),
        P(),
        P(),
        P(),
        P(None, "head"),
        P("head"),
        P(None, "head"),
        P(None, "head"),
        P("head"),
        P("head", None),
        P(),
        P(),
        P(),
        P(None, "head"),
        P("head"),
        P("head", None),
        P(),
        P(),
        P(),
    )
    return jax.shard_map(
        shards,
        mesh=mesh,
        in_specs=placed,
        out_specs=(
            P("dp", None),
            P("dp", None),
            P("dp", "head"),
            P("head"),
            P("dp", "head"),
            P("dp", "head"),
            P("head"),
            P("head", "dp"),
            P(),
            P(),
            P(),
            P("dp", "head"),
            P("head"),
            P("head", "dp"),
            P(),
            P(),
            P(),
        ),
        check_vma=False,
    )
```
